32 devices in a mesh: dp: 8 (over y, x, core), mp: 4 (over z).
Axes of the slice: x: 2, y: 2, z: 4, core: 2. Of those that a mesh axis runs over, the one named last changes fastest.
Arguments:
- layer_in: bfloat16 [32, 1024, 512], P('dp'), may hold values from -6 to 6
- doc_ids: int32 [32, 1024], P('dp'), may hold values from 0 to 3, never falling along the last dimension, each value on 1 to 512 neighbouring positions
- out_grad: float32 [32, 1024, 512], P('dp', 'mp'), may hold values from -13 to 13
- w_query: float32 [512, 512], P(None, 'mp'), may hold values from -0.25 to 0.25
- w_key: float32 [512, 512], P(None, 'mp'), may hold values from -0.25 to 0.25
- w_value: float32 [512, 512], P(None, 'mp'), may hold values from -0.25 to 0.25
- w_output: float32 [512, 512], P('mp')
- w_expand: float32 [2048, 512], P('mp'), may hold values from -0.25 to 0.25
- w_contract: float32 [2048, 512], P('mp'), may hold values from -0.125 to 0.125
- small_params: float32 [2562], replicated, may hold values from -2.5 to 2.5
- buffer_query: float32 [512, 512], P(None, 'mp')
- buffer_key: float32 [512, 512], P(None, 'mp')
- buffer_value: float32 [512, 512], P(None, 'mp')
- buffer_output: float32 [512, 512], P('mp')
- buffer_expand: float32 [2048, 512], P('mp')
- buffer_contract: float32 [2048, 512], P('mp')
- small_first: float32 [2562], replicated
- small_second: float32 [2562], replicated, as said below
Outputs:
- layer_out: float32 [32, 1024, 512], P('dp', 'mp')
- in_grad: float32 [32, 1024, 512], P('dp', 'mp')
- new_buffer_query: float32 [512, 512], P(None, 'mp')
- new_buffer_key: float32 [512, 512], P(None, 'mp')
- new_buffer_value: float32 [512, 512], P(None, 'mp')
- new_buffer_output: float32 [512, 512], P('mp')
- new_buffer_expand: float32 [2048, 512], P('mp')
- new_buffer_contract: float32 [2048, 512], P('mp')
- new_w_query: float32 [512, 512], P(None, 'mp')
- new_w_key: float32 [512, 512], P(None, 'mp')
- new_w_value: float32 [512, 512], P(None, 'mp')
- new_w_output: float32 [512, 512], P('mp')
- new_w_expand: float32 [2048, 512], P('mp')
- new_w_contract: float32 [2048, 512], P('mp')
- new_small_params: float32 [2562], replicated
- new_small_first: float32 [2562], replicated
- new_small_second: float32 [2562], replicated
The draws below stay inside these ranges and needn't reach their ends.
Inputs may be any that keep to these rules, and one draw needn't show every extreme that they name: `doc_ids`: along each row the document numbers never fall; a document covers 1 to 512 positions, and one covers exactly 512. `small_second`: every entry is positive.
All inputs are finite; a program needn't handle non-finite values.
Results may differ from the reference program's by a relative error of at most 0.029.
Values may be sent and summed in bfloat16 or wider, within the bound.
No kernel may reach another device: no remote copies, remote signals or barrier semaphores. Data moves between devices by JAX's collectives and lax.ppermute only.
A program may use at most 192 MiB of HBM per device.

```python
import math
import jax
import jax.numpy as jnp
import numpy as np
from jax import lax

D = 512
HEADS = 8
HEAD_DIM = 64
FF = 2048
L = 1024
SEGS = 4
STEP = 10
SEQS = 32
TOKENS = 32768
N_MP = 4


def rising(count, start, finish):
    return start + (finish - start) * jnp.arange(count, dtype=jnp.float32) / max(count - 1, 1)


def spread_factors(key, count, low_end, high_end):
    return jnp.exp(jax.random.uniform(key, (count,), jnp.float32, math.log(low_end), math.log(high_end)))


def normal_base(key, rows, cols):
    return jnp.clip(jax.random.normal(key, (rows, cols), jnp.float32), -4.0, 4.0)


def scaled_buffer(key, base, along_rows, scale, start, finish):
    rows, cols = base.shape
    key_one, key_two = jax.random.split(key)
    if along_rows:
        row_factor = rising(rows, start, finish) * spread_factors(key_one, rows, 0.55, 1.8)
        col_factor = spread_factors(key_two, cols, 0.32, 3.2)
    else:
        row_factor = spread_factors(key_one, rows, 0.32, 3.2)
        col_factor = rising(cols, start, finish) * spread_factors(key_two, cols, 0.55, 1.8)
    return scale * base * row_factor[:, None] * col_factor[None, :]


def small_scales():
    root = math.sqrt(TOKENS)
    wide_root = math.sqrt(TOKENS * D)
    return jnp.concatenate((jnp.full((FF,), 0.27 * root, jnp.float32), jnp.full((D,), 0.9 * root, jnp.float32), jnp.array([0.8 * wide_root, wide_root], jnp.float32)))


def draw_out_grad(key, part):
    key = jax.random.fold_in(key, 41)
    base = jnp.clip(jax.random.normal(key, (SEQS, L, D), jnp.float32), -4.0, 4.0)
    start, finish = (0.6, 1.8)
    seq_factor = rising(SEQS, start, finish)
    pos_factor = rising(L, start, finish)
    return base * seq_factor[:, None, None] * pos_factor[None, :, None]


def draw_w_output(key, part):
    key = jax.random.fold_in(key, 31)
    base = normal_base(key, D, D)
    start, finish = (0.6, 1.8)
    return 0.18 * base * rising(D, start, finish)[:, None]


def draw_small_params(key, part):
    key = jax.random.fold_in(key, 51)
    bias_key, alpha_key = jax.random.split(key)
    biases = 0.5 * jnp.clip(jax.random.normal(bias_key, (FF + D,), jnp.float32), -5.0, 5.0)
    alphas = jax.random.uniform(alpha_key, (2,), jnp.float32, 0.5, 1.0)
    return jnp.concatenate((biases, alphas))


def draw_buffer_query(key, part):
    key = jax.random.fold_in(key, 21)
    base_key, factor_key = jax.random.split(key)
    base = normal_base(base_key, D, D)
    start, finish = (0.6, 1.8)
    return scaled_buffer(factor_key, base, False, 0.5 * math.sqrt(TOKENS), start, finish)


def draw_buffer_key(key, part):
    key = jax.random.fold_in(key, 22)
    base_key, factor_key = jax.random.split(key)
    base = normal_base(base_key, D, D)
    start, finish = (0.6, 1.8)
    return scaled_buffer(factor_key, base, False, 0.5 * math.sqrt(TOKENS), start, finish)


def draw_buffer_value(key, part):
    key = jax.random.fold_in(key, 23)
    base_key, factor_key = jax.random.split(key)
    base = normal_base(base_key, D, D)
    start, finish = (0.6, 1.8)
    return scaled_buffer(factor_key, base, False, 0.5 * math.sqrt(TOKENS), start, finish)


def draw_buffer_output(key, part):
    key = jax.random.fold_in(key, 24)
    base_key, factor_key = jax.random.split(key)
    base = normal_base(base_key, D, D)
    start, finish = (0.6, 1.8)
    return scaled_buffer(factor_key, base, True, 0.12 * math.sqrt(TOKENS), start, finish)


def draw_buffer_expand(key, part):
    key = jax.random.fold_in(key, 25)
    base_key, factor_key = jax.random.split(key)
    base = normal_base(base_key, FF, D)
    start, finish = (0.6, 1.8)
    return scaled_buffer(factor_key, base, True, 0.3 * math.sqrt(TOKENS), start, finish)


def draw_buffer_contract(key, part):
    key = jax.random.fold_in(key, 26)
    base_key, factor_key = jax.random.split(key)
    base = normal_base(base_key, FF, D)
    start, finish = (0.6, 1.8)
    return scaled_buffer(factor_key, base, True, 0.55 * math.sqrt(TOKENS), start, finish)


def draw_small_first(key, part):
    key = jax.random.fold_in(key, 61)
    base = jnp.clip(jax.random.normal(key, (FF + D + 2,), jnp.float32), -3.0, 3.0)
    return base * small_scales()


def draw_small_second(key, part):
    key = jax.random.fold_in(key, 71)
    scales = small_scales()
    return 2.0 * scales * scales * spread_factors(key, FF + D + 2, 0.5, 2.0)


def block_scale(stream_key, shape, pieces, smallest, largest):
    level = 1.0
    for position, blocks in pieces:
        heights = jax.random.uniform(jax.random.fold_in(jax.random.fold_in(stream_key, 6), position), (blocks,), jnp.float32, smallest / len(pieces), largest / len(pieces))
        level = level * jnp.repeat(jnp.exp(heights), shape[position] // blocks).reshape((-1,) + (1,) * (len(shape) - 1 - position))
    return level


def split_up(count, total, most, slope):
    loads = [(1 << 20) // math.isqrt(grade ** slope) + 1 for grade in range(2, count + 1)]
    spare, given = total - most - (count - 1), [1] * (count - 1)
    while spare > 0:
        free = [i for i in range(count - 1) if given[i] < most]
        pool, budget = sum([loads[i] for i in free]), spare
        for i in free:
            addition = min(most - given[i], max(1, budget * loads[i] // pool), spare)
            given[i] = given[i] + addition
            spare = spare - addition
    return np.array([most] + given)


def ragged(rng, amount, total, reach, skew):
    if amount == 2:
        one = jax.random.randint(rng, (), max(1, total - reach), min(reach, total - 1) + 1)
        return jnp.stack([one, total - one])
    lengths = jnp.asarray(split_up(amount, total, reach, skew), jnp.int32)
    twos = (amount - 1) // 2
    donor, taker = lengths[1:1 + 2 * twos:2], lengths[2:2 + 2 * twos:2]
    margin = jnp.minimum(donor - 1, reach - taker)
    shifted = jax.random.randint(jax.random.fold_in(rng, 1), (twos,), 0, 1 << 20) % (margin + 1)
    lengths = lengths.at[1:1 + 2 * twos:2].set(donor - shifted).at[2:2 + 2 * twos:2].set(taker + shifted)
    return lengths[jax.random.permutation(jax.random.fold_in(rng, 2), amount)]


def gaussian(key, shape, deviation, bound, pieces=(), held_as=jnp.bfloat16):
    entries = jax.random.normal(key, shape, jnp.float32) * deviation
    if len(pieces) > 0:
        entries = block_scale(key, shape, pieces, -0.22, 0.18) * entries
    return jnp.clip(entries, min=-bound, max=bound).astype(held_as)


def setup_inputs(seed: int = 0) -> dict:
    key_list = jax.random.split(jax.random.key(seed), 19)
    return {
        "layer_in": gaussian(key_list[0], (SEQS, L, D), 1.0, 6.0, ((0, 8),)),
        "doc_ids": jax.vmap(lambda own: jnp.searchsorted(jnp.cumsum(ragged(own, SEGS, L, L // 2, 1)), jnp.arange(L), side="right"))(jax.random.split(key_list[1], SEQS)).reshape((SEQS, L)).astype(jnp.int32),
        "out_grad": draw_out_grad(jax.random.fold_in(key_list[18], 71), 0),
        "w_query": gaussian(key_list[3], (D, D), D ** -0.5, 0.25, ((1, 4),), jnp.float32),
        "w_key": gaussian(key_list[4], (D, D), D ** -0.5, 0.25, ((1, 4),), jnp.float32),
        "w_value": gaussian(key_list[5], (D, D), D ** -0.5, 0.25, ((1, 4),), jnp.float32),
        "w_output": draw_w_output(jax.random.fold_in(key_list[18], 71), 0),
        "w_expand": gaussian(key_list[7], (FF, D), D ** -0.5, 0.25, ((0, 4),), jnp.float32),
        "w_contract": gaussian(key_list[8], (FF, D), FF ** -0.5, 0.125, ((0, 4),), jnp.float32),
        "small_params": draw_small_params(jax.random.fold_in(key_list[18], 71), 0),
        "buffer_query": draw_buffer_query(jax.random.fold_in(key_list[18], 71), 0),
        "buffer_key": draw_buffer_key(jax.random.fold_in(key_list[18], 71), 0),
        "buffer_value": draw_buffer_value(jax.random.fold_in(key_list[18], 71), 0),
        "buffer_output": draw_buffer_output(jax.random.fold_in(key_list[18], 71), 0),
        "buffer_expand": draw_buffer_expand(jax.random.fold_in(key_list[18], 71), 0),
        "buffer_contract": draw_buffer_contract(jax.random.fold_in(key_list[18], 71), 0),
        "small_first": draw_small_first(jax.random.fold_in(key_list[18], 71), 0),
        "small_second": draw_small_second(jax.random.fold_in(key_list[18], 71), 0),
    }


@jax.custom_vjp
def low(v):
    return lax.optimization_barrier(v.astype(jnp.bfloat16)).astype(jnp.float32)

@jax.custom_vjp
def low_back(v):
    return v

def low_keep(v):
    return (low(v), None)

def low_pass(kept, grad):
    return (grad,)

def back_keep(v):
    return (v, None)

def back_low(kept, grad):
    return (low(grad),)
low.defvjp(low_keep, low_pass)
low_back.defvjp(back_keep, back_low)
newton_one = 3.4445
newton_two = -4.775
newton_three = 2.0315
muon_rates = (1.0, 1.0, 1.0, 5.0, 2.0, 1.0)
adam_rate = 0.25
mask_fill = -1e+30
highest_precision = lax.Precision.HIGHEST

def gelu_tanh(values):
    return jax.nn.gelu(values, approximate=True)

def round_low(values):
    return values.astype(jnp.bfloat16).astype(jnp.float32)

def layer_group(weights, layer_inputs, documents):
    query_key_value_weight, projection_weight, expansion_weight, contraction_weight, expansion_bias, contraction_bias, alpha_attend, alpha_ffn = weights
    seq_count = layer_inputs.shape[0]
    query_key_value_rows = jnp.einsum('orv,vx->orx', layer_inputs, query_key_value_weight, precision=highest_precision)
    query_key_value_rows = low(low_back(query_key_value_rows)).reshape(seq_count, L, 3, HEADS, HEAD_DIM)
    query_all = query_key_value_rows[:, :, 0]
    key_all = query_key_value_rows[:, :, 1]
    value_all = query_key_value_rows[:, :, 2]
    scores = low_back(jnp.einsum('sqhd,skhd->shqk', query_all, key_all, precision=highest_precision) * HEAD_DIM ** (-0.5))
    places = jnp.arange(L)
    allowed = (places[:, None] >= places[None, :])[None] & (documents[:, :, None] == documents[:, None, :])
    scores = jnp.where(allowed[:, None], scores, mask_fill)
    probs = low(jax.nn.softmax(scores, axis=-1))
    head_outputs = jnp.einsum('shqk,skhd->sqhd', probs, value_all, precision=highest_precision).reshape(seq_count, L, D)
    head_outputs = low(low_back(head_outputs))
    attention_result = low_back(jnp.einsum('byq,qz->byz', head_outputs, projection_weight, precision=highest_precision))
    middle_activation = layer_inputs + alpha_attend * attention_result
    preactivation = low_back(jnp.einsum('ibv,gv->ibg', low(middle_activation), expansion_weight, precision=highest_precision) + expansion_bias)
    hidden_state = low(gelu_tanh(preactivation))
    residual_branch = low_back(jnp.einsum('pci,in->pcn', hidden_state, contraction_weight, precision=highest_precision) + contraction_bias)
    return middle_activation + alpha_ffn * residual_branch

def reference(layer_in, doc_ids, out_grad, w_query, w_key, w_value, w_output, w_expand, w_contract, small_params, buffer_query, buffer_key, buffer_value, buffer_output, buffer_expand, buffer_contract, small_first, small_second):
    group_size = math.gcd(SEQS, max(1, 4096 // L))
    stepper = jax.checkpoint(layer_group)

    def forward(layer_inputs, wq_in, wk_in, wv_in, wo_in, we_in, wc_in, params):
        weights = (low(jnp.concatenate((wq_in, wk_in, wv_in), 1)), low(wo_in), low(we_in), low(wc_in), params[:FF], params[FF:FF + D], params[FF + D], params[FF + D + 1])
        results = lax.map(lambda packed: stepper(weights, packed[0], packed[1]), (layer_inputs.reshape(SEQS // group_size, group_size, L, D), doc_ids.reshape(SEQS // group_size, group_size, L)))
        return results.reshape(SEQS, L, D)
    primals = (layer_in.astype(jnp.float32), w_query, w_key, w_value, w_output, w_expand, w_contract, small_params)
    layer_out, pullback = jax.vjp(forward, *primals)
    gradients = pullback(out_grad)
    in_grad = gradients[0]
    small_grad = gradients[7]
    first_new = 0.5 * small_first + 0.5 * small_grad
    second_new = 0.5 * small_second + 0.5 * small_grad * small_grad
    correction = 1.0 - 0.5 ** STEP
    small_new = small_params - adam_rate * (first_new / correction) / (jnp.sqrt(second_new / correction) + 1e-08)
    olds = (buffer_query, buffer_key, buffer_value, buffer_output, buffer_expand, buffer_contract)
    weights_old = (w_query, w_key, w_value, w_output, w_expand, w_contract)
    buffers = tuple((0.5 * old_buffer + grad_matrix for old_buffer, grad_matrix in zip(olds, gradients[1:7])))
    new_weights = []
    for matrix_index in range(6):
        matrix = buffers[matrix_index]
        by_columns = matrix_index < 3
        iterate = matrix if by_columns else matrix.T
        iterate = iterate / (jnp.sqrt(jnp.sum(matrix * matrix)) + 1e-07)
        for newton_step in range(5):
            blocks = iterate.reshape(D, N_MP, iterate.shape[1] // N_MP)
            partial_gram = jnp.einsum('ibk,jbk->bij', blocks, blocks, precision=highest_precision)
            gram_sum = lax.optimization_barrier(jnp.sum(round_low(partial_gram), axis=0))
            polynomial = newton_two * gram_sum + newton_three * jnp.dot(gram_sum, gram_sum, precision=highest_precision)
            iterate = newton_one * iterate + jnp.dot(polynomial, iterate, precision=highest_precision)
        step_matrix = iterate if by_columns else iterate.T
        new_weights.append(weights_old[matrix_index] - muon_rates[matrix_index] * step_matrix)
    return (layer_out, in_grad, buffers[0], buffers[1], buffers[2], buffers[3], buffers[4], buffers[5], new_weights[0], new_weights[1], new_weights[2], new_weights[3], new_weights[4], new_weights[5], small_new, first_new, second_new)
```

```python
import functools

import jax
import jax.numpy as jnp
from jax import lax
from jax.experimental import pallas as pl
from jax.experimental.pallas import tpu as pltpu
from jax.sharding import PartitionSpec as P

D = 512
HEAD_DIM = 64
FF = 2048
MICRO = 2
STEP = 10


newton_one = 3.4445
newton_two = -4.775
newton_three = 2.0315
muon_rates = (1.0, 1.0, 1.0, 5.0, 2.0, 1.0)
adam_rate = 0.25
mask_fill = -1e30
highest_precision = lax.Precision.HIGHEST


def shortened(x):
    return jax.tree.map(lambda a: a.astype(jnp.bfloat16) if a.dtype == jnp.float32 else a, x)


def gelu_tanh(values):
    return jax.nn.gelu(values, approximate=True)


def block_scores(query_blk, key_part, docs_query, docs_key, first_row):
    scores = jnp.einsum(
        "sqhd,skhd->shqk", query_blk, key_part, preferred_element_type=jnp.float32
    ) * HEAD_DIM ** (-0.5)
    rows_at = first_row + jnp.arange(query_blk.shape[1])
    cols_at = jnp.arange(key_part.shape[1])
    allowed = (rows_at[:, None] >= cols_at[None, :])[None] & (
        docs_query[:, :, None] == docs_key[:, None, :]
    )
    return jnp.where(allowed[:, None], scores, mask_fill)


def attend(query_all, key_all, value_all, documents, span_rows):
    block_outs = []
    log_sums = []
    for block_index in range(query_all.shape[1] // span_rows):
        row_start = block_index * span_rows
        finish = row_start + span_rows
        scores = block_scores(
            query_all[:, row_start:finish],
            key_all[:, :finish],
            documents[:, row_start:finish],
            documents[:, :finish],
            row_start,
        )
        row_peak = jnp.max(scores, axis=-1, keepdims=True)
        exponent = jnp.exp(scores - row_peak)
        row_total = jnp.sum(exponent, axis=-1, keepdims=True)
        prob_low = (exponent / row_total).astype(jnp.bfloat16)
        block_outs.append(
            jnp.einsum(
                "shqk,skhd->sqhd",
                prob_low,
                value_all[:, :finish],
                preferred_element_type=jnp.float32,
            ).astype(jnp.bfloat16)
        )
        log_sums.append(row_peak + jnp.log(row_total))
    return (jnp.concatenate(block_outs, 1), log_sums)


def attend_back(query_all, key_all, value_all, documents, span_rows, log_sums, heads_grad):
    query_grads = []
    key_grad = jnp.zeros(key_all.shape, jnp.float32)
    value_grad = jnp.zeros(value_all.shape, jnp.float32)
    scale = HEAD_DIM ** (-0.5)
    for block_index in range(query_all.shape[1] // span_rows):
        row_start = block_index * span_rows
        finish = row_start + span_rows
        query_blk = query_all[:, row_start:finish]
        scores = block_scores(
            query_blk,
            key_all[:, :finish],
            documents[:, row_start:finish],
            documents[:, :finish],
            row_start,
        )
        probs = jnp.exp(scores - log_sums[block_index])
        prob_low = probs.astype(jnp.bfloat16)
        grad_blk = heads_grad[:, row_start:finish]
        grad_probs = jnp.einsum(
            "sqhd,skhd->shqk", grad_blk, value_all[:, :finish], preferred_element_type=jnp.float32
        )
        row_delta = jnp.sum(probs * grad_probs, axis=-1, keepdims=True)
        grad_scores = (probs * (grad_probs - row_delta)).astype(jnp.bfloat16)
        query_grads.append(
            jnp.einsum(
                "shqk,skhd->sqhd",
                grad_scores,
                key_all[:, :finish],
                preferred_element_type=jnp.float32,
            )
            * scale
        )
        key_grad = key_grad.at[:, :finish].add(
            jnp.einsum(
                "shqk,sqhd->skhd", grad_scores, query_blk, preferred_element_type=jnp.float32
            )
            * scale
        )
        value_grad = value_grad.at[:, :finish].add(
            jnp.einsum("shqk,sqhd->skhd", prob_low, grad_blk, preferred_element_type=jnp.float32)
        )
    return (jnp.concatenate(query_grads, 1), key_grad, value_grad)


def gram_part(iterate, by_columns):
    if by_columns:
        return lax.dot_general(
            iterate,
            iterate,
            (((1,), (1,)), ((), ())),
            precision=highest_precision,
            preferred_element_type=jnp.float32,
        )
    return lax.dot_general(
        iterate,
        iterate,
        (((0,), (0,)), ((), ())),
        precision=highest_precision,
        preferred_element_type=jnp.float32,
    )


def newton_update(iterate, gram_sum, by_columns):
    square = jnp.dot(gram_sum, gram_sum, precision=highest_precision)
    polynomial = newton_two * gram_sum + newton_three * square
    if by_columns:
        applied = jnp.dot(polynomial, iterate, precision=highest_precision)
    else:
        applied = lax.dot_general(
            iterate,
            polynomial,
            (((1,), (1,)), ((), ())),
            precision=highest_precision,
            preferred_element_type=jnp.float32,
        )
    return newton_one * iterate + applied


def general_shards(
    layer_in,
    doc_ids,
    out_grad,
    w_query,
    w_key,
    w_value,
    w_output,
    w_expand,
    w_contract,
    small_params,
    buffer_query,
    buffer_key,
    buffer_value,
    buffer_output,
    buffer_expand,
    buffer_contract,
    small_first,
    small_second,
):
    group_count = lax.axis_size("mp")
    group_index = lax.axis_index("mp")
    seq_count, length, model_width = layer_in.shape
    per_micro = seq_count // MICRO
    token_span = length // group_count
    head_cols = w_query.shape[1]
    heads_here = head_cols // HEAD_DIM
    span_rows = min(512, length)
    expansion_bias = small_params[:FF]
    contraction_bias = small_params[FF : FF + D]
    alpha_attend = small_params[FF + D]
    alpha_ffn = small_params[FF + D + 1]
    query_key_value_weight = jnp.concatenate((w_query, w_key, w_value), 1).astype(jnp.bfloat16)
    row_local = (
        w_output.astype(jnp.bfloat16),
        w_expand.astype(jnp.bfloat16),
        w_contract.astype(jnp.bfloat16),
    )
    grad_qkv_weight = jnp.zeros((model_width, 3 * head_cols), jnp.float32)
    grad_output = jnp.zeros((D, D), jnp.float32)
    grad_expand = jnp.zeros((FF, D), jnp.float32)
    grad_contract = jnp.zeros((FF, D), jnp.float32)
    grad_bias_expand = jnp.zeros((FF,), jnp.float32)
    grad_bias_contract = jnp.zeros((D,), jnp.float32)
    grad_alpha_attend = jnp.zeros((), jnp.float32)
    grad_alpha_ffn = jnp.zeros((), jnp.float32)
    out_blocks = []
    grad_blocks = []
    for micro_index in range(MICRO):
        rows_from = micro_index * per_micro
        layer_inputs = layer_in[rows_from : rows_from + per_micro]
        documents = doc_ids[rows_from : rows_from + per_micro]
        upstream = out_grad[rows_from : rows_from + per_micro]
        query_key_value_rows = jnp.einsum(
            "orv,vx->orx", layer_inputs, query_key_value_weight, preferred_element_type=jnp.float32
        ).astype(jnp.bfloat16)
        qkv_split = query_key_value_rows.reshape(per_micro, length, 3, heads_here, HEAD_DIM)
        query_all = qkv_split[:, :, 0]
        key_all = qkv_split[:, :, 1]
        value_all = qkv_split[:, :, 2]
        head_outputs, log_sums = attend(query_all, key_all, value_all, documents, span_rows)
        heads_flat = head_outputs.reshape(per_micro, length, head_cols)
        heads_tok = lax.all_to_all(heads_flat, "mp", split_axis=1, concat_axis=2, tiled=True)
        row_now = (
            lax.all_gather(row_local[0], "mp", axis=0, tiled=True),
            lax.all_gather(row_local[1], "mp", axis=0, tiled=True),
            lax.all_gather(row_local[2], "mp", axis=0, tiled=True),
        )
        output_full, expand_full, contract_full = row_now
        attention_result = jnp.einsum(
            "std,de->ste", heads_tok, output_full, preferred_element_type=jnp.float32
        )
        local_in = lax.dynamic_slice_in_dim(
            layer_inputs, group_index * token_span, token_span, 1
        ).astype(jnp.float32)
        middle_activation = local_in + alpha_attend * attention_result
        middle_low = middle_activation.astype(jnp.bfloat16)
        preactivation = (
            jnp.einsum("std,fd->stf", middle_low, expand_full, preferred_element_type=jnp.float32)
            + expansion_bias
        )
        hidden_state, gelu_back = jax.vjp(gelu_tanh, preactivation)
        hidden_low = hidden_state.astype(jnp.bfloat16)
        residual_branch = (
            jnp.einsum("stf,fd->std", hidden_low, contract_full, preferred_element_type=jnp.float32)
            + contraction_bias
        )
        out_blocks.append(middle_activation + alpha_ffn * residual_branch)
        grad_alpha_ffn = grad_alpha_ffn + jnp.sum(upstream * residual_branch)
        branch_grad = (alpha_ffn * upstream).astype(jnp.bfloat16)
        grad_bias_contract = grad_bias_contract + jnp.sum(
            branch_grad, axis=(0, 1), dtype=jnp.float32
        )
        grad_contract = grad_contract + jnp.einsum(
            "stf,std->fd", hidden_low, branch_grad, preferred_element_type=jnp.float32
        )
        hidden_grad = jnp.einsum(
            "std,fd->stf", branch_grad, contract_full, preferred_element_type=jnp.float32
        )
        pre_grad = gelu_back(hidden_grad)[0].astype(jnp.bfloat16)
        grad_bias_expand = grad_bias_expand + jnp.sum(pre_grad, axis=(0, 1), dtype=jnp.float32)
        grad_expand = grad_expand + jnp.einsum(
            "stf,std->fd", pre_grad, middle_low, preferred_element_type=jnp.float32
        )
        middle_grad = upstream + jnp.einsum(
            "stf,fd->std", pre_grad, expand_full, preferred_element_type=jnp.float32
        )
        grad_alpha_attend = grad_alpha_attend + jnp.sum(middle_grad * attention_result)
        attend_grad = (alpha_attend * middle_grad).astype(jnp.bfloat16)
        grad_output = grad_output + jnp.einsum(
            "std,ste->de", heads_tok, attend_grad, preferred_element_type=jnp.float32
        )
        heads_grad_tok = jnp.einsum(
            "ste,de->std", attend_grad, output_full, preferred_element_type=jnp.float32
        ).astype(jnp.bfloat16)
        heads_grad = lax.all_to_all(heads_grad_tok, "mp", split_axis=2, concat_axis=1, tiled=True)
        heads_grad = heads_grad.reshape(per_micro, length, heads_here, HEAD_DIM)
        query_grad, key_grad, value_grad = attend_back(
            query_all, key_all, value_all, documents, span_rows, log_sums, heads_grad
        )
        query_key_value_gradient = (
            jnp.stack((query_grad, key_grad, value_grad), 2)
            .reshape(per_micro, length, 3 * head_cols)
            .astype(jnp.bfloat16)
        )
        grad_qkv_weight = grad_qkv_weight + jnp.einsum(
            "tmf,tmp->fp",
            layer_inputs,
            query_key_value_gradient,
            preferred_element_type=jnp.float32,
        )
        partial_grad = jnp.einsum(
            "nrj,yj->nry",
            query_key_value_gradient,
            query_key_value_weight,
            preferred_element_type=jnp.float32,
        )
        head_part = lax.psum_scatter(
            partial_grad.astype(jnp.bfloat16), "mp", scatter_dimension=1, tiled=True
        ).astype(jnp.float32)
        grad_blocks.append(middle_grad + head_part)
    layer_out = jnp.concatenate(out_blocks, 0)
    in_grad = jnp.concatenate(grad_blocks, 0)
    output_part, expand_part, contract_part = (
        lax.psum_scatter(
            grad_output.astype(jnp.bfloat16), "mp", scatter_dimension=0, tiled=True
        ).astype(jnp.float32),
        lax.psum_scatter(
            grad_expand.astype(jnp.bfloat16), "mp", scatter_dimension=0, tiled=True
        ).astype(jnp.float32),
        lax.psum_scatter(
            grad_contract.astype(jnp.bfloat16), "mp", scatter_dimension=0, tiled=True
        ).astype(jnp.float32),
    )
    matrix_grads = (
        lax.psum(grad_qkv_weight[:, :head_cols].astype(jnp.bfloat16), "dp").astype(jnp.float32),
        lax.psum(grad_qkv_weight[:, head_cols : 2 * head_cols].astype(jnp.bfloat16), "dp").astype(
            jnp.float32
        ),
        lax.psum(grad_qkv_weight[:, 2 * head_cols :].astype(jnp.bfloat16), "dp").astype(
            jnp.float32
        ),
        lax.psum(output_part.astype(jnp.bfloat16), "dp").astype(jnp.float32),
        lax.psum(expand_part.astype(jnp.bfloat16), "dp").astype(jnp.float32),
        lax.psum(contract_part.astype(jnp.bfloat16), "dp").astype(jnp.float32),
    )
    small_local = jnp.concatenate(
        (grad_bias_expand, grad_bias_contract, jnp.stack((grad_alpha_attend, grad_alpha_ffn)))
    )
    small_grad = lax.psum(small_local, ("dp", "mp"))
    first_new = 0.5 * small_first + 0.5 * small_grad
    second_new = 0.5 * small_second + 0.5 * small_grad * small_grad
    correction = 1.0 - 0.5**STEP
    small_new = small_params - adam_rate * (first_new / correction) / (
        jnp.sqrt(second_new / correction) + 1e-08
    )
    olds = (buffer_query, buffer_key, buffer_value, buffer_output, buffer_expand, buffer_contract)
    weights_old = (w_query, w_key, w_value, w_output, w_expand, w_contract)
    by_columns = (True, True, True, False, False, False)
    buffers = tuple(
        (0.5 * old_buffer + grad_matrix for old_buffer, grad_matrix in zip(olds, matrix_grads))
    )
    squares = lax.psum(tuple((jnp.sum(matrix * matrix) for matrix in buffers)), "mp")
    iterates = [
        matrix / (jnp.sqrt(square_sum) + 1e-07) for matrix, square_sum in zip(buffers, squares)
    ]
    for newton_step in range(5):
        gram_sums = jax.tree.map(
            lambda part: part.astype(jnp.float32),
            lax.psum(
                shortened(
                    tuple(
                        (
                            gram_part(iterate, column_flag)
                            for iterate, column_flag in zip(iterates, by_columns)
                        )
                    )
                ),
                "mp",
            ),
        )
        iterates = [
            newton_update(iterate, gram_sum, column_flag)
            for iterate, gram_sum, column_flag in zip(iterates, gram_sums, by_columns)
        ]
    new_weights = tuple(
        (
            weight - rate * iterate
            for weight, rate, iterate in zip(weights_old, muon_rates, iterates)
        )
    )
    return (layer_out, in_grad) + buffers + new_weights + (small_new, first_new, second_new)


max_doc = 512
q_rows = 256
f32 = jnp.float32
bf16 = jnp.bfloat16
nt = (((1,), (1,)), ((), ()))
nn = (((1,), (0,)), ((), ()))
tn = (((0,), (0,)), ((), ()))


def mm(a, b, dims):
    return lax.dot_general(a, b, dims, preferred_element_type=f32)


def swap(x, axis, mask):
    size = lax.axis_size(axis)
    return lax.ppermute(x, axis, [(a, a ^ mask) for a in range(size)])


def reorder(x, index, axis):
    parts = [
        lax.dynamic_slice_in_dim(x, slot ^ index, 1, axis) for slot in range(x.shape[axis])
    ]
    return jnp.concatenate(parts, axis)


def pick(x, index):
    return lax.dynamic_index_in_dim(x, index, 0, keepdims=False)


def gather_rows(piece):
    planes = lax.axis_size("mp")
    chips = lax.axis_size("dp") // 2
    slots = jnp.stack([piece] + [swap(piece, "mp", k) for k in range(1, planes)])
    slots = jnp.stack([slots] + [swap(slots, "dp", 2 * m) for m in range(1, chips)], 1)
    return jnp.stack([slots, swap(slots, "dp", 1)], 2)


def window(first_row):
    return max(0, first_row + 1 - max_doc) // 128 * 128


def forward_kernel(last_ref, q_ref, k_ref, v_ref, o_ref):
    length = q_ref.shape[0]
    lane = lax.broadcasted_iota(jnp.int32, (q_rows, 128), 1)
    for first in range(0, length, q_rows):
        low, high = window(first), first + q_rows
        row = first + lax.broadcasted_iota(jnp.int32, (q_rows, high - low), 0)
        col = low + lax.broadcasted_iota(jnp.int32, (q_rows, high - low), 1)
        allowed = (col <= row) & (row <= last_ref[:, low:high])
        query = q_ref[first:high, :] * jnp.asarray(HEAD_DIM**-0.5, bf16)
        halves = []
        for half in range(2):
            mine = (lane >= HEAD_DIM * half) & (lane < HEAD_DIM * (half + 1))
            scores = mm(jnp.where(mine, query, jnp.zeros_like(query)), k_ref[low:high, :], nt)
            scores = jnp.where(allowed, scores, mask_fill)
            weight = jnp.exp(scores - jnp.max(scores, axis=1, keepdims=True))
            total = jnp.sum(weight, axis=1, keepdims=True)
            halves.append(mm((weight * (1.0 / total)).astype(bf16), v_ref[low:high, :], nn))
        o_ref[first:high, :] = jnp.where(lane < HEAD_DIM, halves[0], halves[1]).astype(bf16)


def backward_kernel(start_ref, q_ref, k_ref, v_ref, g_ref, out_ref, dk_ref, dv_ref):
    length = q_ref.shape[0]
    lane = lax.broadcasted_iota(jnp.int32, (q_rows, 128), 1)
    dk_ref[...] = jnp.zeros_like(dk_ref)
    dv_ref[...] = jnp.zeros_like(dv_ref)
    key_t = k_ref[...].astype(f32).T.astype(bf16)
    for first in range(0, length, q_rows):
        low, high = window(first), first + q_rows
        col = low + lax.broadcasted_iota(jnp.int32, (high - low, q_rows), 0)
        row = first + lax.broadcasted_iota(jnp.int32, (high - low, q_rows), 1)
        allowed = (col <= row) & (col >= start_ref[:, first:high])
        query = q_ref[first:high, :] * jnp.asarray(HEAD_DIM**-0.5, bf16)
        grad = g_ref[first:high, :]
        key = k_ref[low:high, :]
        value = v_ref[low:high, :]
        dk = dk_ref[low:high, :]
        dv = dv_ref[low:high, :]
        dq = []
        for half in range(2):
            mine = (lane >= HEAD_DIM * half) & (lane < HEAD_DIM * (half + 1))
            q_half = jnp.where(mine, query, jnp.zeros_like(query))
            g_half = jnp.where(mine, grad, jnp.zeros_like(grad))
            scores = jnp.where(allowed, mm(key, q_half, nt), mask_fill)
            weight = jnp.exp(scores - jnp.max(scores, axis=0, keepdims=True))
            probs = weight * (1.0 / jnp.sum(weight, axis=0, keepdims=True))
            g_probs = mm(value, g_half, nt)
            delta = jnp.sum(probs * g_probs, axis=0, keepdims=True)
            g_scores = (probs * (g_probs - delta)).astype(bf16)
            dv = dv + mm(probs.astype(bf16), g_half, nn)
            dk = dk + mm(g_scores, q_half, nn)
            dq.append(mm(key_t[HEAD_DIM * half : HEAD_DIM * (half + 1), low:high], g_scores, nn))
        dk_ref[low:high, :] = dk
        dv_ref[low:high, :] = dv
        dq = jnp.concatenate(dq, 0) * HEAD_DIM**-0.5
        out_ref[0, first:high, :] = dq.T.astype(bf16)
    out_ref[1] = dk_ref[...].astype(bf16)
    out_ref[2] = dv_ref[...].astype(bf16)


def attention(qkv, last):
    length, width = qkv.shape[0], qkv.shape[1] // 3
    pairs = width // 128
    part = lambda which: pl.BlockSpec((length, 128), lambda h: (0, which * pairs + h))
    return pl.pallas_call(
        forward_kernel,
        grid=(pairs,),
        in_specs=[pl.BlockSpec((1, length), lambda h: (0, 0)), part(0), part(1), part(2)],
        out_specs=pl.BlockSpec((length, 128), lambda h: (0, h)),
        out_shape=jax.ShapeDtypeStruct((length, width), bf16),
        compiler_params=pltpu.CompilerParams(vmem_limit_bytes=48 << 20),
        cost_estimate=pl.CostEstimate(
            flops=2 * length * 768 * 512 * pairs, bytes_accessed=8 * length * width, transcendentals=0
        ),
        name="attention_forward",
    )(last, qkv, qkv, qkv)


def attention_back(qkv, start, grad):
    length, width = grad.shape
    pairs = width // 128
    part = lambda which: pl.BlockSpec((length, 128), lambda h: (0, which * pairs + h))
    return pl.pallas_call(
        backward_kernel,
        grid=(pairs,),
        in_specs=[
            pl.BlockSpec((1, length), lambda h: (0, 0)),
            part(0),
            part(1),
            part(2),
            pl.BlockSpec((length, 128), lambda h: (0, h)),
        ],
        out_specs=pl.BlockSpec((3, length, 128), lambda h: (0, 0, h)),
        out_shape=jax.ShapeDtypeStruct((3, length, width), bf16),
        scratch_shapes=[pltpu.VMEM((length, 128), f32), pltpu.VMEM((length, 128), f32)],
        compiler_params=pltpu.CompilerParams(vmem_limit_bytes=48 << 20),
        cost_estimate=pl.CostEstimate(
            flops=5 * length * 768 * 512 * pairs, bytes_accessed=14 * length * width, transcendentals=0
        ),
        name="attention_backward",
    )(start, qkv, qkv, qkv, grad)


def newton_kernel(rows_ref, out_ref, x_ref, low_ref):
    dim = x_ref.shape[0]
    cols = x_ref.shape[1]
    chunk = min(cols, 512)
    total = jnp.zeros((1, 1), f32)
    for at in range(0, cols, chunk):
        part = rows_ref[at : at + chunk, :].astype(f32)
        total = total + jnp.sum(jnp.sum(part * part, axis=0, keepdims=True), axis=1, keepdims=True)
    inverse = 1.0 / (jnp.sqrt(total) + 1e-07)
    for at in range(0, cols, chunk):
        part = rows_ref[at : at + chunk, :].astype(f32).T * inverse
        x_ref[:, at : at + chunk] = part
        low_ref[:, at : at + chunk] = part.astype(bf16)
    diagonal = lax.broadcasted_iota(jnp.int32, (dim, dim), 0) == lax.broadcasted_iota(
        jnp.int32, (dim, dim), 1
    )

    def step(limit):
        gram = jnp.zeros((dim, dim), f32)
        for at in range(0, cols, chunk):
            part = low_ref[:, at : at + chunk]
            gram = gram + mm(part, part, nt)
        trace = jnp.sum(
            jnp.sum(jnp.where(diagonal, gram, 0.0), axis=0, keepdims=True), axis=1, keepdims=True
        )
        shift = trace * (1.0 / dim)
        rest = jnp.where(diagonal, gram - shift, gram)
        rest_low = rest.astype(bf16)
        poly = (newton_two + 2.0 * newton_three * shift) * rest + newton_three * mm(
            rest_low, rest_low, nn
        )
        poly = poly.astype(bf16)
        scale = newton_one + newton_two * shift + newton_three * shift * shift
        for at in range(0, limit, chunk):
            part = scale * x_ref[:, at : at + chunk] + mm(poly, low_ref[:, at : at + chunk], nn)
            x_ref[:, at : at + chunk] = part
            low_ref[:, at : at + chunk] = part.astype(bf16)

    @pl.loop(0, 4)
    def _(_):
        step(cols)

    kept = out_ref.shape[0]
    step(kept)
    for at in range(0, kept, chunk):
        out_ref[at : at + chunk, :] = x_ref[:, at : at + chunk].T.astype(bf16)


def newton(rows, kept):
    cols, dim = rows.shape
    return pl.pallas_call(
        newton_kernel,
        in_specs=[pl.BlockSpec(memory_space=pltpu.VMEM)],
        out_specs=pl.BlockSpec(memory_space=pltpu.VMEM),
        out_shape=jax.ShapeDtypeStruct((kept, dim), bf16),
        scratch_shapes=[pltpu.VMEM((dim, cols), f32), pltpu.VMEM((dim, cols), bf16)],
        compiler_params=pltpu.CompilerParams(vmem_limit_bytes=48 << 20),
        cost_estimate=pl.CostEstimate(
            flops=10 * dim * dim * (2 * cols + dim), bytes_accessed=4 * cols * dim, transcendentals=0
        ),
        name="newton",
    )(rows)


def shards(
    layer_in,
    doc_ids,
    out_grad,
    w_query,
    w_key,
    w_value,
    w_output,
    w_expand,
    w_contract,
    small_params,
    buffer_query,
    buffer_key,
    buffer_value,
    buffer_output,
    buffer_expand,
    buffer_contract,
    small_first,
    small_second,
):
    planes = lax.axis_size("mp")
    spots = lax.axis_size("dp")
    chips = spots // 2
    plane = lax.axis_index("mp")
    spot = lax.axis_index("dp")
    core = spot % 2
    length = layer_in.shape[1]
    token_span = length // planes
    head_cols = w_query.shape[1]
    hidden_rows = w_expand.shape[0]
    qkv_span = head_cols // spots
    hid_span = hidden_rows // spots
    to_planes = range(1, planes)
    to_chips = range(1, chips)

    columns = lambda w: lax.dynamic_slice_in_dim(w, spot * qkv_span, qkv_span, 1).T
    rows = lambda w, span: lax.dynamic_slice_in_dim(w, spot * span, span, 0)
    qkv_piece = jnp.concatenate([columns(w).astype(bf16) for w in (w_query, w_key, w_value)])
    rest_piece = jnp.concatenate(
        [
            rows(w_output, qkv_span).astype(bf16),
            rows(w_expand, hid_span).astype(bf16),
            rows(w_contract, hid_span).astype(bf16),
        ]
    )
    qkv_slots = gather_rows(qkv_piece).reshape(planes, spots, 3, qkv_span, D)
    qkv_weight = qkv_slots.transpose(2, 0, 1, 3, 4).reshape(3 * planes * head_cols, D)
    rest_slots = gather_rows(rest_piece).reshape(planes * spots, qkv_span + 2 * hid_span, D)
    output_full = rest_slots[:, :qkv_span].reshape(planes * head_cols, D)
    expand_full = rest_slots[:, qkv_span : qkv_span + hid_span].reshape(planes * hidden_rows, D)
    contract_full = rest_slots[:, qkv_span + hid_span :].reshape(planes * hidden_rows, D)

    def to_slots(bias):
        shaped = bias.reshape(planes, spots, hid_span)
        return reorder(reorder(shaped, plane, 0), spot, 1).reshape(-1)

    expansion_bias = to_slots(small_params[:FF])
    contraction_bias = small_params[FF : FF + D]
    alpha_attend = small_params[FF + D]
    alpha_ffn = small_params[FF + D + 1]

    inputs = pick(layer_in, plane)
    documents = pick(doc_ids, plane)
    last = (
        jnp.sum(documents[None, :] <= documents[:, None], axis=1, dtype=jnp.int32)[None, :] - 1
    )
    start = jnp.sum(documents[None, :] < documents[:, None], axis=1, dtype=jnp.int32)[None, :]
    grad_low = out_grad.astype(bf16)
    upstream = jnp.stack(
        [pick(grad_low, plane)] + [swap(pick(grad_low, plane ^ k), "mp", k) for k in to_planes]
    )
    upstream = reorder(upstream, plane, 0).reshape(length, D).astype(f32)

    qkv = mm(inputs, qkv_weight, nt).astype(bf16)
    heads = attention(qkv, last)
    attended = mm(heads, output_full, nn)
    middle = inputs.astype(f32) + alpha_attend * attended
    middle_low = middle.astype(bf16)
    pre = mm(middle_low, expand_full, nt) + expansion_bias
    hidden, gelu_back = jax.vjp(gelu_tanh, pre)
    hidden_low = hidden.astype(bf16)
    branch = mm(hidden_low, contract_full, nn) + contraction_bias
    layer_out = middle + alpha_ffn * branch

    def to_positions(whole):
        blocks = whole.astype(bf16).reshape(planes, token_span, D)
        got = jnp.stack(
            [pick(blocks, plane)] + [swap(pick(blocks, plane ^ k), "mp", k) for k in to_planes]
        )
        return reorder(got, plane, 0).astype(f32)

    layer_out = to_positions(layer_out)

    grad_alpha_ffn = jnp.sum(upstream * branch)
    branch_grad = (alpha_ffn * upstream).astype(bf16)
    grad_bias_contract = jnp.sum(branch_grad, axis=0, dtype=f32)
    grad_contract = mm(hidden_low, branch_grad, tn)
    hidden_grad = mm(branch_grad, contract_full, nt)
    pre_grad = gelu_back(hidden_grad)[0].astype(bf16)
    grad_bias_expand = to_slots(jnp.sum(pre_grad, axis=0, dtype=f32))
    grad_expand = mm(pre_grad, middle_low, tn)
    middle_grad = upstream + mm(pre_grad, expand_full, nn)
    grad_alpha_attend = jnp.sum(middle_grad * attended)
    attend_grad = (alpha_attend * middle_grad).astype(bf16)
    grad_output = mm(heads, attend_grad, tn)
    heads_grad = mm(attend_grad, output_full, nt).astype(bf16)

    ffn_shape = (planes, chips, 2, hid_span, D)
    is_zero = core == 0
    grad_expand = grad_expand.astype(bf16)
    grad_contract = grad_contract.astype(bf16)
    kept = jnp.where(is_zero, grad_expand, grad_contract).reshape(ffn_shape)
    given = jnp.where(is_zero, grad_contract, grad_expand).reshape(ffn_shape)
    ffn_sum = (kept.astype(f32) + jnp.flip(swap(given, "dp", 1), 2).astype(f32)).astype(bf16)
    got = [swap(ffn_sum[:, m], "dp", 2 * m) for m in to_chips]
    ffn_sum = ffn_sum[:, 0].astype(f32)
    for block in got:
        ffn_sum = ffn_sum + block.astype(f32)
    ffn_sum = ffn_sum.astype(bf16)
    got = [swap(ffn_sum[k], "mp", k) for k in to_planes]
    ffn_sum = ffn_sum[0].astype(f32)
    for block in got:
        ffn_sum = ffn_sum + block.astype(f32)
    ffn_buffer = jnp.where(is_zero, buffer_expand, buffer_contract)
    ffn_buffer = jnp.stack(
        [
            lax.dynamic_slice_in_dim(ffn_buffer, (spot ^ c) * hid_span, hid_span, 0)
            for c in range(2)
        ]
    )
    ffn_piece = (0.5 * ffn_buffer + ffn_sum).astype(bf16)
    ffn_rows = jnp.stack([ffn_piece] + [swap(ffn_piece, "mp", k) for k in to_planes])
    ffn_rows = jnp.stack([ffn_rows] + [swap(ffn_rows, "dp", 2 * m) for m in to_chips], 1)

    qkv_grad = attention_back(qkv, start, heads_grad)
    weight_three = qkv_weight.reshape(3, D, D)
    in_grad = middle_grad
    for which in range(3):
        in_grad = in_grad + mm(qkv_grad[which], weight_three[which], nn)
    grads = [mm(qkv_grad[which], inputs, tn).astype(bf16) for which in range(3)]
    grads.append(grad_output.astype(bf16))
    grads = jnp.stack(grads).reshape(4, planes, chips, 2, qkv_span, D)
    total = grads[:, :, :, 0].astype(f32) + swap(grads[:, :, :, 1], "dp", 1).astype(f32)
    total = total.astype(bf16)
    got = [swap(total[:, :, m], "dp", 2 * m) for m in to_chips]
    total = total[:, :, 0].astype(f32)
    for block in got:
        total = total + block.astype(f32)
    old = jnp.stack(
        [columns(w) for w in (buffer_query, buffer_key, buffer_value)]
        + [rows(buffer_output, qkv_span)]
    )
    total = jnp.concatenate([total[:, :1] + 0.5 * old[:, None], total[:, 1:]], 1)
    total = reorder(total, plane, 1)
    sent = total.astype(bf16)
    got = [swap(pick(sent, plane ^ k), "mp", k) for k in to_planes]
    total = pick(total, plane)
    for block in got:
        total = total + block.astype(f32)
    total = total.astype(bf16)
    att_rows = jnp.stack([total] + [swap(total, "dp", 2 * m) for m in to_chips], 1)
    att_rows = jnp.stack([att_rows, swap(att_rows, "dp", 1)], 2)
    att_rows = att_rows.reshape(D, D)

    in_grad = to_positions(in_grad)

    ffn_rows = ffn_rows.reshape(planes * hidden_rows, D)
    ffn_step = newton(ffn_rows, hidden_rows)

    def spread_ffn(mine):
        mine = reorder(mine.reshape(spots, hid_span, D), spot, 0).reshape(hidden_rows, D)
        other = swap(mine, "dp", 1)
        expand = jnp.where(is_zero, mine, other).astype(f32)
        contract = jnp.where(is_zero, other, mine).astype(f32)
        return expand, contract

    new_buffer_expand, new_buffer_contract = spread_ffn(ffn_rows[:hidden_rows])
    step_expand, step_contract = spread_ffn(ffn_step)

    def spread_att(whole):
        blocks = whole.reshape(planes, spots, qkv_span, D)
        got = jnp.stack(
            [pick(blocks, plane)] + [swap(pick(blocks, plane ^ k), "mp", k) for k in to_planes]
        )
        got = reorder(reorder(got, plane, 0), spot, 1).reshape(planes, head_cols, D).astype(f32)
        return got[0].T, got[1].T, got[2].T, got[3]

    att_buffers = spread_att(att_rows)
    att_steps = spread_att(newton(att_rows, D))

    small_local = jnp.concatenate(
        (grad_bias_expand, grad_bias_contract, jnp.stack((grad_alpha_attend, grad_alpha_ffn)))
    )
    small_grad = lax.psum(small_local, ("dp", "mp"))
    first_new = 0.5 * small_first + 0.5 * small_grad
    second_new = 0.5 * small_second + 0.5 * small_grad * small_grad
    correction = 1.0 - 0.5**STEP
    small_new = small_params - adam_rate * (first_new / correction) / (
        jnp.sqrt(second_new / correction) + 1e-08
    )
    buffers = att_buffers + (new_buffer_expand, new_buffer_contract)
    steps = att_steps + (step_expand, step_contract)
    weights_old = (w_query, w_key, w_value, w_output, w_expand, w_contract)
    new_weights = tuple(
        weight - rate * step for weight, rate, step in zip(weights_old, muon_rates, steps)
    )
    return (layer_out, in_grad) + buffers + new_weights + (small_new, first_new, second_new)


def solution(mesh):
    in_specs = (
        P("dp", None, None),
        P("dp", None),
        P("dp", "mp", None),
        P(None, "mp"),
        P(None, "mp"),
        P(None, "mp"),
        P("mp", None),
        P("mp", None),
        P("mp", None),
        P(),
        P(None, "mp"),
        P(None, "mp"),
        P(None, "mp"),
        P("mp", None),
        P("mp", None),
        P("mp", None),
        P(),
        P(),
    )
    out_specs = (
        P("dp", "mp", None),
        P("dp", "mp", None),
        P(None, "mp"),
        P(None, "mp"),
        P(None, "mp"),
        P("mp", None),
        P("mp", None),
        P("mp", None),
        P(None, "mp"),
        P(None, "mp"),
        P(None, "mp"),
        P("mp", None),
        P("mp", None),
        P("mp", None),
        P(),
        P(),
        P(),
    )
    whole = mesh.shape["mp"] == 4 and mesh.shape["dp"] == 8
    return jax.shard_map(shards if whole else general_shards, mesh=mesh, in_specs=in_specs, out_specs=out_specs, check_vma=False)
```

```python
import functools

import jax
import jax.numpy as jnp
from jax import lax
from jax.experimental import pallas as pl
from jax.experimental.pallas import tpu as pltpu
from jax.sharding import PartitionSpec as P

D = 512
HEAD_DIM = 64
FF = 2048
MICRO = 2
STEP = 10


newton_one = 3.4445
newton_two = -4.775
newton_three = 2.0315
muon_rates = (1.0, 1.0, 1.0, 5.0, 2.0, 1.0)
adam_rate = 0.25
mask_fill = -1e30
highest_precision = lax.Precision.HIGHEST


def shortened(x):
    return jax.tree.map(lambda a: a.astype(jnp.bfloat16) if a.dtype == jnp.float32 else a, x)


def gelu_tanh(values):
    return jax.nn.gelu(values, approximate=True)


def block_scores(query_blk, key_part, docs_query, docs_key, first_row):
    scores = jnp.einsum(
        "sqhd,skhd->shqk", query_blk, key_part, preferred_element_type=jnp.float32
    ) * HEAD_DIM ** (-0.5)
    rows_at = first_row + jnp.arange(query_blk.shape[1])
    cols_at = jnp.arange(key_part.shape[1])
    allowed = (rows_at[:, None] >= cols_at[None, :])[None] & (
        docs_query[:, :, None] == docs_key[:, None, :]
    )
    return jnp.where(allowed[:, None], scores, mask_fill)


def attend(query_all, key_all, value_all, documents, span_rows):
    block_outs = []
    log_sums = []
    for block_index in range(query_all.shape[1] // span_rows):
        row_start = block_index * span_rows
        finish = row_start + span_rows
        scores = block_scores(
            query_all[:, row_start:finish],
            key_all[:, :finish],
            documents[:, row_start:finish],
            documents[:, :finish],
            row_start,
        )
        row_peak = jnp.max(scores, axis=-1, keepdims=True)
        exponent = jnp.exp(scores - row_peak)
        row_total = jnp.sum(exponent, axis=-1, keepdims=True)
        prob_low = (exponent / row_total).astype(jnp.bfloat16)
        block_outs.append(
            jnp.einsum(
                "shqk,skhd->sqhd",
                prob_low,
                value_all[:, :finish],
                preferred_element_type=jnp.float32,
            ).astype(jnp.bfloat16)
        )
        log_sums.append(row_peak + jnp.log(row_total))
    return (jnp.concatenate(block_outs, 1), log_sums)


def attend_back(query_all, key_all, value_all, documents, span_rows, log_sums, heads_grad):
    query_grads = []
    key_grad = jnp.zeros(key_all.shape, jnp.float32)
    value_grad = jnp.zeros(value_all.shape, jnp.float32)
    scale = HEAD_DIM ** (-0.5)
    for block_index in range(query_all.shape[1] // span_rows):
        row_start = block_index * span_rows
        finish = row_start + span_rows
        query_blk = query_all[:, row_start:finish]
        scores = block_scores(
            query_blk,
            key_all[:, :finish],
            documents[:, row_start:finish],
            documents[:, :finish],
            row_start,
        )
        probs = jnp.exp(scores - log_sums[block_index])
        prob_low = probs.astype(jnp.bfloat16)
        grad_blk = heads_grad[:, row_start:finish]
        grad_probs = jnp.einsum(
            "sqhd,skhd->shqk", grad_blk, value_all[:, :finish], preferred_element_type=jnp.float32
        )
        row_delta = jnp.sum(probs * grad_probs, axis=-1, keepdims=True)
        grad_scores = (probs * (grad_probs - row_delta)).astype(jnp.bfloat16)
        query_grads.append(
            jnp.einsum(
                "shqk,skhd->sqhd",
                grad_scores,
                key_all[:, :finish],
                preferred_element_type=jnp.float32,
            )
            * scale
        )
        key_grad = key_grad.at[:, :finish].add(
            jnp.einsum(
                "shqk,sqhd->skhd", grad_scores, query_blk, preferred_element_type=jnp.float32
            )
            * scale
        )
        value_grad = value_grad.at[:, :finish].add(
            jnp.einsum("shqk,sqhd->skhd", prob_low, grad_blk, preferred_element_type=jnp.float32)
        )
    return (jnp.concatenate(query_grads, 1), key_grad, value_grad)


def gram_part(iterate, by_columns):
    if by_columns:
        return lax.dot_general(
            iterate,
            iterate,
            (((1,), (1,)), ((), ())),
            precision=highest_precision,
            preferred_element_type=jnp.float32,
        )
    return lax.dot_general(
        iterate,
        iterate,
        (((0,), (0,)), ((), ())),
        precision=highest_precision,
        preferred_element_type=jnp.float32,
    )


def newton_update(iterate, gram_sum, by_columns):
    square = jnp.dot(gram_sum, gram_sum, precision=highest_precision)
    polynomial = newton_two * gram_sum + newton_three * square
    if by_columns:
        applied = jnp.dot(polynomial, iterate, precision=highest_precision)
    else:
        applied = lax.dot_general(
            iterate,
            polynomial,
            (((1,), (1,)), ((), ())),
            precision=highest_precision,
            preferred_element_type=jnp.float32,
        )
    return newton_one * iterate + applied


def general_shards(
    layer_in,
    doc_ids,
    out_grad,
    w_query,
    w_key,
    w_value,
    w_output,
    w_expand,
    w_contract,
    small_params,
    buffer_query,
    buffer_key,
    buffer_value,
    buffer_output,
    buffer_expand,
    buffer_contract,
    small_first,
    small_second,
):
    group_count = lax.axis_size("mp")
    group_index = lax.axis_index("mp")
    seq_count, length, model_width = layer_in.shape
    per_micro = seq_count // MICRO
    token_span = length // group_count
    head_cols = w_query.shape[1]
    heads_here = head_cols // HEAD_DIM
    span_rows = min(512, length)
    expansion_bias = small_params[:FF]
    contraction_bias = small_params[FF : FF + D]
    alpha_attend = small_params[FF + D]
    alpha_ffn = small_params[FF + D + 1]
    query_key_value_weight = jnp.concatenate((w_query, w_key, w_value), 1).astype(jnp.bfloat16)
    row_local = (
        w_output.astype(jnp.bfloat16),
        w_expand.astype(jnp.bfloat16),
        w_contract.astype(jnp.bfloat16),
    )
    grad_qkv_weight = jnp.zeros((model_width, 3 * head_cols), jnp.float32)
    grad_output = jnp.zeros((D, D), jnp.float32)
    grad_expand = jnp.zeros((FF, D), jnp.float32)
    grad_contract = jnp.zeros((FF, D), jnp.float32)
    grad_bias_expand = jnp.zeros((FF,), jnp.float32)
    grad_bias_contract = jnp.zeros((D,), jnp.float32)
    grad_alpha_attend = jnp.zeros((), jnp.float32)
    grad_alpha_ffn = jnp.zeros((), jnp.float32)
    out_blocks = []
    grad_blocks = []
    for micro_index in range(MICRO):
        rows_from = micro_index * per_micro
        layer_inputs = layer_in[rows_from : rows_from + per_micro]
        documents = doc_ids[rows_from : rows_from + per_micro]
        upstream = out_grad[rows_from : rows_from + per_micro]
        query_key_value_rows = jnp.einsum(
            "orv,vx->orx", layer_inputs, query_key_value_weight, preferred_element_type=jnp.float32
        ).astype(jnp.bfloat16)
        qkv_split = query_key_value_rows.reshape(per_micro, length, 3, heads_here, HEAD_DIM)
        query_all = qkv_split[:, :, 0]
        key_all = qkv_split[:, :, 1]
        value_all = qkv_split[:, :, 2]
        head_outputs, log_sums = attend(query_all, key_all, value_all, documents, span_rows)
        heads_flat = head_outputs.reshape(per_micro, length, head_cols)
        heads_tok = lax.all_to_all(heads_flat, "mp", split_axis=1, concat_axis=2, tiled=True)
        row_now = (
            lax.all_gather(row_local[0], "mp", axis=0, tiled=True),
            lax.all_gather(row_local[1], "mp", axis=0, tiled=True),
            lax.all_gather(row_local[2], "mp", axis=0, tiled=True),
        )
        output_full, expand_full, contract_full = row_now
        attention_result = jnp.einsum(
            "std,de->ste", heads_tok, output_full, preferred_element_type=jnp.float32
        )
        local_in = lax.dynamic_slice_in_dim(
            layer_inputs, group_index * token_span, token_span, 1
        ).astype(jnp.float32)
        middle_activation = local_in + alpha_attend * attention_result
        middle_low = middle_activation.astype(jnp.bfloat16)
        preactivation = (
            jnp.einsum("std,fd->stf", middle_low, expand_full, preferred_element_type=jnp.float32)
            + expansion_bias
        )
        hidden_state, gelu_back = jax.vjp(gelu_tanh, preactivation)
        hidden_low = hidden_state.astype(jnp.bfloat16)
        residual_branch = (
            jnp.einsum("stf,fd->std", hidden_low, contract_full, preferred_element_type=jnp.float32)
            + contraction_bias
        )
        out_blocks.append(middle_activation + alpha_ffn * residual_branch)
        grad_alpha_ffn = grad_alpha_ffn + jnp.sum(upstream * residual_branch)
        branch_grad = (alpha_ffn * upstream).astype(jnp.bfloat16)
        grad_bias_contract = grad_bias_contract + jnp.sum(
            branch_grad, axis=(0, 1), dtype=jnp.float32
        )
        grad_contract = grad_contract + jnp.einsum(
            "stf,std->fd", hidden_low, branch_grad, preferred_element_type=jnp.float32
        )
        hidden_grad = jnp.einsum(
            "std,fd->stf", branch_grad, contract_full, preferred_element_type=jnp.float32
        )
        pre_grad = gelu_back(hidden_grad)[0].astype(jnp.bfloat16)
        grad_bias_expand = grad_bias_expand + jnp.sum(pre_grad, axis=(0, 1), dtype=jnp.float32)
        grad_expand = grad_expand + jnp.einsum(
            "stf,std->fd", pre_grad, middle_low, preferred_element_type=jnp.float32
        )
        middle_grad = upstream + jnp.einsum(
            "stf,fd->std", pre_grad, expand_full, preferred_element_type=jnp.float32
        )
        grad_alpha_attend = grad_alpha_attend + jnp.sum(middle_grad * attention_result)
        attend_grad = (alpha_attend * middle_grad).astype(jnp.bfloat16)
        grad_output = grad_output + jnp.einsum(
            "std,ste->de", heads_tok, attend_grad, preferred_element_type=jnp.float32
        )
        heads_grad_tok = jnp.einsum(
            "ste,de->std", attend_grad, output_full, preferred_element_type=jnp.float32
        ).astype(jnp.bfloat16)
        heads_grad = lax.all_to_all(heads_grad_tok, "mp", split_axis=2, concat_axis=1, tiled=True)
        heads_grad = heads_grad.reshape(per_micro, length, heads_here, HEAD_DIM)
        query_grad, key_grad, value_grad = attend_back(
            query_all, key_all, value_all, documents, span_rows, log_sums, heads_grad
        )
        query_key_value_gradient = (
            jnp.stack((query_grad, key_grad, value_grad), 2)
            .reshape(per_micro, length, 3 * head_cols)
            .astype(jnp.bfloat16)
        )
        grad_qkv_weight = grad_qkv_weight + jnp.einsum(
            "tmf,tmp->fp",
            layer_inputs,
            query_key_value_gradient,
            preferred_element_type=jnp.float32,
        )
        partial_grad = jnp.einsum(
            "nrj,yj->nry",
            query_key_value_gradient,
            query_key_value_weight,
            preferred_element_type=jnp.float32,
        )
        head_part = lax.psum_scatter(
            partial_grad.astype(jnp.bfloat16), "mp", scatter_dimension=1, tiled=True
        ).astype(jnp.float32)
        grad_blocks.append(middle_grad + head_part)
    layer_out = jnp.concatenate(out_blocks, 0)
    in_grad = jnp.concatenate(grad_blocks, 0)
    output_part, expand_part, contract_part = (
        lax.psum_scatter(
            grad_output.astype(jnp.bfloat16), "mp", scatter_dimension=0, tiled=True
        ).astype(jnp.float32),
        lax.psum_scatter(
            grad_expand.astype(jnp.bfloat16), "mp", scatter_dimension=0, tiled=True
        ).astype(jnp.float32),
        lax.psum_scatter(
            grad_contract.astype(jnp.bfloat16), "mp", scatter_dimension=0, tiled=True
        ).astype(jnp.float32),
    )
    matrix_grads = (
        lax.psum(grad_qkv_weight[:, :head_cols].astype(jnp.bfloat16), "dp").astype(jnp.float32),
        lax.psum(grad_qkv_weight[:, head_cols : 2 * head_cols].astype(jnp.bfloat16), "dp").astype(
            jnp.float32
        ),
        lax.psum(grad_qkv_weight[:, 2 * head_cols :].astype(jnp.bfloat16), "dp").astype(
            jnp.float32
        ),
        lax.psum(output_part.astype(jnp.bfloat16), "dp").astype(jnp.float32),
        lax.psum(expand_part.astype(jnp.bfloat16), "dp").astype(jnp.float32),
        lax.psum(contract_part.astype(jnp.bfloat16), "dp").astype(jnp.float32),
    )
    small_local = jnp.concatenate(
        (grad_bias_expand, grad_bias_contract, jnp.stack((grad_alpha_attend, grad_alpha_ffn)))
    )
    small_grad = lax.psum(small_local, ("dp", "mp"))
    first_new = 0.5 * small_first + 0.5 * small_grad
    second_new = 0.5 * small_second + 0.5 * small_grad * small_grad
    correction = 1.0 - 0.5**STEP
    small_new = small_params - adam_rate * (first_new / correction) / (
        jnp.sqrt(second_new / correction) + 1e-08
    )
    olds = (buffer_query, buffer_key, buffer_value, buffer_output, buffer_expand, buffer_contract)
    weights_old = (w_query, w_key, w_value, w_output, w_expand, w_contract)
    by_columns = (True, True, True, False, False, False)
    buffers = tuple(
        (0.5 * old_buffer + grad_matrix for old_buffer, grad_matrix in zip(olds, matrix_grads))
    )
    squares = lax.psum(tuple((jnp.sum(matrix * matrix) for matrix in buffers)), "mp")
    iterates = [
        matrix / (jnp.sqrt(square_sum) + 1e-07) for matrix, square_sum in zip(buffers, squares)
    ]
    for newton_step in range(5):
        gram_sums = jax.tree.map(
            lambda part: part.astype(jnp.float32),
            lax.psum(
                shortened(
                    tuple(
                        (
                            gram_part(iterate, column_flag)
                            for iterate, column_flag in zip(iterates, by_columns)
                        )
                    )
                ),
                "mp",
            ),
        )
        iterates = [
            newton_update(iterate, gram_sum, column_flag)
            for iterate, gram_sum, column_flag in zip(iterates, gram_sums, by_columns)
        ]
    new_weights = tuple(
        (
            weight - rate * iterate
            for weight, rate, iterate in zip(weights_old, muon_rates, iterates)
        )
    )
    return (layer_out, in_grad) + buffers + new_weights + (small_new, first_new, second_new)


max_doc = 512
q_rows = 256
f32 = jnp.float32
bf16 = jnp.bfloat16
nt = (((1,), (1,)), ((), ()))
nn = (((1,), (0,)), ((), ()))
tn = (((0,), (0,)), ((), ()))
gelu_root = 0.7978845608028654
gelu_cube = 0.044715


def mm(a, b, dims):
    return lax.dot_general(a, b, dims, preferred_element_type=f32)


def swap(x, axis, mask):
    size = lax.axis_size(axis)
    return lax.ppermute(x, axis, [(a, a ^ mask) for a in range(size)])


def reorder(x, index, axis):
    parts = [
        lax.dynamic_slice_in_dim(x, slot ^ index, 1, axis) for slot in range(x.shape[axis])
    ]
    return jnp.concatenate(parts, axis)


def pick(x, index):
    return lax.dynamic_index_in_dim(x, index, 0, keepdims=False)


def like(shape, dtype):
    return jax.ShapeDtypeStruct(shape, dtype)


whole = pl.BlockSpec(memory_space=pltpu.VMEM)


def run(kernel, place, args, outs, name, grid=(1,), in_specs=None, out_specs=None, scratch=(), flops=0):
    moved = sum(a.size * a.dtype.itemsize for a in args)
    moved += sum(o.size * jnp.dtype(o.dtype).itemsize for o in outs)
    return pl.pallas_call(
        kernel,
        grid_spec=pltpu.PrefetchScalarGridSpec(
            num_scalar_prefetch=1,
            grid=grid,
            in_specs=in_specs or [whole] * len(args),
            out_specs=out_specs or [whole] * len(outs),
            scratch_shapes=list(scratch),
        ),
        out_shape=list(outs),
        compiler_params=pltpu.CompilerParams(vmem_limit_bytes=56 << 20),
        cost_estimate=pl.CostEstimate(flops=flops, bytes_accessed=moved, transcendentals=0),
        name=name,
    )(place, *args)


def weight_pieces_kernel(place, q, k, v, o, e, c, qkv_out, rest_out, turned):
    span = o.shape[0]
    at = pl.multiple_of(place[1] * span, span)
    for which, ref in enumerate((q, k, v)):
        turned[...] = ref[...].T
        qkv_out[which * span : (which + 1) * span, :] = turned[pl.ds(at, span), :].astype(bf16)
    hid = e.shape[0]
    rest_out[:span, :] = o[...].astype(bf16)
    rest_out[span : span + hid, :] = e[...].astype(bf16)
    rest_out[span + hid :, :] = c[...].astype(bf16)


def buffer_pieces_kernel(place, q, k, v, o, e, c, att_out, ffn_out, turned):
    span = o.shape[0]
    at = pl.multiple_of(place[1] * span, span)
    for which, ref in enumerate((q, k, v)):
        turned[...] = ref[...].T
        att_out[which] = 0.5 * turned[pl.ds(at, span), :]
    att_out[3] = 0.5 * o[...]
    ffn_out[0] = 0.5 * c[...]
    ffn_out[1] = 0.5 * e[...]


def pieces(kernel, place, arrays, outs, name):
    q, k, v, o, e, c = arrays
    spots = lax.axis_size("dp")
    span, hid = o.shape[0] // spots, e.shape[0] // spots
    row = lambda size: pl.BlockSpec((size, D), lambda g, place: (place[1], 0))
    return run(
        kernel,
        place,
        arrays,
        outs,
        name,
        in_specs=[whole, whole, whole, row(span), row(hid), row(hid)],
        scratch=[pltpu.VMEM((q.shape[1], D), f32)],
    )


def split_positions_kernel(place, *refs):
    count = len(refs) // 2
    for u in range(count):
        refs[count + u][...] = refs[u][0].astype(bf16)


def split_positions(x, place):
    planes, span, width = x.shape
    block = lambda u: pl.BlockSpec((1, span, width), lambda g, place: (place[0] ^ u, 0, 0))
    return run(
        split_positions_kernel,
        place,
        [x] * planes,
        [like((span, width), bf16)] * planes,
        "split_positions",
        in_specs=[block(u) for u in range(planes)],
    )


def join_positions_kernel(place, *refs):
    out = refs[-1]
    for u, ref in enumerate(refs[:-1]):
        out[place[0] ^ u] = ref[...].astype(f32)


def join_positions(parts, place):
    span, width = parts[0].shape
    return run(
        join_positions_kernel,
        place,
        parts,
        [like((len(parts), span, width), f32)],
        "join_positions",
    )[0]


def window(first_row):
    return max(0, first_row + 1 - max_doc) // 128 * 128


def pair_weights(halves, which, span):
    return jnp.concatenate([half[0, which * span : (which + 1) * span, :] for half in halves], 0)


def interleave(own, other):
    return [half for pair in zip(own, other) for half in pair]


def forward_kernel(place, last_ref, in_ref, *refs):
    halves, (qkv_ref, o_ref) = refs[:-2], refs[-2:]
    length = in_ref.shape[0]
    span = halves[0].shape[1] // 3
    for which in range(3):
        weight = pair_weights(halves, which, span)
        qkv_ref[which] = mm(in_ref[...], weight, nt).astype(bf16)
    lane = lax.broadcasted_iota(jnp.int32, (q_rows, 128), 1)
    for first in range(0, length, q_rows):
        low, high = window(first), first + q_rows
        row = first + lax.broadcasted_iota(jnp.int32, (q_rows, high - low), 0)
        col = low + lax.broadcasted_iota(jnp.int32, (q_rows, high - low), 1)
        allowed = (col <= row) & (row <= last_ref[:, low:high])
        query = qkv_ref[0, first:high, :] * jnp.asarray(HEAD_DIM**-0.5, bf16)
        halves = []
        for half in range(2):
            mine = (lane >= HEAD_DIM * half) & (lane < HEAD_DIM * (half + 1))
            scores = mm(jnp.where(mine, query, jnp.zeros_like(query)), qkv_ref[1, low:high, :], nt)
            scores = jnp.where(allowed, scores, mask_fill)
            weight = jnp.exp(scores - jnp.max(scores, axis=1, keepdims=True))
            total = jnp.sum(weight, axis=1, keepdims=True)
            halves.append(mm((weight * (1.0 / total)).astype(bf16), qkv_ref[2, low:high, :], nn))
        o_ref[first:high, :] = jnp.where(lane < HEAD_DIM, halves[0], halves[1]).astype(bf16)


def attention(place, last, inputs, halves):
    length = inputs.shape[0]
    planes, rows, _ = halves[0].shape
    half = pl.BlockSpec((1, rows, D), lambda h, place: (h, 0, 0))
    return run(
        forward_kernel,
        place,
        [last, inputs, *halves],
        [like((3, length, D), bf16), like((length, D), bf16)],
        "attention_forward",
        grid=(planes,),
        in_specs=[whole, whole] + [half] * len(halves),
        out_specs=[
            pl.BlockSpec((3, length, 128), lambda h, place: (0, 0, h)),
            pl.BlockSpec((length, 128), lambda h, place: (0, h)),
        ],
        flops=8 * length * D * D + 2 * length * 768 * 512 * planes,
    )


def backward_kernel(is_last, spots, place, start_ref, in_ref, qkv_ref, g_ref, gout_ref, gmid_ref, *rest):
    halves, rest = rest[:spots], rest[spots:]
    ins, (keep_ref, give_ref, dk_ref, dv_ref, dq_ref, acc_ref) = rest[:-6], rest[-6:]
    length = in_ref.shape[0]
    span = halves[0].shape[1] // 3
    chips = spots // 2
    step = pl.program_id(0)
    lane = lax.broadcasted_iota(jnp.int32, (q_rows, 128), 1)
    dk_ref[...] = jnp.zeros_like(dk_ref)
    dv_ref[...] = jnp.zeros_like(dv_ref)
    key_t = qkv_ref[1].astype(f32).T.astype(bf16)
    for first in range(0, length, q_rows):
        low, high = window(first), first + q_rows
        col = low + lax.broadcasted_iota(jnp.int32, (high - low, q_rows), 0)
        row = first + lax.broadcasted_iota(jnp.int32, (high - low, q_rows), 1)
        allowed = (col <= row) & (col >= start_ref[:, first:high])
        query = qkv_ref[0, first:high, :] * jnp.asarray(HEAD_DIM**-0.5, bf16)
        grad = g_ref[first:high, :]
        key = qkv_ref[1, low:high, :]
        value = qkv_ref[2, low:high, :]
        dk = dk_ref[low:high, :]
        dv = dv_ref[low:high, :]
        dq = []
        for half in range(2):
            mine = (lane >= HEAD_DIM * half) & (lane < HEAD_DIM * (half + 1))
            q_half = jnp.where(mine, query, jnp.zeros_like(query))
            g_half = jnp.where(mine, grad, jnp.zeros_like(grad))
            scores = jnp.where(allowed, mm(key, q_half, nt), mask_fill)
            weight = jnp.exp(scores - jnp.max(scores, axis=0, keepdims=True))
            probs = weight * (1.0 / jnp.sum(weight, axis=0, keepdims=True))
            g_probs = mm(value, g_half, nt)
            delta = jnp.sum(probs * g_probs, axis=0, keepdims=True)
            g_scores = (probs * (g_probs - delta)).astype(bf16)
            dv = dv + mm(probs.astype(bf16), g_half, nn)
            dk = dk + mm(g_scores, q_half, nn)
            dq.append(mm(key_t[HEAD_DIM * half : HEAD_DIM * (half + 1), low:high], g_scores, nn))
        dk_ref[low:high, :] = dk
        dv_ref[low:high, :] = dv
        dq = jnp.concatenate(dq, 0) * HEAD_DIM**-0.5
        dq_ref[first:high, :] = dq.T.astype(bf16)
    grads = (dq_ref[...], dk_ref[...].astype(bf16), dv_ref[...].astype(bf16))

    @pl.when(step == 0)
    def _():
        acc_ref[...] = gmid_ref[...]

    for which, grad in enumerate(grads):
        acc_ref[...] += mm(grad, pair_weights(halves, which, span), nn)
    for which in range(4):
        if which < 3:
            rows = mm(grads[which], in_ref[...], tn).astype(bf16)
        else:
            rows = gout_ref[...]
        for m in range(chips):
            for c, ref in enumerate((keep_ref, give_ref)):
                at = (2 * m + c) * span
                ref[m, 0, which * span : (which + 1) * span, :] = rows[at : at + span, :]

    @pl.when(step == pl.num_programs(0) - 1)
    def _():
        if not is_last:
            ins[0][...] = acc_ref[...]
            return
        rows = ins[0].shape[0]
        for u, ref in enumerate(ins):
            at = pl.multiple_of((place[0] ^ u) * rows, rows)
            ref[...] = acc_ref[pl.ds(at, rows), :].astype(bf16)


def attention_back(
    place, start, inputs, halves, qkv, heads_grad, grad_output, so_far, first, count, is_last
):
    length = inputs.shape[0]
    planes, rows, _ = halves[0].shape
    spots = len(halves)
    chips = spots // 2
    span = rows // 3
    half = pl.BlockSpec((1, rows, D), lambda h, place: (first + h, 0, 0))
    out_half = pl.BlockSpec((chips, 1, 4 * span, D), lambda h, place: (0, h, 0, 0))
    outs = [like((length // planes, D), bf16)] * planes if is_last else [like((length, D), f32)]
    out = run(
        functools.partial(backward_kernel, is_last, spots),
        place,
        [start, inputs, qkv, heads_grad, grad_output, so_far, *halves],
        outs + [like((chips, count, 4 * span, D), bf16)] * 2,
        "attention_backward",
        grid=(count,),
        in_specs=[
            whole,
            whole,
            pl.BlockSpec((3, length, 128), lambda h, place: (0, 0, first + h)),
            pl.BlockSpec((length, 128), lambda h, place: (0, first + h)),
            pl.BlockSpec((128, D), lambda h, place: (first + h, 0)),
            whole,
        ]
        + [half] * spots,
        out_specs=[whole] * len(outs) + [out_half] * 2,
        scratch=[
            pltpu.VMEM((length, 128), f32),
            pltpu.VMEM((length, 128), f32),
            pltpu.VMEM((length, 128), bf16),
            pltpu.VMEM((length, D), f32),
        ],
        flops=(12 * length * D * D + 5 * length * 768 * 512 * planes) * count // planes,
    )
    return out[:-2], out[-2], out[-1]


def ffn_kernel(planes, spots, place, *refs):
    alphas, in_ref, heads_ref = refs[:3]
    ups = refs[3 : 3 + planes]
    halves = refs[3 + planes : 3 + planes + spots]
    bias_ref, bout_ref = refs[3 + planes + spots : 5 + planes + spots]
    outs = refs[5 + planes + spots :]
    lays = outs[:planes]
    g_ref, gout_ref, gheads_ref, gmid_ref, gbin_ref, gbout_ref, galpha_ref = outs[
        planes : planes + 7
    ]
    attended, middle, mid_low, g_low, up, branch, o_low, lay, weights = outs[planes + 7 :]
    chips = spots // 2
    length = in_ref.shape[0]
    block = length // planes
    hid = g_ref.shape[3] // planes
    span = halves[0].shape[1] - 2 * hid
    core, chip = pl.program_id(0), pl.program_id(1)
    alpha_att, alpha_ffn = alphas[0], alphas[1]
    tiles = [slice(at, at + 256) for at in range(0, length, 256)]

    @pl.when((core == 0) & (chip == 0))
    def _():
        for k in range(planes):
            for at, half in enumerate(halves):
                m, c = at // 2, at % 2
                row = (k * spots + at) * span
                o_low[row : row + span, :] = half[k, :span, :]
                row = span
                for which in range(2):
                    weights[c, m, which, k * hid : (k + 1) * hid, :] = half[k, row : row + hid, :]
                    row += hid
        for u in range(planes):
            at = pl.multiple_of((place[0] ^ u) * block, block)
            up[pl.ds(at, block), :] = ups[u][...]
        total = jnp.zeros((1, D), f32)
        for t in tiles:
            found = mm(heads_ref[t, :], o_low[...], nn)
            attended[t, :] = found
            mid = in_ref[t, :].astype(f32) + alpha_att * found
            middle[t, :] = mid
            mid_low[t, :] = mid.astype(bf16)
            upstream = up[t, :].astype(f32)
            grad = (alpha_ffn * upstream).astype(bf16)
            g_low[t, :] = grad
            total = total + jnp.sum(grad.astype(f32), axis=0, keepdims=True)
            branch[t, :] = jnp.zeros((256, D), f32)
            gmid_ref[t, :] = upstream
        gbout_ref[...] = total

    expand = weights[core, chip, 0]
    contract = weights[core, chip, 1]
    bias = bias_ref[0, 0]
    gc = jnp.zeros((planes * hid, D), f32)
    ge = jnp.zeros((planes * hid, D), f32)
    gb = jnp.zeros((1, planes * hid), f32)
    for t in tiles:
        mid = mid_low[t, :]
        grad = g_low[t, :]
        pre = mm(mid, expand, nt) + bias
        square = pre * pre
        tanh = jnp.tanh(gelu_root * pre * (1.0 + gelu_cube * square))
        half = 0.5 * (1.0 + tanh)
        hidden = (pre * half).astype(bf16)
        slope = half + (0.5 * gelu_root) * pre * (1.0 - tanh * tanh) * (
            1.0 + (3.0 * gelu_cube) * square
        )
        branch[t, :] += mm(hidden, contract, nn)
        g_pre = (mm(grad, contract, nt) * slope).astype(bf16)
        gmid_ref[t, :] += mm(g_pre, expand, nn)
        gc = gc + mm(hidden, grad, tn)
        ge = ge + mm(g_pre, mid, tn)
        gb = gb + jnp.sum(g_pre.astype(f32), axis=0, keepdims=True)
    g_ref[0, 0, 0] = gc.astype(bf16)
    g_ref[0, 0, 1] = ge.astype(bf16)
    gbin_ref[0, 0] = gb

    @pl.when((core == 1) & (chip == chips - 1))
    def _():
        sum_ffn = jnp.zeros((1, D), f32)
        sum_att = jnp.zeros((1, D), f32)
        gout = jnp.zeros((D, D), f32)
        for t in tiles:
            final = branch[t, :] + bout_ref[...]
            lay[t, :] = middle[t, :] + alpha_ffn * final
            sum_ffn = sum_ffn + jnp.sum(up[t, :].astype(f32) * final, axis=0, keepdims=True)
            gm = gmid_ref[t, :]
            sum_att = sum_att + jnp.sum(gm * attended[t, :], axis=0, keepdims=True)
            g_att = (alpha_att * gm).astype(bf16)
            gout = gout + mm(heads_ref[t, :], g_att, tn)
            gheads_ref[t, :] = mm(g_att, o_low[...], nt).astype(bf16)
        gout_ref[...] = gout.astype(bf16)
        galpha_ref[0:1, :] = sum_att
        galpha_ref[1:2, :] = sum_ffn
        for u, ref in enumerate(lays):
            at = pl.multiple_of((place[0] ^ u) * block, block)
            ref[...] = lay[pl.ds(at, block), :].astype(bf16)


def feed_forward(place, alphas, inputs, heads, ups, halves, bias, bout):
    length = inputs.shape[0]
    planes = len(ups)
    spots = len(halves)
    chips = spots // 2
    hid = bias.shape[-1]
    step = lambda *tail: pl.BlockSpec((1, 1) + tail, lambda c, m, place: (c, m) + (0,) * len(tail))
    out = run(
        functools.partial(ffn_kernel, planes, spots),
        place,
        [alphas, inputs, heads, *ups, *halves, bias, bout],
        [like((length // planes, D), bf16)] * planes
        + [
            like((2, chips, 2, hid, D), bf16),
            like((D, D), bf16),
            like((length, D), bf16),
            like((length, D), f32),
            like((2, chips, 1, hid), f32),
            like((1, D), f32),
            like((2, D), f32),
        ],
        "feed_forward",
        grid=(2, chips),
        in_specs=[pl.BlockSpec(memory_space=pltpu.SMEM)]
        + [whole] * (2 + planes + spots)
        + [step(1, hid), whole],
        out_specs=[whole] * planes
        + [step(2, hid, D), whole, whole, whole, step(1, hid), whole, whole],
        scratch=[
            pltpu.VMEM((length, D), f32),
            pltpu.VMEM((length, D), f32),
            pltpu.VMEM((length, D), bf16),
            pltpu.VMEM((length, D), bf16),
            pltpu.VMEM((length, D), bf16),
            pltpu.VMEM((length, D), f32),
            pltpu.VMEM((D, D), bf16),
            pltpu.VMEM((length, D), f32),
            pltpu.VMEM((2, chips, 2, hid, D), bf16),
        ],
        flops=12 * length * D * 2 * chips * hid,
    )
    return out[:planes], out[planes:]


def sum_kernel(count, place, *refs):
    ins, outs = refs[:count], refs[count:]
    rows = outs[0].shape[0]
    for at, out in enumerate(outs):
        span = slice(at * rows, (at + 1) * rows)
        total = ins[0][span, :].astype(f32)
        for ref in ins[1:]:
            total = total + ref[span, :].astype(f32)
        out[...] = total.astype(out.dtype)


def sum_parts(place, ins, parts, name):
    rows = ins[0].shape[0] // parts
    return run(
        functools.partial(sum_kernel, len(ins)),
        place,
        ins,
        [like((rows, ins[0].shape[1]), bf16)] * parts,
        name,
    )


def small_write(out, total):
    at = out.shape[0] - 2 * total.shape[0]
    high = total.astype(bf16)
    out[at : at + total.shape[0], :] = high
    out[at + total.shape[0] :, :] = (total - high.astype(f32)).astype(bf16)


def small_read(ref):
    rows = ref.shape[0]
    return ref[rows - 16 : rows - 8, :].astype(f32) + ref[rows - 8 :, :].astype(f32)


def ffn_core_kernel(place, own, got, small, *outs):
    rows = own.shape[0] // len(outs)
    total = small[...]
    for at, out in enumerate(outs):
        for r in range(0, rows, 256):
            a = own[at * rows + r : at * rows + r + 256, :].astype(f32)
            b = got[at * rows + r : at * rows + r + 256, :].astype(f32)
            out[r : r + 256, :] = (a + b).astype(bf16)
        small_write(out, total)


def ffn_chip_kernel(count, hid, place, *refs):
    ins, outs = refs[:count], refs[count:]
    small = small_read(ins[0])
    for ref in ins[1:]:
        small = small + small_read(ref)
    for k, out in enumerate(outs):
        for which in range(2):
            at = (which * len(outs) + k) * hid
            total = ins[0][at : at + hid, :].astype(f32)
            for ref in ins[1:]:
                total = total + ref[at : at + hid, :].astype(f32)
            out[which * hid : (which + 1) * hid, :] = total.astype(bf16)
        small_write(out, small)


def ffn_plane_kernel(place, old, *refs):
    ins, (out, small_out) = refs[:-2], refs[-2:]
    rows = out.shape[0]
    total = old[...].reshape(rows, D)
    small = small_read(ins[0])
    for ref in ins:
        total = total + ref[:rows, :].astype(f32)
    for ref in ins[1:]:
        small = small + small_read(ref)
    out[...] = total.astype(bf16)
    small_out[...] = small


def att_to_owner_kernel(chips, planes, place, *refs):
    ins, old, outs, scratch = refs[:chips], refs[chips], refs[chips + 1 : -1], refs[-1]
    span = old.shape[1]
    for k in range(planes):
        for which in range(4):
            at = (k * 4 + which) * span
            total = ins[0][at : at + span, :].astype(f32)
            for ref in ins[1:]:
                total = total + ref[at : at + span, :].astype(f32)
            if k == 0:
                total = total + old[which]
            scratch[which, k * span : (k + 1) * span, :] = total.astype(bf16)
    for u, out in enumerate(outs):
        out[...] = scratch[place[0] ^ u]


def att_sum_kernel(planes, place, *refs):
    ins, out = refs[:-1], refs[-1]
    span = out.shape[0] // planes
    for k in range(planes):
        total = jnp.zeros((span, D), f32)
        for u, ref in enumerate(ins):
            at = (k ^ u) * span
            total = total + ref[at : at + span, :].astype(f32)
        out[k * span : (k + 1) * span, :] = total.astype(bf16)


def spread_kernel(spots, place, *refs):
    halves, outs = refs[:spots], refs[spots:]
    span = outs[0].shape[0] // spots
    for at, half in enumerate(halves):
        to = pl.multiple_of((place[1] ^ at) * span, span)
        for k, out in enumerate(outs):
            out[pl.ds(to, span), :] = half[k * span : (k + 1) * span, :]


def newton_kernel(planes, spots, first_only, place, *refs):
    halves, outs, x_ref, low_ref = refs[:spots], refs[spots:-2], refs[-2], refs[-1]
    dim, cols = x_ref.shape
    span = cols // (planes * spots)
    group = spots * span
    chunk = 512
    total = jnp.zeros((1, D), f32)
    for half in halves:
        part = half[: planes * span, :].astype(f32)
        total = total + jnp.sum(part * part, axis=0, keepdims=True)
    inverse = 1.0 / (jnp.sqrt(jnp.sum(total, axis=1, keepdims=True)) + 1e-07)
    for k in range(planes):
        rows = [half[k * span : (k + 1) * span, :] for half in halves]
        part = jnp.concatenate(rows, 0).astype(f32).T * inverse
        x_ref[:, k * group : (k + 1) * group] = part
        low_ref[:, k * group : (k + 1) * group] = part.astype(bf16)
    diagonal = lax.broadcasted_iota(jnp.int32, (dim, dim), 0) == lax.broadcasted_iota(
        jnp.int32, (dim, dim), 1
    )

    def step(limit):
        gram = jnp.zeros((dim, dim), f32)
        for at in range(0, cols, chunk):
            part = low_ref[:, at : at + chunk]
            gram = gram + mm(part, part, nt)
        trace = jnp.sum(
            jnp.sum(jnp.where(diagonal, gram, 0.0), axis=0, keepdims=True), axis=1, keepdims=True
        )
        shift = trace * (1.0 / dim)
        rest = jnp.where(diagonal, gram - shift, gram)
        rest_low = rest.astype(bf16)
        poly = (newton_two + 2.0 * newton_three * shift) * rest + newton_three * mm(
            rest_low, rest_low, nn
        )
        poly = poly.astype(bf16)
        scale = newton_one + newton_two * shift + newton_three * shift * shift
        for at in range(0, limit, chunk):
            part = scale * x_ref[:, at : at + chunk] + mm(poly, low_ref[:, at : at + chunk], nn)
            x_ref[:, at : at + chunk] = part
            low_ref[:, at : at + chunk] = part.astype(bf16)

    @pl.loop(0, 4)
    def _(_):
        step(cols)

    step(group if first_only else cols)
    for k, out in enumerate(outs):
        part = x_ref[:, k * group : (k + 1) * group].T.astype(bf16)
        for at in range(spots):
            to = pl.multiple_of((place[1] ^ at) * span, span)
            out[pl.ds(to, span), :] = part[at * span : (at + 1) * span, :]


def newton(place, halves, planes, first_only, name):
    spots = len(halves)
    cols = spots * halves[0].shape[0]
    count = 1 if first_only else planes
    return run(
        functools.partial(newton_kernel, planes, spots, first_only),
        place,
        halves,
        [like((cols // planes, D), bf16)] * count,
        name,
        scratch=[pltpu.VMEM((D, cols), f32), pltpu.VMEM((D, cols), bf16)],
        flops=10 * D * D * (2 * cols + D),
    )


def att_final_kernel(planes, place, *refs):
    ms, xs = refs[:planes], refs[planes : 2 * planes]
    old = refs[2 * planes : 2 * planes + 4]
    outs, scratch = refs[2 * planes + 4 : -1], refs[-1]
    for u in range(planes):
        scratch[0, u] = ms[u][...]
        scratch[1, u] = xs[u][...]
    for which in range(4):
        m = scratch[0, place[0] ^ which].astype(f32)
        x = scratch[1, place[0] ^ which].astype(f32)
        if which < 3:
            m, x = m.T, x.T
        outs[which][...] = m
        outs[4 + which][...] = old[which][...] - muon_rates[which] * x


def ffn_give_kernel(planes, hid, place, *refs):
    count = len(refs) // 3
    ins, give, keep = refs[:count], refs[count : 2 * count], refs[2 * count :]

    def fill(given):
        for m in range(count):
            for k in range(planes):
                to = slice(k * hid, (k + 1) * hid)
                at = (2 * k + given) * hid
                give[m][to, :] = ins[m][at : at + hid, :]
                at = (2 * k + 1 - given) * hid
                keep[m][to, :] = ins[m][at : at + hid, :]
            give[m][planes * hid :, :] = keep[m][:hid, :]

    @pl.when(place[1] % 2 == 0)
    def _():
        fill(0)

    @pl.when(place[1] % 2 == 1)
    def _():
        fill(1)


def ffn_buffers_kernel(chips, hid, place, *refs):
    give, keep, got = refs[:chips], refs[chips : 2 * chips], refs[2 * chips : 3 * chips]
    eo, co = refs[3 * chips :]
    tail = keep[0].shape[0]

    def fill(kept, given):
        for m in range(chips):
            one = pl.multiple_of((place[1] ^ (2 * m)) * hid, hid)
            two = pl.multiple_of((place[1] ^ (2 * m + 1)) * hid, hid)
            kept[pl.ds(one, hid), :] = keep[m][:hid, :].astype(f32)
            kept[pl.ds(two, hid), :] = got[m][:hid, :].astype(f32)
            given[pl.ds(one, hid), :] = give[m][:hid, :].astype(f32)
            given[pl.ds(two, hid), :] = got[m][tail:, :].astype(f32)

    @pl.when(place[1] % 2 == 0)
    def _():
        fill(eo, co)

    @pl.when(place[1] % 2 == 1)
    def _():
        fill(co, eo)


def ffn_final_kernel(place, mine, got, we, wc, eo, co):
    def fill(e, c):
        eo[...] = we[...] - muon_rates[4] * e[...].astype(f32)
        co[...] = wc[...] - muon_rates[5] * c[...].astype(f32)

    @pl.when(place[1] % 2 == 0)
    def _():
        fill(mine, got)

    @pl.when(place[1] % 2 == 1)
    def _():
        fill(got, mine)


def shards(
    layer_in,
    doc_ids,
    out_grad,
    w_query,
    w_key,
    w_value,
    w_output,
    w_expand,
    w_contract,
    small_params,
    buffer_query,
    buffer_key,
    buffer_value,
    buffer_output,
    buffer_expand,
    buffer_contract,
    small_first,
    small_second,
):
    planes = lax.axis_size("mp")
    spots = lax.axis_size("dp")
    chips = spots // 2
    plane = lax.axis_index("mp")
    spot = lax.axis_index("dp")
    place = jnp.stack([plane, spot]).astype(jnp.int32)
    length = layer_in.shape[1]
    head_cols = w_query.shape[1]
    hidden_rows = w_expand.shape[0]
    span = head_cols // spots
    hid = hidden_rows // spots
    to_planes = range(1, planes)
    to_chips = range(1, chips)
    weights_old = (w_query, w_key, w_value, w_output, w_expand, w_contract)
    buffers_old = (
        buffer_query,
        buffer_key,
        buffer_value,
        buffer_output,
        buffer_expand,
        buffer_contract,
    )

    def around_planes(x):
        return [x] + [swap(x, "mp", k) for k in to_planes]

    def around_chips(x):
        return [x] + [swap(x, "dp", 2 * m) for m in to_chips]

    def together(*groups):
        return lax.optimization_barrier(groups)

    qkv_piece, rest_piece = pieces(
        weight_pieces_kernel,
        place,
        weights_old,
        [like((3 * span, D), bf16), like((span + 2 * hid, D), bf16)],
        "weight_pieces",
    )
    qkv_own, rest_piece = together(jnp.stack(around_planes(qkv_piece)), rest_piece)
    qkv_own, rest_own = around_chips(qkv_own), around_planes(rest_piece)
    up_parts = split_positions(out_grad, place)
    qkv_own, rest_own, up_parts = together(qkv_own, jnp.stack(rest_own), up_parts)
    qkv_halves = interleave(qkv_own, [swap(part, "dp", 1) for part in qkv_own])
    rest_own = around_chips(rest_own)
    ups = [up_parts[0]] + [swap(up_parts[u], "mp", u) for u in to_planes]

    def to_slots(bias):
        return reorder(reorder(bias, plane, 0), spot, 1)

    bias = to_slots(small_params[:FF].reshape(planes, spots, hid))
    bias = bias.reshape(planes, chips, 2, hid).transpose(2, 1, 0, 3)
    bias = bias.reshape(2, chips, 1, planes * hid)
    bout = small_params[FF : FF + D].reshape(1, D)
    alphas = small_params[FF + D :]

    inputs = pick(layer_in, plane)
    documents = pick(doc_ids, plane)
    last = (
        jnp.sum(documents[None, :] <= documents[:, None], axis=1, dtype=jnp.int32)[None, :] - 1
    )
    start = jnp.sum(documents[None, :] < documents[:, None], axis=1, dtype=jnp.int32)[None, :]

    qkv, heads = attention(place, last, inputs, qkv_halves)
    heads, rest_own, ups = together(heads, rest_own, ups)
    rest_halves = interleave(rest_own, [swap(part, "dp", 1) for part in rest_own])
    att_old, ffn_old = pieces(
        buffer_pieces_kernel,
        place,
        buffers_old,
        [like((4, span, D), f32), like((2, hid, D), f32)],
        "buffer_pieces",
    )
    rest_halves, att_old, ffn_old = together(rest_halves, att_old, ffn_old)
    lays, rest = feed_forward(place, alphas, inputs, heads, ups, rest_halves, bias, bout)
    ffn_grad, grad_output, heads_grad, middle_grad, gb_in, gb_out, g_alpha = rest

    ffn_grad = ffn_grad.reshape(2, chips * 2 * planes * hid, D)
    ffn_got = swap(ffn_grad[1], "dp", 1)
    lay_got = [lays[0]] + [swap(lays[u], "mp", u) for u in to_planes]
    gb_in = gb_in.reshape(2, chips, planes, hid).transpose(2, 1, 0, 3).reshape(planes, spots, hid)
    small = jnp.concatenate(
        [to_slots(gb_in).reshape(-1), gb_out.reshape(-1), jnp.sum(g_alpha, axis=1)]
    )
    small = jnp.pad(small, (0, 8 * D - small.size)).reshape(8, D)
    high = lax.reduce_precision(small, 8, 7)
    pair = jnp.concatenate([high, lax.reduce_precision(small - high, 8, 7)]).astype(bf16)
    pair = swap(pair, "dp", 1).astype(f32)
    small = small + pair[:8] + pair[8:]
    pairs = planes // 2
    so_far, keep_one, give_one = attention_back(
        place, start, inputs, qkv_halves, qkv, heads_grad, grad_output, middle_grad, 0, pairs, False
    )
    so_far, ffn_got, small = together(so_far, ffn_got, small)
    parts = run(
        ffn_core_kernel,
        place,
        [ffn_grad[0], ffn_got, small],
        [like((2 * planes * hid + 16, D), bf16)] * chips,
        "ffn_core_sum",
    )
    so_far, parts = together(so_far, parts)
    got = [parts[0]] + [swap(parts[m], "dp", 2 * m) for m in to_chips]
    ins, keep_two, give_two = attention_back(
        place,
        start,
        inputs,
        qkv_halves,
        qkv,
        heads_grad,
        grad_output,
        so_far[0],
        pairs,
        planes - pairs,
        True,
    )
    ins, keep_two, give_two, got, lay_got = together(ins, keep_two, give_two, got, lay_got)

    att_keep = jnp.concatenate([keep_one, keep_two], 1)
    att_give = jnp.concatenate([give_one, give_two], 1)
    att_rows = chips * planes * 4 * span
    att_got = swap(att_give.reshape(att_rows, D), "dp", 1)
    parts = run(
        functools.partial(ffn_chip_kernel, chips, hid),
        place,
        got,
        [like((2 * hid + 16, D), bf16)] * planes,
        "ffn_chip_sum",
    )
    parts, att_got = together(parts, att_got)
    got = [parts[0]] + [swap(parts[k], "mp", k) for k in to_planes]
    att_parts = sum_parts(place, [att_keep.reshape(att_rows, D), att_got], chips, "att_core_sum")
    got, att_parts = together(got, att_parts)
    att_got = [att_parts[0]] + [swap(att_parts[m], "dp", 2 * m) for m in to_chips]
    piece, small_grad = run(
        ffn_plane_kernel,
        place,
        [ffn_old, *got],
        [like((2 * hid, D), bf16), like((8, D), f32)],
        "ffn_plane_sum",
    )
    small_grad = small_grad.reshape(-1)[: FF + D + 2]
    piece, att_got = together(piece, att_got)
    got = around_planes(piece)
    parts = run(
        functools.partial(att_to_owner_kernel, chips, planes),
        place,
        att_got + [att_old],
        [like((planes * span, D), bf16)] * planes,
        "att_chip_sum",
        scratch=[pltpu.VMEM((4, planes * span, D), bf16)],
    )
    got, parts = together(got, parts)
    att_got = [parts[0]] + [swap(parts[u], "mp", u) for u in to_planes]
    got = around_chips(jnp.concatenate(got))
    att_piece = run(
        functools.partial(att_sum_kernel, planes),
        place,
        att_got,
        [like((planes * span, D), bf16)],
        "att_plane_sum",
    )[0]
    att_piece, ins = together(att_piece, ins)
    att_own = around_chips(att_piece)
    in_got = [ins[0]] + [swap(ins[u], "mp", u) for u in to_planes]
    att_halves = interleave(att_own, [swap(part, "dp", 1) for part in att_own])
    att_m = run(
        functools.partial(spread_kernel, spots),
        place,
        att_halves,
        [like((head_cols, D), bf16)] * planes,
        "att_spread",
    )
    att_m, att_halves = together(att_m, att_halves)
    att_m = [att_m[0]] + [swap(att_m[u], "mp", u) for u in to_planes]
    att_x = newton(place, att_halves, planes, False, "newton_att")
    att_x, in_got, att_m = together(att_x, in_got, att_m)
    att_x = [att_x[0]] + [swap(att_x[u], "mp", u) for u in to_planes]
    layer_out = join_positions(lay_got, place)
    in_grad = join_positions(in_got, place)

    outs = run(
        functools.partial(ffn_give_kernel, planes, hid),
        place,
        got,
        [like(((planes + 1) * hid, D), bf16)] * chips + [like((planes * hid, D), bf16)] * chips,
        "ffn_give",
    )
    give, keep = outs[:chips], outs[chips:]
    ffn_got = [swap(part, "dp", 1) for part in give]
    step = newton(place, interleave(keep, ffn_got), planes, True, "newton_ffn")[0]
    step, give, keep, ffn_got = together(step, give, keep, ffn_got)
    step_got = swap(step, "dp", 1)
    new_be, new_bc = run(
        functools.partial(ffn_buffers_kernel, chips, hid),
        place,
        [*give, *keep, *ffn_got],
        [like((hidden_rows, D), f32)] * 2,
        "ffn_buffers",
    )
    att_out = run(
        functools.partial(att_final_kernel, planes),
        place,
        att_m + att_x + list(weights_old[:4]),
        [like(w.shape, f32) for w in weights_old[:4]] * 2,
        "att_final",
        scratch=[pltpu.VMEM((2, planes, head_cols, D), bf16)],
    )
    new_we, new_wc = run(
        ffn_final_kernel,
        place,
        [step, step_got, w_expand, w_contract],
        [like((hidden_rows, D), f32)] * 2,
        "ffn_final",
    )

    first_new = 0.5 * small_first + 0.5 * small_grad
    second_new = 0.5 * small_second + 0.5 * small_grad * small_grad
    correction = 1.0 - 0.5**STEP
    small_new = small_params - adam_rate * (first_new / correction) / (
        jnp.sqrt(second_new / correction) + 1e-08
    )
    return (
        (layer_out, in_grad)
        + tuple(att_out[:4])
        + (new_be, new_bc)
        + tuple(att_out[4:])
        + (new_we, new_wc)
        + (small_new, first_new, second_new)
    )


def solution(mesh):
    in_specs = (
        P("dp", None, None),
        P("dp", None),
        P("dp", "mp", None),
        P(None, "mp"),
        P(None, "mp"),
        P(None, "mp"),
        P("mp", None),
        P("mp", None),
        P("mp", None),
        P(),
        P(None, "mp"),
        P(None, "mp"),
        P(None, "mp"),
        P("mp", None),
        P("mp", None),
        P("mp", None),
        P(),
        P(),
    )
    out_specs = (
        P("dp", "mp", None),
        P("dp", "mp", None),
        P(None, "mp"),
        P(None, "mp"),
        P(None, "mp"),
        P("mp", None),
        P("mp", None),
        P("mp", None),
        P(None, "mp"),
        P(None, "mp"),
        P(None, "mp"),
        P("mp", None),
        P("mp", None),
        P("mp", None),
        P(),
        P(),
        P(),
    )
    block = mesh.shape["mp"] == 4 and mesh.shape["dp"] == 8
    return jax.shard_map(shards if block else general_shards, mesh=mesh, in_specs=in_specs, out_specs=out_specs, check_vma=False)
```

```python
import functools
import math

import jax
import jax.numpy as jnp
from jax import lax
from jax.experimental import pallas as pl
from jax.experimental.pallas import tpu as pltpu
from jax.sharding import PartitionSpec as P

D = 512
HEAD_DIM = 64
FF = 2048
MICRO = 2
STEP = 10


newton_one = 3.4445
newton_two = -4.775
newton_three = 2.0315
muon_rates = (1.0, 1.0, 1.0, 5.0, 2.0, 1.0)
adam_rate = 0.25
mask_fill = -1e30
highest_precision = lax.Precision.HIGHEST


def shortened(x):
    return jax.tree.map(lambda a: a.astype(jnp.bfloat16) if a.dtype == jnp.float32 else a, x)


def gelu_tanh(values):
    return jax.nn.gelu(values, approximate=True)


def block_scores(query_blk, key_part, docs_query, docs_key, first_row):
    scores = jnp.einsum(
        "sqhd,skhd->shqk", query_blk, key_part, preferred_element_type=jnp.float32
    ) * HEAD_DIM ** (-0.5)
    rows_at = first_row + jnp.arange(query_blk.shape[1])
    cols_at = jnp.arange(key_part.shape[1])
    allowed = (rows_at[:, None] >= cols_at[None, :])[None] & (
        docs_query[:, :, None] == docs_key[:, None, :]
    )
    return jnp.where(allowed[:, None], scores, mask_fill)


def attend(query_all, key_all, value_all, documents, span_rows):
    block_outs = []
    log_sums = []
    for block_index in range(query_all.shape[1] // span_rows):
        row_start = block_index * span_rows
        finish = row_start + span_rows
        scores = block_scores(
            query_all[:, row_start:finish],
            key_all[:, :finish],
            documents[:, row_start:finish],
            documents[:, :finish],
            row_start,
        )
        row_peak = jnp.max(scores, axis=-1, keepdims=True)
        exponent = jnp.exp(scores - row_peak)
        row_total = jnp.sum(exponent, axis=-1, keepdims=True)
        prob_low = (exponent / row_total).astype(jnp.bfloat16)
        block_outs.append(
            jnp.einsum(
                "shqk,skhd->sqhd",
                prob_low,
                value_all[:, :finish],
                preferred_element_type=jnp.float32,
            ).astype(jnp.bfloat16)
        )
        log_sums.append(row_peak + jnp.log(row_total))
    return (jnp.concatenate(block_outs, 1), log_sums)


def attend_back(query_all, key_all, value_all, documents, span_rows, log_sums, heads_grad):
    query_grads = []
    key_grad = jnp.zeros(key_all.shape, jnp.float32)
    value_grad = jnp.zeros(value_all.shape, jnp.float32)
    scale = HEAD_DIM ** (-0.5)
    for block_index in range(query_all.shape[1] // span_rows):
        row_start = block_index * span_rows
        finish = row_start + span_rows
        query_blk = query_all[:, row_start:finish]
        scores = block_scores(
            query_blk,
            key_all[:, :finish],
            documents[:, row_start:finish],
            documents[:, :finish],
            row_start,
        )
        probs = jnp.exp(scores - log_sums[block_index])
        prob_low = probs.astype(jnp.bfloat16)
        grad_blk = heads_grad[:, row_start:finish]
        grad_probs = jnp.einsum(
            "sqhd,skhd->shqk", grad_blk, value_all[:, :finish], preferred_element_type=jnp.float32
        )
        row_delta = jnp.sum(probs * grad_probs, axis=-1, keepdims=True)
        grad_scores = (probs * (grad_probs - row_delta)).astype(jnp.bfloat16)
        query_grads.append(
            jnp.einsum(
                "shqk,skhd->sqhd",
                grad_scores,
                key_all[:, :finish],
                preferred_element_type=jnp.float32,
            )
            * scale
        )
        key_grad = key_grad.at[:, :finish].add(
            jnp.einsum(
                "shqk,sqhd->skhd", grad_scores, query_blk, preferred_element_type=jnp.float32
            )
            * scale
        )
        value_grad = value_grad.at[:, :finish].add(
            jnp.einsum("shqk,sqhd->skhd", prob_low, grad_blk, preferred_element_type=jnp.float32)
        )
    return (jnp.concatenate(query_grads, 1), key_grad, value_grad)


def gram_part(iterate, by_columns):
    if by_columns:
        return lax.dot_general(
            iterate,
            iterate,
            (((1,), (1,)), ((), ())),
            precision=highest_precision,
            preferred_element_type=jnp.float32,
        )
    return lax.dot_general(
        iterate,
        iterate,
        (((0,), (0,)), ((), ())),
        precision=highest_precision,
        preferred_element_type=jnp.float32,
    )


def newton_update(iterate, gram_sum, by_columns):
    square = jnp.dot(gram_sum, gram_sum, precision=highest_precision)
    polynomial = newton_two * gram_sum + newton_three * square
    if by_columns:
        applied = jnp.dot(polynomial, iterate, precision=highest_precision)
    else:
        applied = lax.dot_general(
            iterate,
            polynomial,
            (((1,), (1,)), ((), ())),
            precision=highest_precision,
            preferred_element_type=jnp.float32,
        )
    return newton_one * iterate + applied


def general_shards(
    layer_in,
    doc_ids,
    out_grad,
    w_query,
    w_key,
    w_value,
    w_output,
    w_expand,
    w_contract,
    small_params,
    buffer_query,
    buffer_key,
    buffer_value,
    buffer_output,
    buffer_expand,
    buffer_contract,
    small_first,
    small_second,
):
    group_count = lax.axis_size("mp")
    group_index = lax.axis_index("mp")
    seq_count, length, model_width = layer_in.shape
    per_micro = seq_count // MICRO
    token_span = length // group_count
    head_cols = w_query.shape[1]
    heads_here = head_cols // HEAD_DIM
    span_rows = min(512, length)
    expansion_bias = small_params[:FF]
    contraction_bias = small_params[FF : FF + D]
    alpha_attend = small_params[FF + D]
    alpha_ffn = small_params[FF + D + 1]
    query_key_value_weight = jnp.concatenate((w_query, w_key, w_value), 1).astype(jnp.bfloat16)
    row_local = (
        w_output.astype(jnp.bfloat16),
        w_expand.astype(jnp.bfloat16),
        w_contract.astype(jnp.bfloat16),
    )
    grad_qkv_weight = jnp.zeros((model_width, 3 * head_cols), jnp.float32)
    grad_output = jnp.zeros((D, D), jnp.float32)
    grad_expand = jnp.zeros((FF, D), jnp.float32)
    grad_contract = jnp.zeros((FF, D), jnp.float32)
    grad_bias_expand = jnp.zeros((FF,), jnp.float32)
    grad_bias_contract = jnp.zeros((D,), jnp.float32)
    grad_alpha_attend = jnp.zeros((), jnp.float32)
    grad_alpha_ffn = jnp.zeros((), jnp.float32)
    out_blocks = []
    grad_blocks = []
    for micro_index in range(MICRO):
        rows_from = micro_index * per_micro
        layer_inputs = layer_in[rows_from : rows_from + per_micro]
        documents = doc_ids[rows_from : rows_from + per_micro]
        upstream = out_grad[rows_from : rows_from + per_micro]
        query_key_value_rows = jnp.einsum(
            "orv,vx->orx", layer_inputs, query_key_value_weight, preferred_element_type=jnp.float32
        ).astype(jnp.bfloat16)
        qkv_split = query_key_value_rows.reshape(per_micro, length, 3, heads_here, HEAD_DIM)
        query_all = qkv_split[:, :, 0]
        key_all = qkv_split[:, :, 1]
        value_all = qkv_split[:, :, 2]
        head_outputs, log_sums = attend(query_all, key_all, value_all, documents, span_rows)
        heads_flat = head_outputs.reshape(per_micro, length, head_cols)
        heads_tok = lax.all_to_all(heads_flat, "mp", split_axis=1, concat_axis=2, tiled=True)
        row_now = (
            lax.all_gather(row_local[0], "mp", axis=0, tiled=True),
            lax.all_gather(row_local[1], "mp", axis=0, tiled=True),
            lax.all_gather(row_local[2], "mp", axis=0, tiled=True),
        )
        output_full, expand_full, contract_full = row_now
        attention_result = jnp.einsum(
            "std,de->ste", heads_tok, output_full, preferred_element_type=jnp.float32
        )
        local_in = lax.dynamic_slice_in_dim(
            layer_inputs, group_index * token_span, token_span, 1
        ).astype(jnp.float32)
        middle_activation = local_in + alpha_attend * attention_result
        middle_low = middle_activation.astype(jnp.bfloat16)
        preactivation = (
            jnp.einsum("std,fd->stf", middle_low, expand_full, preferred_element_type=jnp.float32)
            + expansion_bias
        )
        hidden_state, gelu_back = jax.vjp(gelu_tanh, preactivation)
        hidden_low = hidden_state.astype(jnp.bfloat16)
        residual_branch = (
            jnp.einsum("stf,fd->std", hidden_low, contract_full, preferred_element_type=jnp.float32)
            + contraction_bias
        )
        out_blocks.append(middle_activation + alpha_ffn * residual_branch)
        grad_alpha_ffn = grad_alpha_ffn + jnp.sum(upstream * residual_branch)
        branch_grad = (alpha_ffn * upstream).astype(jnp.bfloat16)
        grad_bias_contract = grad_bias_contract + jnp.sum(
            branch_grad, axis=(0, 1), dtype=jnp.float32
        )
        grad_contract = grad_contract + jnp.einsum(
            "stf,std->fd", hidden_low, branch_grad, preferred_element_type=jnp.float32
        )
        hidden_grad = jnp.einsum(
            "std,fd->stf", branch_grad, contract_full, preferred_element_type=jnp.float32
        )
        pre_grad = gelu_back(hidden_grad)[0].astype(jnp.bfloat16)
        grad_bias_expand = grad_bias_expand + jnp.sum(pre_grad, axis=(0, 1), dtype=jnp.float32)
        grad_expand = grad_expand + jnp.einsum(
            "stf,std->fd", pre_grad, middle_low, preferred_element_type=jnp.float32
        )
        middle_grad = upstream + jnp.einsum(
            "stf,fd->std", pre_grad, expand_full, preferred_element_type=jnp.float32
        )
        grad_alpha_attend = grad_alpha_attend + jnp.sum(middle_grad * attention_result)
        attend_grad = (alpha_attend * middle_grad).astype(jnp.bfloat16)
        grad_output = grad_output + jnp.einsum(
            "std,ste->de", heads_tok, attend_grad, preferred_element_type=jnp.float32
        )
        heads_grad_tok = jnp.einsum(
            "ste,de->std", attend_grad, output_full, preferred_element_type=jnp.float32
        ).astype(jnp.bfloat16)
        heads_grad = lax.all_to_all(heads_grad_tok, "mp", split_axis=2, concat_axis=1, tiled=True)
        heads_grad = heads_grad.reshape(per_micro, length, heads_here, HEAD_DIM)
        query_grad, key_grad, value_grad = attend_back(
            query_all, key_all, value_all, documents, span_rows, log_sums, heads_grad
        )
        query_key_value_gradient = (
            jnp.stack((query_grad, key_grad, value_grad), 2)
            .reshape(per_micro, length, 3 * head_cols)
            .astype(jnp.bfloat16)
        )
        grad_qkv_weight = grad_qkv_weight + jnp.einsum(
            "tmf,tmp->fp",
            layer_inputs,
            query_key_value_gradient,
            preferred_element_type=jnp.float32,
        )
        partial_grad = jnp.einsum(
            "nrj,yj->nry",
            query_key_value_gradient,
            query_key_value_weight,
            preferred_element_type=jnp.float32,
        )
        head_part = lax.psum_scatter(
            partial_grad.astype(jnp.bfloat16), "mp", scatter_dimension=1, tiled=True
        ).astype(jnp.float32)
        grad_blocks.append(middle_grad + head_part)
    layer_out = jnp.concatenate(out_blocks, 0)
    in_grad = jnp.concatenate(grad_blocks, 0)
    output_part, expand_part, contract_part = (
        lax.psum_scatter(
            grad_output.astype(jnp.bfloat16), "mp", scatter_dimension=0, tiled=True
        ).astype(jnp.float32),
        lax.psum_scatter(
            grad_expand.astype(jnp.bfloat16), "mp", scatter_dimension=0, tiled=True
        ).astype(jnp.float32),
        lax.psum_scatter(
            grad_contract.astype(jnp.bfloat16), "mp", scatter_dimension=0, tiled=True
        ).astype(jnp.float32),
    )
    matrix_grads = (
        lax.psum(grad_qkv_weight[:, :head_cols].astype(jnp.bfloat16), "dp").astype(jnp.float32),
        lax.psum(grad_qkv_weight[:, head_cols : 2 * head_cols].astype(jnp.bfloat16), "dp").astype(
            jnp.float32
        ),
        lax.psum(grad_qkv_weight[:, 2 * head_cols :].astype(jnp.bfloat16), "dp").astype(
            jnp.float32
        ),
        lax.psum(output_part.astype(jnp.bfloat16), "dp").astype(jnp.float32),
        lax.psum(expand_part.astype(jnp.bfloat16), "dp").astype(jnp.float32),
        lax.psum(contract_part.astype(jnp.bfloat16), "dp").astype(jnp.float32),
    )
    small_local = jnp.concatenate(
        (grad_bias_expand, grad_bias_contract, jnp.stack((grad_alpha_attend, grad_alpha_ffn)))
    )
    small_grad = lax.psum(small_local, ("dp", "mp"))
    first_new = 0.5 * small_first + 0.5 * small_grad
    second_new = 0.5 * small_second + 0.5 * small_grad * small_grad
    correction = 1.0 - 0.5**STEP
    small_new = small_params - adam_rate * (first_new / correction) / (
        jnp.sqrt(second_new / correction) + 1e-08
    )
    olds = (buffer_query, buffer_key, buffer_value, buffer_output, buffer_expand, buffer_contract)
    weights_old = (w_query, w_key, w_value, w_output, w_expand, w_contract)
    by_columns = (True, True, True, False, False, False)
    buffers = tuple(
        (0.5 * old_buffer + grad_matrix for old_buffer, grad_matrix in zip(olds, matrix_grads))
    )
    squares = lax.psum(tuple((jnp.sum(matrix * matrix) for matrix in buffers)), "mp")
    iterates = [
        matrix / (jnp.sqrt(square_sum) + 1e-07) for matrix, square_sum in zip(buffers, squares)
    ]
    for newton_step in range(5):
        gram_sums = jax.tree.map(
            lambda part: part.astype(jnp.float32),
            lax.psum(
                shortened(
                    tuple(
                        (
                            gram_part(iterate, column_flag)
                            for iterate, column_flag in zip(iterates, by_columns)
                        )
                    )
                ),
                "mp",
            ),
        )
        iterates = [
            newton_update(iterate, gram_sum, column_flag)
            for iterate, gram_sum, column_flag in zip(iterates, gram_sums, by_columns)
        ]
    new_weights = tuple(
        (
            weight - rate * iterate
            for weight, rate, iterate in zip(weights_old, muon_rates, iterates)
        )
    )
    return (layer_out, in_grad) + buffers + new_weights + (small_new, first_new, second_new)


max_doc = 512
q_rows = 256
f32 = jnp.float32
bf16 = jnp.bfloat16
nt = (((1,), (1,)), ((), ()))
nn = (((1,), (0,)), ((), ()))
tn = (((0,), (0,)), ((), ()))
gelu_root = 0.7978845608028654
gelu_cube = 0.044715


def mm(a, b, dims):
    return lax.dot_general(a, b, dims, preferred_element_type=f32)


def swap(x, axis, mask):
    size = lax.axis_size(axis)
    return lax.ppermute(x, axis, [(a, a ^ mask) for a in range(size)])


def reorder(x, index, axis):
    parts = [
        lax.dynamic_slice_in_dim(x, slot ^ index, 1, axis) for slot in range(x.shape[axis])
    ]
    return jnp.concatenate(parts, axis)


def pick(x, index):
    return lax.dynamic_index_in_dim(x, index, 0, keepdims=False)


def like(shape, dtype):
    return jax.ShapeDtypeStruct(shape, dtype)


whole = pl.BlockSpec(memory_space=pltpu.VMEM)
hbm = pl.BlockSpec(memory_space=pl.ANY)


def run(kernel, place, args, outs, name, grid=(1,), in_specs=None, out_specs=None, scratch=(), flops=0, spare=4):
    moved = sum(a.size * a.dtype.itemsize for a in args)
    moved += sum(o.size * jnp.dtype(o.dtype).itemsize for o in outs)
    held = moved + sum(
        math.prod(b.shape) * b.dtype.itemsize for b in scratch if b.memory_space == pltpu.VMEM
    )
    return pl.pallas_call(
        kernel,
        grid_spec=pltpu.PrefetchScalarGridSpec(
            num_scalar_prefetch=1,
            grid=grid,
            in_specs=in_specs or [whole] * len(args),
            out_specs=out_specs or [whole] * len(outs),
            scratch_shapes=list(scratch),
        ),
        out_shape=list(outs),
        compiler_params=pltpu.CompilerParams(vmem_limit_bytes=min(56 << 20, held + (spare << 20))),
        cost_estimate=pl.CostEstimate(
            flops=flops, bytes_accessed=moved if flops else 0, transcendentals=0
        ),
        name=name,
    )(place, *args)


def weight_pieces_kernel(place, q, k, v, o, e, c, qkv_out, rest_out, turned):
    span = o.shape[0]
    at = pl.multiple_of(place[1] * span, span)
    for which, ref in enumerate((q, k, v)):
        turned[...] = ref[...].T
        qkv_out[which * span : (which + 1) * span, :] = turned[pl.ds(at, span), :].astype(bf16)
    hid = e.shape[0]
    rest_out[:span, :] = o[...].astype(bf16)
    rest_out[span : span + hid, :] = e[...].astype(bf16)
    rest_out[span + hid :, :] = c[...].astype(bf16)


def buffer_pieces_kernel(place, q, k, v, o, e, c, att_out, ffn_out, turned):
    span = o.shape[0]
    at = pl.multiple_of(place[1] * span, span)
    for which, ref in enumerate((q, k, v)):
        turned[...] = ref[...].T
        att_out[which] = 0.5 * turned[pl.ds(at, span), :]
    att_out[3] = 0.5 * o[...]
    ffn_out[0] = 0.5 * c[...]
    ffn_out[1] = 0.5 * e[...]


def pieces(kernel, place, arrays, outs, name):
    q, k, v, o, e, c = arrays
    spots = lax.axis_size("dp")
    span, hid = o.shape[0] // spots, e.shape[0] // spots
    row = lambda size: pl.BlockSpec((size, D), lambda g, place: (place[1], 0))
    return run(
        kernel,
        place,
        arrays,
        outs,
        name,
        in_specs=[whole, whole, whole, row(span), row(hid), row(hid)],
        spare=56,
        scratch=[pltpu.VMEM((q.shape[1], D), f32)],
    )


def split_positions_kernel(place, *refs):
    count = len(refs) // 2
    for u in range(count):
        refs[count + u][...] = refs[u][0].astype(bf16)


def split_positions(x, place):
    planes, span, width = x.shape
    block = lambda u: pl.BlockSpec((1, span, width), lambda g, place: (place[0] ^ u, 0, 0))
    return run(
        split_positions_kernel,
        place,
        [x] * planes,
        [like((span, width), bf16)] * planes,
        "split_positions",
        in_specs=[block(u) for u in range(planes)],
    )


def join_positions_kernel(place, *refs):
    out = refs[-1]
    for u, ref in enumerate(refs[:-1]):
        out[place[0] ^ u] = ref[...].astype(f32)


def join_positions(parts, place):
    span, width = parts[0].shape
    return run(
        join_positions_kernel,
        place,
        parts,
        [like((len(parts), span, width), f32)],
        "join_positions",
    )[0]


def window(first_row):
    return max(0, first_row + 1 - max_doc) // 128 * 128


def pair_weights(halves, which, span):
    return jnp.concatenate([half[0, which * span : (which + 1) * span, :] for half in halves], 0)


def interleave(own, other):
    return [half for pair in zip(own, other) for half in pair]


def in_lanes(low, high, x, rest):
    lane = lax.broadcasted_iota(jnp.int32, x.shape, 1)
    return jnp.where((lane >= low) & (lane < high), x, rest)


def spare_lanes(half, values, like_x):
    lane = lax.broadcasted_iota(jnp.int32, like_x.shape, 1)
    first = HEAD_DIM * (1 - half)
    out = jnp.zeros_like(like_x)
    for at, value in enumerate(values):
        out = jnp.where(lane == first + at, value, out)
    return out


def head_lanes(half, x, values=()):
    return in_lanes(HEAD_DIM * half, HEAD_DIM * (half + 1), x, spare_lanes(half, values, x))


def two_parts(x):
    high = x.astype(bf16)
    return high, (x - high.astype(f32)).astype(bf16)


def forward_kernel(place, last_ref, in_ref, *refs):
    halves, (x_ref, o_ref, bias_ref, q_ref, v_ref) = refs[:-5], refs[-5:]
    length = in_ref.shape[1]
    span = halves[0].shape[1] // 3
    blocks = [(first, window(first), first + q_rows) for first in range(0, length, q_rows)]

    @pl.when(pl.program_id(0) == 0)
    def _():
        for first, low, high in blocks:
            row = first + lax.broadcasted_iota(jnp.int32, (q_rows, high - low), 0)
            col = low + lax.broadcasted_iota(jnp.int32, (q_rows, high - low), 1)
            allowed = (col <= row) & (row <= last_ref[:, low:high])
            bias_ref[first:high, : high - low] = jnp.where(allowed, 0.0, mask_fill)

    weight = jnp.concatenate([pair_weights(halves, which, span) for which in range(3)], 0)
    rows = mm(in_ref[0], weight, nt).astype(bf16)
    query = rows[:, :128] * jnp.asarray(HEAD_DIM**-0.5, bf16)
    x_ref[0, 2] = rows[:, 128:256]
    x_ref[0, 3] = rows[:, 256:]
    one = jnp.asarray(1, bf16)
    for half in range(2):
        q_ref[half] = head_lanes(half, query)
        v_ref[half] = head_lanes(half, rows[:, 256:], (one,))
    for first, low, high in blocks:
        found = []
        for half in range(2):
            spare = HEAD_DIM * (1 - half)
            scores = mm(q_ref[half, first:high, :], x_ref[0, 2, low:high, :], nt)
            scores = scores + bias_ref[first:high, : high - low]
            peak = jnp.max(scores, axis=1, keepdims=True)
            weight = jnp.exp(scores - peak).astype(bf16)
            out = mm(weight, v_ref[half, low:high, :], nn)
            total = out[:, spare : spare + 1]
            found.append(out * (1.0 / total))
            parts = two_parts(-(peak + jnp.log(total)))
            x_ref[0, half, first:high, :] = head_lanes(half, q_ref[half, first:high, :], parts)
        o_ref[first:high, :] = in_lanes(0, HEAD_DIM, found[0], found[1]).astype(bf16)


def attention(place, last, inputs, halves):
    length = inputs.shape[1]
    planes, rows, _ = halves[0].shape
    half = pl.BlockSpec((1, rows, D), lambda h, place: (h, 0, 0))
    return run(
        forward_kernel,
        place,
        [last, inputs, *halves],
        [like((planes, 4, length, 128), bf16), like((length, D), bf16)],
        "attention_forward",
        spare=56,
        grid=(planes,),
        in_specs=[whole, pl.BlockSpec((1, length, D), lambda h, place: (place[0], 0, 0))]
        + [half] * len(halves),
        out_specs=[
            pl.BlockSpec((1, 4, length, 128), lambda h, place: (h, 0, 0, 0)),
            pl.BlockSpec((length, 128), lambda h, place: (0, h)),
        ],
        scratch=[
            pltpu.VMEM((length, 768), f32),
            pltpu.VMEM((2, length, 128), bf16),
            pltpu.VMEM((2, length, 128), bf16),
        ],
        flops=8 * length * D * D + 2 * length * 768 * 512 * planes,
    )


def backward_kernel(
    is_last, spots, place, start_ref, in_hbm, x_ref, g_ref, o_ref, gout_ref, gmid_hbm, *rest
):
    halves, rest = rest[:spots], rest[spots:]
    ins, rest = rest[:-12], rest[-12:]
    keep_ref, give_ref, dk_ref, dv_ref, dq_ref, acc_ref, bias_ref, k_ref, v_ref, gs_ref = rest[:10]
    in_ref, sems = rest[10:]
    length = in_ref.shape[0]
    load_acc = pltpu.make_async_copy(gmid_hbm, acc_ref, sems.at[0])
    load_in = pltpu.make_async_copy(in_hbm.at[place[0]], in_ref, sems.at[1])
    span = halves[0].shape[1] // 3
    chips = spots // 2
    step = pl.program_id(0)
    blocks = [(first, window(first), first + q_rows) for first in range(0, length, q_rows)]

    @pl.when(step == 0)
    def _():
        load_acc.start()
        load_in.start()
        for first, low, high in blocks:
            col = low + lax.broadcasted_iota(jnp.int32, (high - low, q_rows), 0)
            row = first + lax.broadcasted_iota(jnp.int32, (high - low, q_rows), 1)
            allowed = (col <= row) & (col >= start_ref[:, first:high])
            bias_ref[: high - low, first:high] = jnp.where(allowed, 0.0, mask_fill)

    dk_ref[...] = jnp.zeros_like(dk_ref)
    dv_ref[...] = jnp.zeros_like(dv_ref)
    one = jnp.asarray(1, bf16)
    product = g_ref[...].astype(f32) * o_ref[...].astype(f32)
    for half in range(2):
        k_ref[half] = head_lanes(half, x_ref[0, 2], (one, one))
        v_ref[half] = head_lanes(half, x_ref[0, 3], (one, one))
        delta = jnp.sum(head_lanes(half, product), axis=1, keepdims=True)
        gs_ref[half] = head_lanes(half, g_ref[...], two_parts(-delta))
    for first, low, high in blocks:
        q_both = jnp.concatenate([head_lanes(half, x_ref[0, half, first:high, :]) for half in range(2)], 0)
        g_both = jnp.concatenate([head_lanes(half, g_ref[first:high, :]) for half in range(2)], 0)
        dq = jnp.zeros((q_rows, 128), f32)
        for at in range(low, high, q_rows):
            keys = slice(at, at + q_rows)
            bias = bias_ref[at - low : at - low + q_rows, first:high]
            probs, g_scores = [], []
            for half in range(2):
                scores = mm(k_ref[half, keys, :], x_ref[0, half, first:high, :], nt) + bias
                weight = jnp.exp(scores)
                g_probs = mm(v_ref[half, keys, :], gs_ref[half, first:high, :], nt)
                probs.append(weight.astype(bf16))
                g_scores.append((weight * g_probs).astype(bf16))
            k_both = jnp.concatenate([head_lanes(half, x_ref[0, 2, keys, :]) for half in range(2)], 0)
            dq = dq + mm(jnp.concatenate(g_scores, 0), k_both, tn)
            dv_ref[keys, :] += mm(jnp.concatenate(probs, 1), g_both, nn)
            dk_ref[keys, :] += mm(jnp.concatenate(g_scores, 1), q_both, nn)
        dq_ref[first:high, :] = (dq * HEAD_DIM**-0.5).astype(bf16)
    grads = (dq_ref[...], dk_ref[...].astype(bf16), dv_ref[...].astype(bf16))
    grads = jnp.concatenate(grads, 1)
    weight = jnp.concatenate([pair_weights(halves, which, span) for which in range(3)], 0)

    @pl.when(step == 0)
    def _():
        load_acc.wait()
        load_in.wait()

    acc_ref[...] += mm(grads, weight, nn)
    all_rows = mm(grads, in_ref[...], tn).astype(bf16)
    for which in range(4):
        if which < 3:
            rows = all_rows[which * 128 : (which + 1) * 128, :]
        else:
            rows = gout_ref[...]
        for m in range(chips):
            for c, ref in enumerate((keep_ref, give_ref)):
                at = (2 * m + c) * span
                ref[m, 0, which * span : (which + 1) * span, :] = rows[at : at + span, :]

    @pl.when(step == pl.num_programs(0) - 1)
    def _():
        if not is_last:
            save = pltpu.make_async_copy(acc_ref, ins[0], sems.at[0])
            save.start()
            save.wait()
            return
        rows = ins[0].shape[0]
        for u, ref in enumerate(ins):
            at = pl.multiple_of((place[0] ^ u) * rows, rows)
            ref[...] = acc_ref[pl.ds(at, rows), :].astype(bf16)


def attention_back(
    place, start, inputs, halves, qkv, heads_grad, heads, grad_output, so_far, first, count, is_last
):
    length = inputs.shape[1]
    planes, rows, _ = halves[0].shape
    spots = len(halves)
    chips = spots // 2
    span = rows // 3
    half = pl.BlockSpec((1, rows, D), lambda h, place: (first + h, 0, 0))
    out_half = pl.BlockSpec((chips, 1, 4 * span, D), lambda h, place: (0, h, 0, 0))
    outs = [like((length // planes, D), bf16)] * planes if is_last else [like((length, D), f32)]
    out = run(
        functools.partial(backward_kernel, is_last, spots),
        place,
        [start, inputs, qkv, heads_grad, heads, grad_output, so_far, *halves],
        outs + [like((chips, count, 4 * span, D), bf16)] * 2,
        "attention_backward",
        spare=56,
        grid=(count,),
        in_specs=[
            whole,
            hbm,
            pl.BlockSpec((1, 4, length, 128), lambda h, place: (first + h, 0, 0, 0)),
            pl.BlockSpec((length, 128), lambda h, place: (0, first + h)),
            pl.BlockSpec((length, 128), lambda h, place: (0, first + h)),
            pl.BlockSpec((128, D), lambda h, place: (first + h, 0)),
            hbm,
        ]
        + [half] * spots,
        out_specs=([whole] * planes if is_last else [hbm]) + [out_half] * 2,
        scratch=[
            pltpu.VMEM((length, 128), f32),
            pltpu.VMEM((length, 128), f32),
            pltpu.VMEM((length, 128), bf16),
            pltpu.VMEM((length, D), f32),
            pltpu.VMEM((768, length), f32),
            pltpu.VMEM((2, length, 128), bf16),
            pltpu.VMEM((2, length, 128), bf16),
            pltpu.VMEM((2, length, 128), bf16),
            pltpu.VMEM((length, D), bf16),
            pltpu.SemaphoreType.DMA((2,)),
        ],
        flops=(12 * length * D * D + 5 * length * 768 * 512 * planes) * count // planes,
    )
    return out[:-2], out[-2], out[-1]


def ffn_kernel(planes, spots, per, place, *refs):
    alphas, in_hbm, heads_hbm = refs[:3]
    ups = refs[3 : 3 + planes]
    halves = refs[3 + planes : 3 + planes + spots]
    bias_ref, bout_ref = refs[3 + planes + spots : 5 + planes + spots]
    outs = refs[5 + planes + spots :]
    lays = outs[:planes]
    keep_ref, give_ref, gout_ref, gheads_hbm, gmid_hbm, gbin_ref, gbout_ref, galpha_ref = outs[
        planes : planes + 8
    ]
    (
        attended, middle, mid_low, g_low, up, branch, o_low, lay, weights, in_ref, heads_ref,
        o_parts, gmid_ref, gheads_ref, sems, w_sems, out_sems,
    ) = outs[planes + 8 :]
    chips = spots // 2
    length = in_ref.shape[0]
    block = length // planes
    hid = keep_ref.shape[2] // planes
    span = halves[0].shape[1] - 2 * hid
    step = pl.program_id(0)
    steps = pl.num_programs(0)
    alpha_att, alpha_ffn = alphas[0], alphas[1]
    size = 512
    tiles = [slice(at, at + size) for at in range(0, length, size)]

    def order(at):
        return 2 * (at % chips) + at // chips

    def weight_copy(at):
        return pltpu.make_async_copy(
            halves[order(at)].at[:, span:, :], weights.at[at], w_sems.at[at]
        )

    @pl.when(step == 0)
    def _():
        first = [
            pltpu.make_async_copy(half.at[:, :span, :], o_parts.at[at], sems.at[at])
            for at, half in enumerate(halves)
        ]
        first.append(pltpu.make_async_copy(heads_hbm, heads_ref, sems.at[spots]))
        first.append(pltpu.make_async_copy(in_hbm.at[place[0]], in_ref, sems.at[spots + 1]))
        for u in range(planes):
            at = pl.multiple_of((place[0] ^ u) * block, block)
            first.append(
                pltpu.make_async_copy(ups[u], up.at[pl.ds(at, block), :], sems.at[spots + 2 + u])
            )
        for copy in first:
            copy.start()
        for at in range(spots):
            weight_copy(at).start()
        for copy in first:
            copy.wait()
        for k in range(planes):
            for at in range(spots):
                row = (k * spots + at) * span
                o_low[row : row + span, :] = o_parts[at, k]
        total = jnp.zeros((1, D), f32)
        for t in tiles:
            found = mm(heads_ref[t, :], o_low[...], nn)
            attended[t, :] = found
            mid = in_ref[t, :].astype(f32) + alpha_att * found
            middle[t, :] = mid
            mid_low[t, :] = mid.astype(bf16)
            upstream = up[t, :].astype(f32)
            grad = (alpha_ffn * upstream).astype(bf16)
            g_low[t, :] = grad
            total = total + jnp.sum(grad.astype(f32), axis=0, keepdims=True)
            branch[t, :] = jnp.zeros((size, D), f32)
            gmid_ref[t, :] = upstream
        gbout_ref[...] = total

    for at in range(spots):

        @pl.when(step == at // per)
        def _():
            weight_copy(at).wait()

    rows = [weights[step * per + g] for g in range(per)]
    expand = jnp.concatenate([row[:, :hid, :].reshape(planes * hid, D) for row in rows], 0)
    contract = jnp.concatenate([row[:, hid:, :].reshape(planes * hid, D) for row in rows], 0)
    bias = bias_ref[0]
    gc = jnp.zeros((per * planes * hid, D), f32)
    ge = jnp.zeros((per * planes * hid, D), f32)
    gb = jnp.zeros((1, per * planes * hid), f32)
    for t in tiles:
        mid = mid_low[t, :]
        grad = g_low[t, :]
        pre = mm(mid, expand, nt) + bias
        square = pre * pre
        tanh = jnp.tanh(gelu_root * pre * (1.0 + gelu_cube * square))
        half = 0.5 * (1.0 + tanh)
        hidden = (pre * half).astype(bf16)
        slope = half + (0.5 * gelu_root) * pre * (1.0 - tanh * tanh) * (
            1.0 + (3.0 * gelu_cube) * square
        )
        branch[t, :] += mm(hidden, contract, nn)
        g_pre = (mm(grad, contract, nt) * slope).astype(bf16)
        gmid_ref[t, :] += mm(g_pre, expand, nn)
        gc = gc + mm(hidden, grad, tn)
        ge = ge + mm(g_pre, mid, tn)
        gb = gb + jnp.sum(g_pre.astype(f32), axis=0, keepdims=True)
    gc = gc.astype(bf16)
    ge = ge.astype(bf16)
    group = planes * hid

    def store(ref):
        for g in range(per):
            ref[g, 0] = gc[g * group : (g + 1) * group, :]
            ref[g, 1] = ge[g * group : (g + 1) * group, :]

    pl.when(step < steps // 2)(lambda: store(keep_ref))
    pl.when(step >= steps // 2)(lambda: store(give_ref))
    gbin_ref[0] = gb

    @pl.when(step == steps - 1)
    def _():
        sum_ffn = jnp.zeros((1, D), f32)
        sum_att = jnp.zeros((1, D), f32)
        gout = jnp.zeros((D, D), f32)
        copies = []
        for at, t in enumerate(tiles):
            gm = gmid_ref[t, :]
            copies.append(
                pltpu.make_async_copy(gmid_ref.at[t, :], gmid_hbm.at[t, :], out_sems.at[0, at])
            )
            copies[-1].start()
            g_att = (alpha_att * gm).astype(bf16)
            gheads_ref[t, :] = mm(g_att, o_low[...], nt).astype(bf16)
            copies.append(
                pltpu.make_async_copy(gheads_ref.at[t, :], gheads_hbm.at[t, :], out_sems.at[1, at])
            )
            copies[-1].start()
            gout = gout + mm(heads_ref[t, :], g_att, tn)
            sum_att = sum_att + jnp.sum(gm * attended[t, :], axis=0, keepdims=True)
            final = branch[t, :] + bout_ref[...]
            lay[t, :] = middle[t, :] + alpha_ffn * final
            sum_ffn = sum_ffn + jnp.sum(up[t, :].astype(f32) * final, axis=0, keepdims=True)
        gout_ref[...] = gout.astype(bf16)
        galpha_ref[0:1, :] = sum_att
        galpha_ref[1:2, :] = sum_ffn
        for u, ref in enumerate(lays):
            at = pl.multiple_of((place[0] ^ u) * block, block)
            ref[...] = lay[pl.ds(at, block), :].astype(bf16)
        for copy in copies:
            copy.wait()


def feed_forward(place, alphas, inputs, heads, ups, halves, bias, bout):
    length = inputs.shape[1]
    planes = len(ups)
    spots = len(halves)
    chips = spots // 2
    span, hid = heads.shape[1] // (planes * spots), bias.shape[-1] // planes
    per = 2 if chips % 2 == 0 else 1
    steps = spots // per
    bias = bias.reshape(steps, 1, per * planes * hid)
    tiles = length // 512
    group = planes * hid
    out = run(
        functools.partial(ffn_kernel, planes, spots, per),
        place,
        [alphas, inputs, heads, *ups, *halves, bias, bout],
        [like((length // planes, D), bf16)] * planes
        + [
            like((chips, 2, group, D), bf16),
            like((chips, 2, group, D), bf16),
            like((D, D), bf16),
            like((length, D), bf16),
            like((length, D), f32),
            like((steps, 1, per * group), f32),
            like((1, D), f32),
            like((2, D), f32),
        ],
        "feed_forward",
        spare=56,
        grid=(steps,),
        in_specs=[pl.BlockSpec(memory_space=pltpu.SMEM)]
        + [hbm] * (2 + planes + spots)
        + [pl.BlockSpec((1, 1, per * group), lambda t, place: (t, 0, 0)), whole],
        out_specs=[whole] * planes
        + [
            pl.BlockSpec(
                (per, 2, group, D), lambda t, place: (jnp.minimum(t, steps // 2 - 1), 0, 0, 0)
            ),
            pl.BlockSpec(
                (per, 2, group, D), lambda t, place: (jnp.maximum(t - steps // 2, 0), 0, 0, 0)
            ),
            whole,
            hbm,
            hbm,
            pl.BlockSpec((1, 1, per * group), lambda t, place: (t, 0, 0)),
            whole,
            whole,
        ],
        scratch=[
            pltpu.VMEM((length, D), f32),
            pltpu.VMEM((length, D), f32),
            pltpu.VMEM((length, D), bf16),
            pltpu.VMEM((length, D), bf16),
            pltpu.VMEM((length, D), bf16),
            pltpu.VMEM((length, D), f32),
            pltpu.VMEM((D, D), bf16),
            pltpu.VMEM((length, D), f32),
            pltpu.VMEM((spots, planes, 2 * hid, D), bf16),
            pltpu.VMEM((length, D), bf16),
            pltpu.VMEM((length, D), bf16),
            pltpu.VMEM((spots, planes, span, D), bf16),
            pltpu.VMEM((length, D), f32),
            pltpu.VMEM((length, D), bf16),
            pltpu.SemaphoreType.DMA((spots + 2 + planes,)),
            pltpu.SemaphoreType.DMA((spots,)),
            pltpu.SemaphoreType.DMA((2, tiles)),
        ],
        flops=12 * length * D * 2 * chips * group,
    )
    return out[:planes], out[planes:]


def att_core_kernel(place, keep, got, *outs):
    rows = keep.shape[2]
    for m, out in enumerate(outs):
        for k in range(keep.shape[1]):
            total = keep[m, k].astype(f32) + got[m, k].astype(f32)
            out[k * rows : (k + 1) * rows, :] = total.astype(bf16)


def small_write(out, total):
    at = out.shape[0] - 2 * total.shape[0]
    high = total.astype(bf16)
    out[at : at + total.shape[0], :] = high
    out[at + total.shape[0] :, :] = (total - high.astype(f32)).astype(bf16)


def small_read(ref):
    rows = ref.shape[0]
    return ref[rows - 16 : rows - 8, :].astype(f32) + ref[rows - 8 :, :].astype(f32)


def ffn_core_kernel(place, own, got, small, *outs):
    rows = own.shape[0] // len(outs)
    total = small[...]
    for at, out in enumerate(outs):
        for r in range(0, rows, 256):
            a = own[at * rows + r : at * rows + r + 256, :].astype(f32)
            b = got[at * rows + r : at * rows + r + 256, :].astype(f32)
            out[r : r + 256, :] = (a + b).astype(bf16)
        small_write(out, total)


def ffn_chip_kernel(count, hid, place, *refs):
    ins, outs = refs[:count], refs[count:]
    small = small_read(ins[0])
    for ref in ins[1:]:
        small = small + small_read(ref)
    for k, out in enumerate(outs):
        for which in range(2):
            at = (which * len(outs) + k) * hid
            total = ins[0][at : at + hid, :].astype(f32)
            for ref in ins[1:]:
                total = total + ref[at : at + hid, :].astype(f32)
            out[which * hid : (which + 1) * hid, :] = total.astype(bf16)
        small_write(out, small)


def plane_messages_kernel(chips, planes, place, *refs):
    ffn, refs = refs[:planes], refs[planes:]
    att, (ffn_old, att_old), refs = refs[:chips], refs[chips : chips + 2], refs[chips + 2 :]
    outs, small_out, scratch = refs[:planes], refs[planes], refs[planes + 1]
    rows = 2 * ffn_old.shape[1]
    span = att_old.shape[1]
    small = small_read(ffn[0])
    total = ffn_old[...].reshape(rows, D) + ffn[0][:rows, :].astype(f32)
    for ref in ffn[1:]:
        small = small + small_read(ref)
        total = total + ref[:rows, :].astype(f32)
    small_out[...] = small
    total = total.astype(bf16)
    for k in range(planes):
        for which in range(4):
            at = (k * 4 + which) * span
            one = att[0][at : at + span, :].astype(f32)
            for ref in att[1:]:
                one = one + ref[at : at + span, :].astype(f32)
            if k == 0:
                one = one + att_old[which]
            scratch[which, k * span : (k + 1) * span, :] = one.astype(bf16)
    for u, out in enumerate(outs):
        out[:rows, :] = total
        out[rows:, :] = scratch[place[0] ^ u]


def plane_split_kernel(rows, place, *refs):
    ins, out = refs[:-1], refs[-1]
    planes = len(ins)
    span = (ins[0].shape[0] - rows) // planes
    for u, ref in enumerate(ins):
        out[u * rows : (u + 1) * rows, :] = ref[:rows, :]
    for k in range(planes):
        total = jnp.zeros((span, D), f32)
        for u, ref in enumerate(ins):
            at = rows + (k ^ u) * span
            total = total + ref[at : at + span, :].astype(f32)
        at = planes * rows + k * span
        out[at : at + span, :] = total.astype(bf16)


def newton_kernel(planes, spots, first_only, place, *refs):
    x_ref, low_ref = refs[-2:]
    dim, cols = x_ref.shape
    span = cols // (planes * spots)
    group = spots * span
    if first_only:
        chips = spots // 2
        got, outs = refs[chips], refs[chips + 1 : -2]
        tall = (planes + 1) * span
        halves = []
        for m in range(chips):
            halves += [refs[m], got.at[m * tall : m * tall + planes * span, :]]
    else:
        outs = refs[2:-2]
        halves = []
        for at in range(spots):
            from_at = refs[0].shape[0] - (spots // 2 - at // 2) * planes * span
            halves.append(refs[at % 2].at[from_at : from_at + planes * span, :])
    chunk = 512
    total = jnp.zeros((1, D), f32)
    for half in halves:
        part = half[...].astype(f32)
        total = total + jnp.sum(part * part, axis=0, keepdims=True)
    inverse = 1.0 / (jnp.sqrt(jnp.sum(total, axis=1, keepdims=True)) + 1e-07)
    for k in range(planes):
        rows = [half[k * span : (k + 1) * span, :] for half in halves]
        part = jnp.concatenate(rows, 0).astype(f32).T * inverse
        x_ref[:, k * group : (k + 1) * group] = part
        low_ref[:, k * group : (k + 1) * group] = part.astype(bf16)
    diagonal = lax.broadcasted_iota(jnp.int32, (dim, dim), 0) == lax.broadcasted_iota(
        jnp.int32, (dim, dim), 1
    )

    def step(limit):
        gram = jnp.zeros((dim, dim), f32)
        for at in range(0, cols, chunk):
            part = low_ref[:, at : at + chunk]
            gram = gram + mm(part, part, nt)
        trace = jnp.sum(
            jnp.sum(jnp.where(diagonal, gram, 0.0), axis=0, keepdims=True), axis=1, keepdims=True
        )
        shift = trace * (1.0 / dim)
        rest = jnp.where(diagonal, gram - shift, gram)
        rest_low = rest.astype(bf16)
        poly = (newton_two + 2.0 * newton_three * shift) * rest + newton_three * mm(
            rest_low, rest_low, nn
        )
        poly = poly.astype(bf16)
        scale = newton_one + newton_two * shift + newton_three * shift * shift
        for at in range(0, limit, chunk):
            part = scale * x_ref[:, at : at + chunk] + mm(poly, low_ref[:, at : at + chunk], nn)
            x_ref[:, at : at + chunk] = part
            low_ref[:, at : at + chunk] = part.astype(bf16)

    @pl.loop(0, 4)
    def _(_):
        step(cols)

    step(group if first_only else cols)
    for k, out in enumerate(outs):
        part = x_ref[:, k * group : (k + 1) * group].T.astype(bf16)
        if first_only:
            for at in range(spots):
                to = pl.multiple_of((place[1] ^ at) * span, span)
                out[pl.ds(to, span), :] = part[at * span : (at + 1) * span, :]
            continue
        for at in range(0, spots, 2):
            to = pl.multiple_of((place[1] // 2 ^ at // 2) * span, span)
            out[pl.ds(to, span), :] = halves[at][k * span : (k + 1) * span, :]
            to = pl.multiple_of((place[1] // 2 ^ at // 2) * span + group // 2, span)
            out[pl.ds(to, span), :] = part[at * span : (at + 1) * span, :]


def newton(place, halves, planes, spots, cols, first_only, name):
    return run(
        functools.partial(newton_kernel, planes, spots, first_only),
        place,
        halves,
        [like((cols // planes, D), bf16)] * (1 if first_only else planes),
        name,
        scratch=[pltpu.VMEM((D, cols), f32), pltpu.VMEM((D, cols), bf16)],
        flops=10 * D * D * (2 * cols + D),
    )


def att_final_kernel(planes, span, place, mine, got, *refs):
    old, outs, rows = refs[:4], refs[4:-1], refs[-1]
    half = mine.shape[1] // 2
    core = place[1] % 2
    for which in range(4):
        slot = place[0] ^ which
        for kind in range(2):
            for at in range(0, half, span):
                from_at = kind * half + at
                rows[pl.ds(pl.multiple_of(2 * at + core * span, span), span), :] = mine[
                    slot, from_at : from_at + span, :
                ]
                rows[pl.ds(pl.multiple_of(2 * at + (1 - core) * span, span), span), :] = got[
                    slot, from_at : from_at + span, :
                ]
            part = rows[...].astype(f32)
            part = part.T if which < 3 else part
            if kind == 0:
                outs[which][...] = part
            else:
                outs[4 + which][...] = old[which][...] - muon_rates[which] * part


def ffn_give_kernel(planes, hid, span, place, *refs):
    count = len(refs) // 2
    ins, give, keep = refs[:count], refs[count], refs[count + 1 :]
    tall = (planes + 1) * hid
    wide = planes * span

    for m in range(count):
        at, to = 2 * planes * hid, count * tall + m * wide
        give[to : to + wide, :] = ins[m][at : at + wide, :]

    def fill(given):
        for m in range(count):
            for k in range(planes):
                to = slice(m * tall + k * hid, m * tall + (k + 1) * hid)
                at = (2 * k + given) * hid
                give[to, :] = ins[m][at : at + hid, :]
                to = slice(k * hid, (k + 1) * hid)
                at = (2 * k + 1 - given) * hid
                keep[m][to, :] = ins[m][at : at + hid, :]
            give[m * tall + planes * hid : (m + 1) * tall, :] = keep[m][:hid, :]

    @pl.when(place[1] % 2 == 0)
    def _():
        fill(0)

    @pl.when(place[1] % 2 == 1)
    def _():
        fill(1)


def ffn_buffers_kernel(chips, hid, place, give, got, *refs):
    keep, (eo, co) = refs[:chips], refs[chips:]
    tall = keep[0].shape[0] + hid
    tail = tall - hid

    def fill(kept, given):
        for m in range(chips):
            one = pl.multiple_of((place[1] ^ (2 * m)) * hid, hid)
            two = pl.multiple_of((place[1] ^ (2 * m + 1)) * hid, hid)
            at = m * tall
            kept[pl.ds(one, hid), :] = keep[m][:hid, :].astype(f32)
            kept[pl.ds(two, hid), :] = got[at : at + hid, :].astype(f32)
            given[pl.ds(one, hid), :] = give[at : at + hid, :].astype(f32)
            given[pl.ds(two, hid), :] = got[at + tail : at + tall, :].astype(f32)

    @pl.when(place[1] % 2 == 0)
    def _():
        fill(eo, co)

    @pl.when(place[1] % 2 == 1)
    def _():
        fill(co, eo)


def ffn_final_kernel(place, mine, got, we, wc, eo, co):
    def fill(e, c):
        eo[...] = we[...] - muon_rates[4] * e[...].astype(f32)
        co[...] = wc[...] - muon_rates[5] * c[...].astype(f32)

    @pl.when(place[1] % 2 == 0)
    def _():
        fill(mine, got)

    @pl.when(place[1] % 2 == 1)
    def _():
        fill(got, mine)


def shards(
    layer_in,
    doc_ids,
    out_grad,
    w_query,
    w_key,
    w_value,
    w_output,
    w_expand,
    w_contract,
    small_params,
    buffer_query,
    buffer_key,
    buffer_value,
    buffer_output,
    buffer_expand,
    buffer_contract,
    small_first,
    small_second,
):
    planes = lax.axis_size("mp")
    spots = lax.axis_size("dp")
    chips = spots // 2
    plane = lax.axis_index("mp")
    spot = lax.axis_index("dp")
    place = jnp.stack([plane, spot]).astype(jnp.int32)
    length = layer_in.shape[1]
    head_cols = w_query.shape[1]
    hidden_rows = w_expand.shape[0]
    span = head_cols // spots
    hid = hidden_rows // spots
    to_planes = range(1, planes)
    to_chips = range(1, chips)
    weights_old = (w_query, w_key, w_value, w_output, w_expand, w_contract)
    buffers_old = (
        buffer_query,
        buffer_key,
        buffer_value,
        buffer_output,
        buffer_expand,
        buffer_contract,
    )

    def around_planes(x):
        return [x] + [swap(x, "mp", k) for k in to_planes]

    def around_chips(x):
        return [x] + [swap(x, "dp", 2 * m) for m in to_chips]

    def together(*groups):
        return lax.optimization_barrier(groups)

    def together(*groups):
        return lax.optimization_barrier(groups)

    qkv_piece, rest_piece = pieces(
        weight_pieces_kernel,
        place,
        weights_old,
        [like((3 * span, D), bf16), like((span + 2 * hid, D), bf16)],
        "weight_pieces",
    )
    inputs = layer_in
    documents = pick(doc_ids, plane)
    last = (
        jnp.sum(documents[None, :] <= documents[:, None], axis=1, dtype=jnp.int32)[None, :] - 1
    )
    start = jnp.sum(documents[None, :] < documents[:, None], axis=1, dtype=jnp.int32)[None, :]

    def to_slots(bias):
        return reorder(reorder(bias, plane, 0), spot, 1)

    bias = to_slots(small_params[:FF].reshape(planes, spots, hid))
    bias = bias.reshape(planes, chips, 2, hid).transpose(2, 1, 0, 3)
    bias = bias.reshape(2, chips, 1, planes * hid)
    bout = small_params[FF : FF + D].reshape(1, D)
    alphas = small_params[FF + D :]
    token_span = length // planes
    ups = split_positions(out_grad, place)

    qkv_own, ups = together(around_planes(qkv_piece), ups)
    qkv_own = around_chips(jnp.stack(qkv_own))
    rest_own = around_planes(rest_piece)
    qkv_own, rest_own, last, start, bias = together(
        qkv_own, rest_own, last, start, bias
    )
    qkv_halves = interleave(qkv_own, [swap(part, "dp", 1) for part in qkv_own])
    rest_own = around_chips(jnp.stack(rest_own))
    ups = [ups[0]] + [swap(ups[u], "mp", u) for u in to_planes]
    qkv, heads = attention(place, last, inputs, qkv_halves)
    heads, rest_own, ups = together(heads, rest_own, ups)
    rest_halves = interleave(rest_own, [swap(part, "dp", 1) for part in rest_own])
    lays, rest = feed_forward(place, alphas, inputs, heads, ups, rest_halves, bias, bout)
    ffn_keep, ffn_give, grad_output, heads_grad, middle_grad, gb_in, gb_out, g_alpha = rest

    ffn_rows = (chips * 2 * planes * hid, D)
    ffn_got = swap(ffn_give.reshape(ffn_rows), "dp", 1)
    gb_in = gb_in.reshape(2, chips, planes, hid).transpose(2, 1, 0, 3).reshape(planes, spots, hid)
    small = jnp.concatenate(
        [to_slots(gb_in).reshape(-1), gb_out.reshape(-1), jnp.sum(g_alpha, axis=1)]
    )
    small = jnp.pad(small, (0, 8 * D - small.size)).reshape(8, D)
    high = lax.reduce_precision(small, 8, 7)
    pair = jnp.concatenate([high, lax.reduce_precision(small - high, 8, 7)]).astype(bf16)
    pair = swap(pair, "dp", 1).astype(f32)
    small = small + pair[:8] + pair[8:]
    parts = run(
        ffn_core_kernel,
        place,
        [ffn_keep.reshape(ffn_rows), ffn_got, small],
        [like((2 * planes * hid + 16, D), bf16)] * chips,
        "ffn_core_sum",
    )
    middle_grad, parts, lays = together(middle_grad, parts, lays)
    got = [parts[0]] + [swap(parts[m], "dp", 2 * m) for m in to_chips]
    lay_far = [swap(lays[u], "mp", u) for u in to_planes[1:]]
    ins, att_keep, att_give = attention_back(
        place, start, inputs, qkv_halves, qkv, heads_grad, heads, grad_output, middle_grad,
        0, planes, True,
    )
    ins, att_keep, att_give, got, lay_far = together(ins, att_keep, att_give, got, lay_far)

    parts = run(
        functools.partial(ffn_chip_kernel, chips, hid),
        place,
        got,
        [like((2 * hid + 16, D), bf16)] * planes,
        "ffn_chip_sum",
    )
    parts, att_give, buffers_old = together(parts, att_give, buffers_old)
    got = [parts[0]] + [swap(parts[k], "mp", k) for k in to_planes]
    att_got = swap(att_give, "dp", 1)
    att_old, ffn_old = pieces(
        buffer_pieces_kernel,
        place,
        buffers_old,
        [like((4, span, D), f32), like((2, hid, D), f32)],
        "buffer_pieces",
    )

    att_parts = run(
        att_core_kernel,
        place,
        [att_keep, att_got],
        [like((planes * 4 * span, D), bf16)] * chips,
        "att_core_sum",
    )
    att_got = [att_parts[0]] + [swap(att_parts[m], "dp", 2 * m) for m in to_chips]
    outs = run(
        functools.partial(plane_messages_kernel, chips, planes),
        place,
        [*got, *att_got, ffn_old, att_old],
        [like((2 * hid + planes * span, D), bf16)] * planes + [like((8, D), f32)],
        "plane_messages",
        scratch=[pltpu.VMEM((4, planes * span, D), bf16)],
    )
    small_grad = outs[-1].reshape(-1)[: FF + D + 2]
    got = [outs[0]] + [swap(outs[k], "mp", k) for k in to_planes]
    message = run(
        functools.partial(plane_split_kernel, 2 * hid),
        place,
        got,
        [like((planes * (2 * hid + span), D), bf16)],
        "plane_split",
    )[0]
    message, ins = together(message, ins)
    got = around_chips(message)
    near = swap(jnp.concatenate([ins[1], lays[1]]), "mp", 1)
    in_far = [swap(ins[u], "mp", u) for u in to_planes[1:]]
    in_grad = join_positions([ins[0], near[:token_span], *in_far], place)
    layer_out = join_positions([lays[0], near[token_span:], *lay_far], place)
    got, in_grad, layer_out = together(got, in_grad, layer_out)
    outs = run(
        functools.partial(ffn_give_kernel, planes, hid, span),
        place,
        got,
        [like((chips * ((planes + 1) * hid + planes * span), D), bf16)]
        + [like((planes * hid, D), bf16)] * chips,
        "ffn_give",
    )
    give, keep = outs[0], outs[1:]
    ffn_got = swap(give, "dp", 1)
    att_x = newton(place, [give, ffn_got], planes, spots, D, False, "newton_att")
    att_x = jnp.stack([att_x[0]] + [swap(att_x[u], "mp", u) for u in to_planes])
    step = newton(
        place, [*keep, ffn_got], planes, spots, planes * hidden_rows, True, "newton_ffn"
    )[0]
    step, give, keep, ffn_got, att_x = together(step, give, keep, ffn_got, att_x)
    step_got = swap(step, "dp", 1)
    att_other = swap(att_x, "dp", 1)
    new_be, new_bc = run(
        functools.partial(ffn_buffers_kernel, chips, hid),
        place,
        [give, ffn_got, *keep],
        [like((hidden_rows, D), f32)] * 2,
        "ffn_buffers",
    )
    att_out = run(
        functools.partial(att_final_kernel, planes, span),
        place,
        [att_x, att_other, *weights_old[:4]],
        [like(w.shape, f32) for w in weights_old[:4]] * 2,
        "att_final",
        scratch=[pltpu.VMEM((head_cols, D), bf16)],
    )
    new_we, new_wc = run(
        ffn_final_kernel,
        place,
        [step, step_got, w_expand, w_contract],
        [like((hidden_rows, D), f32)] * 2,
        "ffn_final",
    )

    first_new = 0.5 * small_first + 0.5 * small_grad
    second_new = 0.5 * small_second + 0.5 * small_grad * small_grad
    correction = 1.0 - 0.5**STEP
    small_new = small_params - adam_rate * (first_new / correction) / (
        jnp.sqrt(second_new / correction) + 1e-08
    )
    return (
        (layer_out, in_grad)
        + tuple(att_out[:4])
        + (new_be, new_bc)
        + tuple(att_out[4:])
        + (new_we, new_wc)
        + (small_new, first_new, second_new)
    )


def solution(mesh):
    in_specs = (
        P("dp", None, None),
        P("dp", None),
        P("dp", "mp", None),
        P(None, "mp"),
        P(None, "mp"),
        P(None, "mp"),
        P("mp", None),
        P("mp", None),
        P("mp", None),
        P(),
        P(None, "mp"),
        P(None, "mp"),
        P(None, "mp"),
        P("mp", None),
        P("mp", None),
        P("mp", None),
        P(),
        P(),
    )
    out_specs = (
        P("dp", "mp", None),
        P("dp", "mp", None),
        P(None, "mp"),
        P(None, "mp"),
        P(None, "mp"),
        P("mp", None),
        P("mp", None),
        P("mp", None),
        P(None, "mp"),
        P(None, "mp"),
        P(None, "mp"),
        P("mp", None),
        P("mp", None),
        P("mp", None),
        P(),
        P(),
        P(),
    )
    block = mesh.shape["mp"] == 4 and mesh.shape["dp"] == 8
    return jax.shard_map(shards if block else general_shards, mesh=mesh, in_specs=in_specs, out_specs=out_specs, check_vma=False)
```

```python
import functools
import math

import jax
import jax.numpy as jnp
from jax import lax
from jax.experimental import pallas as pl
from jax.experimental.pallas import tpu as pltpu
from jax.sharding import PartitionSpec as P

D = 512
HEAD_DIM = 64
FF = 2048
MICRO = 2
STEP = 10


newton_one = 3.4445
newton_two = -4.775
newton_three = 2.0315
muon_rates = (1.0, 1.0, 1.0, 5.0, 2.0, 1.0)
adam_rate = 0.25
mask_fill = -1e30
highest_precision = lax.Precision.HIGHEST


def shortened(x):
    return jax.tree.map(lambda a: a.astype(jnp.bfloat16) if a.dtype == jnp.float32 else a, x)


def gelu_tanh(values):
    return jax.nn.gelu(values, approximate=True)


def block_scores(query_blk, key_part, docs_query, docs_key, first_row):
    scores = jnp.einsum(
        "sqhd,skhd->shqk", query_blk, key_part, preferred_element_type=jnp.float32
    ) * HEAD_DIM ** (-0.5)
    rows_at = first_row + jnp.arange(query_blk.shape[1])
    cols_at = jnp.arange(key_part.shape[1])
    allowed = (rows_at[:, None] >= cols_at[None, :])[None] & (
        docs_query[:, :, None] == docs_key[:, None, :]
    )
    return jnp.where(allowed[:, None], scores, mask_fill)


def attend(query_all, key_all, value_all, documents, span_rows):
    block_outs = []
    log_sums = []
    for block_index in range(query_all.shape[1] // span_rows):
        row_start = block_index * span_rows
        finish = row_start + span_rows
        scores = block_scores(
            query_all[:, row_start:finish],
            key_all[:, :finish],
            documents[:, row_start:finish],
            documents[:, :finish],
            row_start,
        )
        row_peak = jnp.max(scores, axis=-1, keepdims=True)
        exponent = jnp.exp(scores - row_peak)
        row_total = jnp.sum(exponent, axis=-1, keepdims=True)
        prob_low = (exponent / row_total).astype(jnp.bfloat16)
        block_outs.append(
            jnp.einsum(
                "shqk,skhd->sqhd",
                prob_low,
                value_all[:, :finish],
                preferred_element_type=jnp.float32,
            ).astype(jnp.bfloat16)
        )
        log_sums.append(row_peak + jnp.log(row_total))
    return (jnp.concatenate(block_outs, 1), log_sums)


def attend_back(query_all, key_all, value_all, documents, span_rows, log_sums, heads_grad):
    query_grads = []
    key_grad = jnp.zeros(key_all.shape, jnp.float32)
    value_grad = jnp.zeros(value_all.shape, jnp.float32)
    scale = HEAD_DIM ** (-0.5)
    for block_index in range(query_all.shape[1] // span_rows):
        row_start = block_index * span_rows
        finish = row_start + span_rows
        query_blk = query_all[:, row_start:finish]
        scores = block_scores(
            query_blk,
            key_all[:, :finish],
            documents[:, row_start:finish],
            documents[:, :finish],
            row_start,
        )
        probs = jnp.exp(scores - log_sums[block_index])
        prob_low = probs.astype(jnp.bfloat16)
        grad_blk = heads_grad[:, row_start:finish]
        grad_probs = jnp.einsum(
            "sqhd,skhd->shqk", grad_blk, value_all[:, :finish], preferred_element_type=jnp.float32
        )
        row_delta = jnp.sum(probs * grad_probs, axis=-1, keepdims=True)
        grad_scores = (probs * (grad_probs - row_delta)).astype(jnp.bfloat16)
        query_grads.append(
            jnp.einsum(
                "shqk,skhd->sqhd",
                grad_scores,
                key_all[:, :finish],
                preferred_element_type=jnp.float32,
            )
            * scale
        )
        key_grad = key_grad.at[:, :finish].add(
            jnp.einsum(
                "shqk,sqhd->skhd", grad_scores, query_blk, preferred_element_type=jnp.float32
            )
            * scale
        )
        value_grad = value_grad.at[:, :finish].add(
            jnp.einsum("shqk,sqhd->skhd", prob_low, grad_blk, preferred_element_type=jnp.float32)
        )
    return (jnp.concatenate(query_grads, 1), key_grad, value_grad)


def gram_part(iterate, by_columns):
    if by_columns:
        return lax.dot_general(
            iterate,
            iterate,
            (((1,), (1,)), ((), ())),
            precision=highest_precision,
            preferred_element_type=jnp.float32,
        )
    return lax.dot_general(
        iterate,
        iterate,
        (((0,), (0,)), ((), ())),
        precision=highest_precision,
        preferred_element_type=jnp.float32,
    )


def newton_update(iterate, gram_sum, by_columns):
    square = jnp.dot(gram_sum, gram_sum, precision=highest_precision)
    polynomial = newton_two * gram_sum + newton_three * square
    if by_columns:
        applied = jnp.dot(polynomial, iterate, precision=highest_precision)
    else:
        applied = lax.dot_general(
            iterate,
            polynomial,
            (((1,), (1,)), ((), ())),
            precision=highest_precision,
            preferred_element_type=jnp.float32,
        )
    return newton_one * iterate + applied


def general_shards(
    layer_in,
    doc_ids,
    out_grad,
    w_query,
    w_key,
    w_value,
    w_output,
    w_expand,
    w_contract,
    small_params,
    buffer_query,
    buffer_key,
    buffer_value,
    buffer_output,
    buffer_expand,
    buffer_contract,
    small_first,
    small_second,
):
    group_count = lax.axis_size("mp")
    group_index = lax.axis_index("mp")
    seq_count, length, model_width = layer_in.shape
    per_micro = seq_count // MICRO
    token_span = length // group_count
    head_cols = w_query.shape[1]
    heads_here = head_cols // HEAD_DIM
    span_rows = min(512, length)
    expansion_bias = small_params[:FF]
    contraction_bias = small_params[FF : FF + D]
    alpha_attend = small_params[FF + D]
    alpha_ffn = small_params[FF + D + 1]
    query_key_value_weight = jnp.concatenate((w_query, w_key, w_value), 1).astype(jnp.bfloat16)
    row_local = (
        w_output.astype(jnp.bfloat16),
        w_expand.astype(jnp.bfloat16),
        w_contract.astype(jnp.bfloat16),
    )
    grad_qkv_weight = jnp.zeros((model_width, 3 * head_cols), jnp.float32)
    grad_output = jnp.zeros((D, D), jnp.float32)
    grad_expand = jnp.zeros((FF, D), jnp.float32)
    grad_contract = jnp.zeros((FF, D), jnp.float32)
    grad_bias_expand = jnp.zeros((FF,), jnp.float32)
    grad_bias_contract = jnp.zeros((D,), jnp.float32)
    grad_alpha_attend = jnp.zeros((), jnp.float32)
    grad_alpha_ffn = jnp.zeros((), jnp.float32)
    out_blocks = []
    grad_blocks = []
    for micro_index in range(MICRO):
        rows_from = micro_index * per_micro
        layer_inputs = layer_in[rows_from : rows_from + per_micro]
        documents = doc_ids[rows_from : rows_from + per_micro]
        upstream = out_grad[rows_from : rows_from + per_micro]
        query_key_value_rows = jnp.einsum(
            "orv,vx->orx", layer_inputs, query_key_value_weight, preferred_element_type=jnp.float32
        ).astype(jnp.bfloat16)
        qkv_split = query_key_value_rows.reshape(per_micro, length, 3, heads_here, HEAD_DIM)
        query_all = qkv_split[:, :, 0]
        key_all = qkv_split[:, :, 1]
        value_all = qkv_split[:, :, 2]
        head_outputs, log_sums = attend(query_all, key_all, value_all, documents, span_rows)
        heads_flat = head_outputs.reshape(per_micro, length, head_cols)
        heads_tok = lax.all_to_all(heads_flat, "mp", split_axis=1, concat_axis=2, tiled=True)
        row_now = (
            lax.all_gather(row_local[0], "mp", axis=0, tiled=True),
            lax.all_gather(row_local[1], "mp", axis=0, tiled=True),
            lax.all_gather(row_local[2], "mp", axis=0, tiled=True),
        )
        output_full, expand_full, contract_full = row_now
        attention_result = jnp.einsum(
            "std,de->ste", heads_tok, output_full, preferred_element_type=jnp.float32
        )
        local_in = lax.dynamic_slice_in_dim(
            layer_inputs, group_index * token_span, token_span, 1
        ).astype(jnp.float32)
        middle_activation = local_in + alpha_attend * attention_result
        middle_low = middle_activation.astype(jnp.bfloat16)
        preactivation = (
            jnp.einsum("std,fd->stf", middle_low, expand_full, preferred_element_type=jnp.float32)
            + expansion_bias
        )
        hidden_state, gelu_back = jax.vjp(gelu_tanh, preactivation)
        hidden_low = hidden_state.astype(jnp.bfloat16)
        residual_branch = (
            jnp.einsum("stf,fd->std", hidden_low, contract_full, preferred_element_type=jnp.float32)
            + contraction_bias
        )
        out_blocks.append(middle_activation + alpha_ffn * residual_branch)
        grad_alpha_ffn = grad_alpha_ffn + jnp.sum(upstream * residual_branch)
        branch_grad = (alpha_ffn * upstream).astype(jnp.bfloat16)
        grad_bias_contract = grad_bias_contract + jnp.sum(
            branch_grad, axis=(0, 1), dtype=jnp.float32
        )
        grad_contract = grad_contract + jnp.einsum(
            "stf,std->fd", hidden_low, branch_grad, preferred_element_type=jnp.float32
        )
        hidden_grad = jnp.einsum(
            "std,fd->stf", branch_grad, contract_full, preferred_element_type=jnp.float32
        )
        pre_grad = gelu_back(hidden_grad)[0].astype(jnp.bfloat16)
        grad_bias_expand = grad_bias_expand + jnp.sum(pre_grad, axis=(0, 1), dtype=jnp.float32)
        grad_expand = grad_expand + jnp.einsum(
            "stf,std->fd", pre_grad, middle_low, preferred_element_type=jnp.float32
        )
        middle_grad = upstream + jnp.einsum(
            "stf,fd->std", pre_grad, expand_full, preferred_element_type=jnp.float32
        )
        grad_alpha_attend = grad_alpha_attend + jnp.sum(middle_grad * attention_result)
        attend_grad = (alpha_attend * middle_grad).astype(jnp.bfloat16)
        grad_output = grad_output + jnp.einsum(
            "std,ste->de", heads_tok, attend_grad, preferred_element_type=jnp.float32
        )
        heads_grad_tok = jnp.einsum(
            "ste,de->std", attend_grad, output_full, preferred_element_type=jnp.float32
        ).astype(jnp.bfloat16)
        heads_grad = lax.all_to_all(heads_grad_tok, "mp", split_axis=2, concat_axis=1, tiled=True)
        heads_grad = heads_grad.reshape(per_micro, length, heads_here, HEAD_DIM)
        query_grad, key_grad, value_grad = attend_back(
            query_all, key_all, value_all, documents, span_rows, log_sums, heads_grad
        )
        query_key_value_gradient = (
            jnp.stack((query_grad, key_grad, value_grad), 2)
            .reshape(per_micro, length, 3 * head_cols)
            .astype(jnp.bfloat16)
        )
        grad_qkv_weight = grad_qkv_weight + jnp.einsum(
            "tmf,tmp->fp",
            layer_inputs,
            query_key_value_gradient,
            preferred_element_type=jnp.float32,
        )
        partial_grad = jnp.einsum(
            "nrj,yj->nry",
            query_key_value_gradient,
            query_key_value_weight,
            preferred_element_type=jnp.float32,
        )
        head_part = lax.psum_scatter(
            partial_grad.astype(jnp.bfloat16), "mp", scatter_dimension=1, tiled=True
        ).astype(jnp.float32)
        grad_blocks.append(middle_grad + head_part)
    layer_out = jnp.concatenate(out_blocks, 0)
    in_grad = jnp.concatenate(grad_blocks, 0)
    output_part, expand_part, contract_part = (
        lax.psum_scatter(
            grad_output.astype(jnp.bfloat16), "mp", scatter_dimension=0, tiled=True
        ).astype(jnp.float32),
        lax.psum_scatter(
            grad_expand.astype(jnp.bfloat16), "mp", scatter_dimension=0, tiled=True
        ).astype(jnp.float32),
        lax.psum_scatter(
            grad_contract.astype(jnp.bfloat16), "mp", scatter_dimension=0, tiled=True
        ).astype(jnp.float32),
    )
    matrix_grads = (
        lax.psum(grad_qkv_weight[:, :head_cols].astype(jnp.bfloat16), "dp").astype(jnp.float32),
        lax.psum(grad_qkv_weight[:, head_cols : 2 * head_cols].astype(jnp.bfloat16), "dp").astype(
            jnp.float32
        ),
        lax.psum(grad_qkv_weight[:, 2 * head_cols :].astype(jnp.bfloat16), "dp").astype(
            jnp.float32
        ),
        lax.psum(output_part.astype(jnp.bfloat16), "dp").astype(jnp.float32),
        lax.psum(expand_part.astype(jnp.bfloat16), "dp").astype(jnp.float32),
        lax.psum(contract_part.astype(jnp.bfloat16), "dp").astype(jnp.float32),
    )
    small_local = jnp.concatenate(
        (grad_bias_expand, grad_bias_contract, jnp.stack((grad_alpha_attend, grad_alpha_ffn)))
    )
    small_grad = lax.psum(small_local, ("dp", "mp"))
    first_new = 0.5 * small_first + 0.5 * small_grad
    second_new = 0.5 * small_second + 0.5 * small_grad * small_grad
    correction = 1.0 - 0.5**STEP
    small_new = small_params - adam_rate * (first_new / correction) / (
        jnp.sqrt(second_new / correction) + 1e-08
    )
    olds = (buffer_query, buffer_key, buffer_value, buffer_output, buffer_expand, buffer_contract)
    weights_old = (w_query, w_key, w_value, w_output, w_expand, w_contract)
    by_columns = (True, True, True, False, False, False)
    buffers = tuple(
        (0.5 * old_buffer + grad_matrix for old_buffer, grad_matrix in zip(olds, matrix_grads))
    )
    squares = lax.psum(tuple((jnp.sum(matrix * matrix) for matrix in buffers)), "mp")
    iterates = [
        matrix / (jnp.sqrt(square_sum) + 1e-07) for matrix, square_sum in zip(buffers, squares)
    ]
    for newton_step in range(5):
        gram_sums = jax.tree.map(
            lambda part: part.astype(jnp.float32),
            lax.psum(
                shortened(
                    tuple(
                        (
                            gram_part(iterate, column_flag)
                            for iterate, column_flag in zip(iterates, by_columns)
                        )
                    )
                ),
                "mp",
            ),
        )
        iterates = [
            newton_update(iterate, gram_sum, column_flag)
            for iterate, gram_sum, column_flag in zip(iterates, gram_sums, by_columns)
        ]
    new_weights = tuple(
        (
            weight - rate * iterate
            for weight, rate, iterate in zip(weights_old, muon_rates, iterates)
        )
    )
    return (layer_out, in_grad) + buffers + new_weights + (small_new, first_new, second_new)


max_doc = 512
q_rows = 256
f32 = jnp.float32
bf16 = jnp.bfloat16
nt = (((1,), (1,)), ((), ()))
nn = (((1,), (0,)), ((), ()))
tn = (((0,), (0,)), ((), ()))
gelu_root = 0.7978845608028654
gelu_cube = 0.044715


def mm(a, b, dims):
    return lax.dot_general(a, b, dims, preferred_element_type=f32)


def swap(x, axis, mask):
    size = lax.axis_size(axis)
    return lax.ppermute(x, axis, [(a, a ^ mask) for a in range(size)])


def reorder(x, index, axis):
    parts = [
        lax.dynamic_slice_in_dim(x, slot ^ index, 1, axis) for slot in range(x.shape[axis])
    ]
    return jnp.concatenate(parts, axis)


def pick(x, index):
    return lax.dynamic_index_in_dim(x, index, 0, keepdims=False)


def like(shape, dtype):
    return jax.ShapeDtypeStruct(shape, dtype)


whole = pl.BlockSpec(memory_space=pltpu.VMEM)
hbm = pl.BlockSpec(memory_space=pl.ANY)


def run(kernel, place, args, outs, name, grid=(1,), in_specs=None, out_specs=None, scratch=(), flops=0, spare=4):
    moved = sum(a.size * a.dtype.itemsize for a in args)
    moved += sum(o.size * jnp.dtype(o.dtype).itemsize for o in outs)
    held = moved + sum(
        math.prod(b.shape) * b.dtype.itemsize for b in scratch if b.memory_space == pltpu.VMEM
    )
    return pl.pallas_call(
        kernel,
        grid_spec=pltpu.PrefetchScalarGridSpec(
            num_scalar_prefetch=1,
            grid=grid,
            in_specs=in_specs or [whole] * len(args),
            out_specs=out_specs or [whole] * len(outs),
            scratch_shapes=list(scratch),
        ),
        out_shape=list(outs),
        compiler_params=pltpu.CompilerParams(vmem_limit_bytes=min(56 << 20, held + (spare << 20))),
        cost_estimate=pl.CostEstimate(
            flops=flops, bytes_accessed=moved if flops else 0, transcendentals=0
        ),
        name=name,
    )(place, *args)


def weight_pieces_kernel(place, q, k, v, o, e, c, qkv_out, rest_out, turned):
    span = o.shape[0]
    at = pl.multiple_of(place[1] * span, span)
    for which, ref in enumerate((q, k, v)):
        turned[...] = ref[...].T
        qkv_out[which * span : (which + 1) * span, :] = turned[pl.ds(at, span), :].astype(bf16)
    hid = e.shape[0]
    rest_out[:span, :] = o[...].astype(bf16)
    rest_out[span : span + hid, :] = e[...].astype(bf16)
    rest_out[span + hid :, :] = c[...].astype(bf16)


def buffer_pieces_kernel(place, q, k, v, o, e, c, att_out, ffn_out, turned):
    span = o.shape[0]
    at = pl.multiple_of(place[1] * span, span)
    for which, ref in enumerate((q, k, v)):
        turned[...] = ref[...].T
        att_out[which] = 0.5 * turned[pl.ds(at, span), :]
    att_out[3] = 0.5 * o[...]
    ffn_out[0] = 0.5 * c[...]
    ffn_out[1] = 0.5 * e[...]


def pieces(kernel, place, arrays, outs, name):
    q, k, v, o, e, c = arrays
    spots = lax.axis_size("dp")
    span, hid = o.shape[0] // spots, e.shape[0] // spots
    row = lambda size: pl.BlockSpec((size, D), lambda g, place: (place[1], 0))
    return run(
        kernel,
        place,
        arrays,
        outs,
        name,
        in_specs=[whole, whole, whole, row(span), row(hid), row(hid)],
        spare=56,
        scratch=[pltpu.VMEM((q.shape[1], D), f32)],
    )


def split_positions_kernel(place, *refs):
    count = len(refs) // 2
    for u in range(count):
        refs[count + u][...] = refs[u][0].astype(bf16)


def split_positions(x, place):
    planes, span, width = x.shape
    block = lambda u: pl.BlockSpec((1, span, width), lambda g, place: (place[0] ^ u, 0, 0))
    return run(
        split_positions_kernel,
        place,
        [x] * planes,
        [like((span, width), bf16)] * planes,
        "split_positions",
        in_specs=[block(u) for u in range(planes)],
    )


def join_positions_kernel(place, *refs):
    out = refs[-1]
    for u, ref in enumerate(refs[:-1]):
        out[place[0] ^ u] = ref[...].astype(f32)


def join_positions(parts, place):
    span, width = parts[0].shape
    return run(
        join_positions_kernel,
        place,
        parts,
        [like((len(parts), span, width), f32)],
        "join_positions",
    )[0]


def window(first_row):
    return max(0, first_row + 1 - max_doc) // 128 * 128


def pair_weights(own, other, span):
    parts = []
    for which in range(3):
        for m in range(own.shape[0]):
            for half in (own, other):
                parts.append(half[m, 0, which * span : (which + 1) * span, :])
    return jnp.concatenate(parts, 0)


def interleave(own, other):
    return [half for pair in zip(own, other) for half in pair]


def in_lanes(low, high, x, rest):
    lane = lax.broadcasted_iota(jnp.int32, x.shape, 1)
    return jnp.where((lane >= low) & (lane < high), x, rest)


def spare_lanes(half, values, like_x):
    lane = lax.broadcasted_iota(jnp.int32, like_x.shape, 1)
    first = HEAD_DIM * (1 - half)
    out = jnp.zeros_like(like_x)
    for at, value in enumerate(values):
        out = jnp.where(lane == first + at, value, out)
    return out


def head_lanes(half, x, values=()):
    return in_lanes(HEAD_DIM * half, HEAD_DIM * (half + 1), x, spare_lanes(half, values, x))


def two_parts(x):
    high = x.astype(bf16)
    return high, (x - high.astype(f32)).astype(bf16)


def forward_kernel(place, last_ref, in_ref, *refs):
    own, other, x_ref, o_ref, bias_ref, q_ref, v_ref = refs
    length = in_ref.shape[1]
    span = own.shape[2] // 3
    blocks = [(first, window(first), first + q_rows) for first in range(0, length, q_rows)]

    @pl.when(pl.program_id(0) == 0)
    def _():
        for first, low, high in blocks:
            row = first + lax.broadcasted_iota(jnp.int32, (q_rows, high - low), 0)
            col = low + lax.broadcasted_iota(jnp.int32, (q_rows, high - low), 1)
            allowed = (col <= row) & (row <= last_ref[:, low:high])
            bias_ref[first:high, : high - low] = jnp.where(allowed, 0.0, mask_fill)

    weight = pair_weights(own, other, span)
    rows = mm(in_ref[0], weight, nt).astype(bf16)
    query = rows[:, :128] * jnp.asarray(HEAD_DIM**-0.5, bf16)
    x_ref[0, 2] = rows[:, 128:256]
    x_ref[0, 3] = rows[:, 256:]
    one = jnp.asarray(1, bf16)
    for half in range(2):
        q_ref[half] = head_lanes(half, query)
        v_ref[half] = head_lanes(half, rows[:, 256:], (one,))
    for first, low, high in blocks:
        found = []
        for half in range(2):
            spare = HEAD_DIM * (1 - half)
            scores = mm(q_ref[half, first:high, :], x_ref[0, 2, low:high, :], nt)
            scores = scores + bias_ref[first:high, : high - low]
            peak = jnp.max(scores, axis=1, keepdims=True)
            weight = jnp.exp(scores - peak).astype(bf16)
            out = mm(weight, v_ref[half, low:high, :], nn)
            total = out[:, spare : spare + 1]
            found.append(out * (1.0 / total))
            parts = two_parts(-(peak + jnp.log(total)))
            x_ref[0, half, first:high, :] = head_lanes(half, q_ref[half, first:high, :], parts)
        o_ref[first:high, :] = in_lanes(0, HEAD_DIM, found[0], found[1]).astype(bf16)


def attention(place, last, inputs, halves):
    length = inputs.shape[1]
    chips, planes, rows, _ = halves[0].shape
    half = pl.BlockSpec((chips, 1, rows, D), lambda h, place: (0, h, 0, 0))
    return run(
        forward_kernel,
        place,
        [last, inputs, *halves],
        [like((planes, 4, length, 128), bf16), like((length, D), bf16)],
        "attention_forward",
        spare=56,
        grid=(planes,),
        in_specs=[whole, pl.BlockSpec((1, length, D), lambda h, place: (place[0], 0, 0))]
        + [half] * len(halves),
        out_specs=[
            pl.BlockSpec((1, 4, length, 128), lambda h, place: (h, 0, 0, 0)),
            pl.BlockSpec((length, 128), lambda h, place: (0, h)),
        ],
        scratch=[
            pltpu.VMEM((length, 768), f32),
            pltpu.VMEM((2, length, 128), bf16),
            pltpu.VMEM((2, length, 128), bf16),
        ],
        flops=8 * length * D * D + 2 * length * 768 * 512 * planes,
    )


def backward_kernel(
    is_last, spots, place, start_ref, in_hbm, x_ref, g_ref, o_ref, gout_ref, gmid_hbm, *rest
):
    own, other, rest = rest[0], rest[1], rest[2:]
    ins, rest = rest[:-12], rest[-12:]
    keep_ref, give_ref, dk_ref, dv_ref, dq_ref, acc_ref, bias_ref, k_ref, v_ref, gs_ref = rest[:10]
    in_ref, sems = rest[10:]
    length = in_ref.shape[0]
    load_acc = pltpu.make_async_copy(gmid_hbm, acc_ref, sems.at[0])
    load_in = pltpu.make_async_copy(in_hbm.at[place[0]], in_ref, sems.at[1])
    span = own.shape[2] // 3
    chips = spots // 2
    step = pl.program_id(0)
    blocks = [(first, window(first), first + q_rows) for first in range(0, length, q_rows)]

    @pl.when(step == 0)
    def _():
        load_acc.start()
        load_in.start()
        for first, low, high in blocks:
            col = low + lax.broadcasted_iota(jnp.int32, (high - low, q_rows), 0)
            row = first + lax.broadcasted_iota(jnp.int32, (high - low, q_rows), 1)
            allowed = (col <= row) & (col >= start_ref[:, first:high])
            bias_ref[: high - low, first:high] = jnp.where(allowed, 0.0, mask_fill)

    dk_ref[...] = jnp.zeros_like(dk_ref)
    dv_ref[...] = jnp.zeros_like(dv_ref)
    one = jnp.asarray(1, bf16)
    product = g_ref[...].astype(f32) * o_ref[...].astype(f32)
    for half in range(2):
        k_ref[half] = head_lanes(half, x_ref[0, 2], (one, one))
        v_ref[half] = head_lanes(half, x_ref[0, 3], (one, one))
        delta = jnp.sum(head_lanes(half, product), axis=1, keepdims=True)
        gs_ref[half] = head_lanes(half, g_ref[...], two_parts(-delta))
    for first, low, high in blocks:
        q_both = jnp.concatenate([head_lanes(half, x_ref[0, half, first:high, :]) for half in range(2)], 0)
        g_both = jnp.concatenate([head_lanes(half, g_ref[first:high, :]) for half in range(2)], 0)
        dq = jnp.zeros((q_rows, 128), f32)
        for at in range(low, high, q_rows):
            keys = slice(at, at + q_rows)
            bias = bias_ref[at - low : at - low + q_rows, first:high]
            probs, g_scores = [], []
            for half in range(2):
                scores = mm(k_ref[half, keys, :], x_ref[0, half, first:high, :], nt) + bias
                weight = jnp.exp(scores)
                g_probs = mm(v_ref[half, keys, :], gs_ref[half, first:high, :], nt)
                probs.append(weight.astype(bf16))
                g_scores.append((weight * g_probs).astype(bf16))
            k_both = jnp.concatenate([head_lanes(half, x_ref[0, 2, keys, :]) for half in range(2)], 0)
            dq = dq + mm(jnp.concatenate(g_scores, 0), k_both, tn)
            dv_ref[keys, :] += mm(jnp.concatenate(probs, 1), g_both, nn)
            dk_ref[keys, :] += mm(jnp.concatenate(g_scores, 1), q_both, nn)
        dq_ref[first:high, :] = (dq * HEAD_DIM**-0.5).astype(bf16)
    grads = (dq_ref[...], dk_ref[...].astype(bf16), dv_ref[...].astype(bf16))
    grads = jnp.concatenate(grads, 1)
    weight = pair_weights(own, other, span)

    @pl.when(step == 0)
    def _():
        load_acc.wait()
        load_in.wait()

    acc_ref[...] += mm(grads, weight, nn)
    all_rows = mm(grads, in_ref[...], tn).astype(bf16)
    for which in range(4):
        if which < 3:
            rows = all_rows[which * 128 : (which + 1) * 128, :]
        else:
            rows = gout_ref[...]
        for m in range(chips):
            for c, ref in enumerate((keep_ref, give_ref)):
                at = (2 * m + c) * span
                ref[m, 0, which * span : (which + 1) * span, :] = rows[at : at + span, :]

    @pl.when(step == pl.num_programs(0) - 1)
    def _():
        if not is_last:
            save = pltpu.make_async_copy(acc_ref, ins[0], sems.at[0])
            save.start()
            save.wait()
            return
        rows = ins[0].shape[0]
        for u, ref in enumerate(ins):
            at = pl.multiple_of((place[0] ^ u) * rows, rows)
            ref[...] = acc_ref[pl.ds(at, rows), :].astype(bf16)


def attention_back(
    place, start, inputs, halves, qkv, heads_grad, heads, grad_output, so_far, first, count, is_last
):
    length = inputs.shape[1]
    chips, planes, rows, _ = halves[0].shape
    spots = 2 * chips
    span = rows // 3
    half = pl.BlockSpec((chips, 1, rows, D), lambda h, place: (0, first + h, 0, 0))
    out_half = pl.BlockSpec((chips, 1, 4 * span, D), lambda h, place: (0, h, 0, 0))
    outs = [like((length // planes, D), bf16)] * planes if is_last else [like((length, D), f32)]
    out = run(
        functools.partial(backward_kernel, is_last, spots),
        place,
        [start, inputs, qkv, heads_grad, heads, grad_output, so_far, *halves],
        outs + [like((chips, count, 4 * span, D), bf16)] * 2,
        "attention_backward",
        spare=56,
        grid=(count,),
        in_specs=[
            whole,
            hbm,
            pl.BlockSpec((1, 4, length, 128), lambda h, place: (first + h, 0, 0, 0)),
            pl.BlockSpec((length, 128), lambda h, place: (0, first + h)),
            pl.BlockSpec((length, 128), lambda h, place: (0, first + h)),
            pl.BlockSpec((128, D), lambda h, place: (first + h, 0)),
            hbm,
        ]
        + [half] * 2,
        out_specs=([whole] * planes if is_last else [hbm]) + [out_half] * 2,
        scratch=[
            pltpu.VMEM((length, 128), f32),
            pltpu.VMEM((length, 128), f32),
            pltpu.VMEM((length, 128), bf16),
            pltpu.VMEM((length, D), f32),
            pltpu.VMEM((768, length), f32),
            pltpu.VMEM((2, length, 128), bf16),
            pltpu.VMEM((2, length, 128), bf16),
            pltpu.VMEM((2, length, 128), bf16),
            pltpu.VMEM((length, D), bf16),
            pltpu.SemaphoreType.DMA((2,)),
        ],
        flops=(12 * length * D * D + 5 * length * 768 * 512 * planes) * count // planes,
    )
    return out[:-2], out[-2], out[-1]


def ffn_kernel(planes, spots, per, place, *refs):
    alphas, in_hbm, heads_hbm = refs[:3]
    ups = refs[3 : 3 + planes]
    halves = refs[3 + planes : 3 + planes + spots]
    bias_ref, bout_ref = refs[3 + planes + spots : 5 + planes + spots]
    outs = refs[5 + planes + spots :]
    lays = outs[:planes]
    keep_ref, give_ref, gout_ref, gheads_hbm, gmid_hbm, gbin_ref, gbout_ref, galpha_ref = outs[
        planes : planes + 8
    ]
    (
        attended, middle, mid_low, g_low, up, branch, o_low, lay, weights, in_ref, heads_ref,
        o_parts, gmid_ref, gheads_ref, sems, w_sems, out_sems,
    ) = outs[planes + 8 :]
    chips = spots // 2
    length = in_ref.shape[0]
    block = length // planes
    hid = keep_ref.shape[2] // planes
    span = halves[0].shape[1] - 2 * hid
    step = pl.program_id(0)
    steps = pl.num_programs(0)
    alpha_att, alpha_ffn = alphas[0], alphas[1]
    size = 512
    tiles = [slice(at, at + size) for at in range(0, length, size)]

    def order(at):
        return 2 * (at % chips) + at // chips

    def weight_copy(at):
        return pltpu.make_async_copy(
            halves[order(at)].at[:, span:, :], weights.at[at], w_sems.at[at]
        )

    @pl.when(step == 0)
    def _():
        first = [
            pltpu.make_async_copy(half.at[:, :span, :], o_parts.at[at], sems.at[at])
            for at, half in enumerate(halves)
        ]
        first.append(pltpu.make_async_copy(heads_hbm, heads_ref, sems.at[spots]))
        first.append(pltpu.make_async_copy(in_hbm.at[place[0]], in_ref, sems.at[spots + 1]))
        for u in range(planes):
            at = pl.multiple_of((place[0] ^ u) * block, block)
            first.append(
                pltpu.make_async_copy(ups[u], up.at[pl.ds(at, block), :], sems.at[spots + 2 + u])
            )
        for copy in first:
            copy.start()
        for at in range(spots):
            weight_copy(at).start()
        for copy in first:
            copy.wait()
        for k in range(planes):
            for at in range(spots):
                row = (k * spots + at) * span
                o_low[row : row + span, :] = o_parts[at, k]
        total = jnp.zeros((1, D), f32)
        for t in tiles:
            found = mm(heads_ref[t, :], o_low[...], nn)
            attended[t, :] = found
            mid = in_ref[t, :].astype(f32) + alpha_att * found
            middle[t, :] = mid
            mid_low[t, :] = mid.astype(bf16)
            upstream = up[t, :].astype(f32)
            grad = (alpha_ffn * upstream).astype(bf16)
            g_low[t, :] = grad
            total = total + jnp.sum(grad.astype(f32), axis=0, keepdims=True)
            branch[t, :] = jnp.zeros((size, D), f32)
            gmid_ref[t, :] = upstream
        gbout_ref[...] = total

    for at in range(spots):

        @pl.when(step == at // per)
        def _():
            weight_copy(at).wait()

    rows = [weights[step * per + g] for g in range(per)]
    expand = jnp.concatenate([row[:, :hid, :].reshape(planes * hid, D) for row in rows], 0)
    contract = jnp.concatenate([row[:, hid:, :].reshape(planes * hid, D) for row in rows], 0)
    bias = bias_ref[0]
    gc = jnp.zeros((per * planes * hid, D), f32)
    ge = jnp.zeros((per * planes * hid, D), f32)
    gb = jnp.zeros((1, per * planes * hid), f32)
    for t in tiles:
        mid = mid_low[t, :]
        grad = g_low[t, :]
        pre = mm(mid, expand, nt) + bias
        square = pre * pre
        tanh = jnp.tanh(gelu_root * pre * (1.0 + gelu_cube * square))
        half = 0.5 * (1.0 + tanh)
        hidden = (pre * half).astype(bf16)
        slope = half + (0.5 * gelu_root) * pre * (1.0 - tanh * tanh) * (
            1.0 + (3.0 * gelu_cube) * square
        )
        branch[t, :] += mm(hidden, contract, nn)
        g_pre = (mm(grad, contract, nt) * slope).astype(bf16)
        gmid_ref[t, :] += mm(g_pre, expand, nn)
        gc = gc + mm(hidden, grad, tn)
        ge = ge + mm(g_pre, mid, tn)
        gb = gb + jnp.sum(g_pre.astype(f32), axis=0, keepdims=True)
    gc = gc.astype(bf16)
    ge = ge.astype(bf16)
    group = planes * hid

    def store(ref):
        for g in range(per):
            ref[g, 0] = gc[g * group : (g + 1) * group, :]
            ref[g, 1] = ge[g * group : (g + 1) * group, :]

    pl.when(step < steps // 2)(lambda: store(keep_ref))
    pl.when(step >= steps // 2)(lambda: store(give_ref))
    gbin_ref[0] = gb

    @pl.when(step == steps - 1)
    def _():
        sum_ffn = jnp.zeros((1, D), f32)
        sum_att = jnp.zeros((1, D), f32)
        gout = jnp.zeros((D, D), f32)
        copies = []
        for at, t in enumerate(tiles):
            gm = gmid_ref[t, :]
            copies.append(
                pltpu.make_async_copy(gmid_ref.at[t, :], gmid_hbm.at[t, :], out_sems.at[0, at])
            )
            copies[-1].start()
            g_att = (alpha_att * gm).astype(bf16)
            gheads_ref[t, :] = mm(g_att, o_low[...], nt).astype(bf16)
            copies.append(
                pltpu.make_async_copy(gheads_ref.at[t, :], gheads_hbm.at[t, :], out_sems.at[1, at])
            )
            copies[-1].start()
            gout = gout + mm(heads_ref[t, :], g_att, tn)
            sum_att = sum_att + jnp.sum(gm * attended[t, :], axis=0, keepdims=True)
            final = branch[t, :] + bout_ref[...]
            lay[t, :] = middle[t, :] + alpha_ffn * final
            sum_ffn = sum_ffn + jnp.sum(up[t, :].astype(f32) * final, axis=0, keepdims=True)
        gout_ref[...] = gout.astype(bf16)
        galpha_ref[0:1, :] = sum_att
        galpha_ref[1:2, :] = sum_ffn
        for u, ref in enumerate(lays):
            at = pl.multiple_of((place[0] ^ u) * block, block)
            ref[...] = lay[pl.ds(at, block), :].astype(bf16)
        for copy in copies:
            copy.wait()


def feed_forward(place, alphas, inputs, heads, ups, halves, bias, bout):
    length = inputs.shape[1]
    planes = len(ups)
    spots = len(halves)
    chips = spots // 2
    span, hid = heads.shape[1] // (planes * spots), bias.shape[-1] // planes
    per = 2 if chips % 2 == 0 else 1
    steps = spots // per
    bias = bias.reshape(steps, 1, per * planes * hid)
    tiles = length // 512
    group = planes * hid
    out = run(
        functools.partial(ffn_kernel, planes, spots, per),
        place,
        [alphas, inputs, heads, *ups, *halves, bias, bout],
        [like((length // planes, D), bf16)] * planes
        + [
            like((chips, 2, group, D), bf16),
            like((chips, 2, group, D), bf16),
            like((D, D), bf16),
            like((length, D), bf16),
            like((length, D), f32),
            like((steps, 1, per * group), f32),
            like((1, D), f32),
            like((2, D), f32),
        ],
        "feed_forward",
        spare=56,
        grid=(steps,),
        in_specs=[pl.BlockSpec(memory_space=pltpu.SMEM)]
        + [hbm] * (2 + planes + spots)
        + [pl.BlockSpec((1, 1, per * group), lambda t, place: (t, 0, 0)), whole],
        out_specs=[whole] * planes
        + [
            pl.BlockSpec(
                (per, 2, group, D), lambda t, place: (jnp.minimum(t, steps // 2 - 1), 0, 0, 0)
            ),
            pl.BlockSpec(
                (per, 2, group, D), lambda t, place: (jnp.maximum(t - steps // 2, 0), 0, 0, 0)
            ),
            whole,
            hbm,
            hbm,
            pl.BlockSpec((1, 1, per * group), lambda t, place: (t, 0, 0)),
            whole,
            whole,
        ],
        scratch=[
            pltpu.VMEM((length, D), f32),
            pltpu.VMEM((length, D), f32),
            pltpu.VMEM((length, D), bf16),
            pltpu.VMEM((length, D), bf16),
            pltpu.VMEM((length, D), bf16),
            pltpu.VMEM((length, D), f32),
            pltpu.VMEM((D, D), bf16),
            pltpu.VMEM((length, D), f32),
            pltpu.VMEM((spots, planes, 2 * hid, D), bf16),
            pltpu.VMEM((length, D), bf16),
            pltpu.VMEM((length, D), bf16),
            pltpu.VMEM((spots, planes, span, D), bf16),
            pltpu.VMEM((length, D), f32),
            pltpu.VMEM((length, D), bf16),
            pltpu.SemaphoreType.DMA((spots + 2 + planes,)),
            pltpu.SemaphoreType.DMA((spots,)),
            pltpu.SemaphoreType.DMA((2, tiles)),
        ],
        flops=12 * length * D * 2 * chips * group,
    )
    return out[:planes], out[planes:]


def att_core_kernel(place, keep, got, *outs):
    rows = keep.shape[2]
    for m, out in enumerate(outs):
        for k in range(keep.shape[1]):
            total = keep[m, k].astype(f32) + got[m, k].astype(f32)
            out[k * rows : (k + 1) * rows, :] = total.astype(bf16)


def small_write(out, total):
    at = out.shape[0] - 2 * total.shape[0]
    high = total.astype(bf16)
    out[at : at + total.shape[0], :] = high
    out[at + total.shape[0] :, :] = (total - high.astype(f32)).astype(bf16)


def small_read(ref):
    rows = ref.shape[0]
    return ref[rows - 16 : rows - 8, :].astype(f32) + ref[rows - 8 :, :].astype(f32)


def ffn_core_kernel(place, own, got, small, *outs):
    rows = own.shape[0] // len(outs)
    total = small[...]
    for at, out in enumerate(outs):
        for r in range(0, rows, 256):
            a = own[at * rows + r : at * rows + r + 256, :].astype(f32)
            b = got[at * rows + r : at * rows + r + 256, :].astype(f32)
            out[r : r + 256, :] = (a + b).astype(bf16)
        small_write(out, total)


def ffn_chip_kernel(chips, planes, place, old, *refs):
    ins, give, keep, both = refs[:chips], refs[-3], refs[-2], refs[-1]
    hid = old.shape[1]
    rows = planes * hid
    small = small_read(ins[0])
    for ref in ins[1:]:
        small = small + small_read(ref)
    for which in range(2):
        for k in range(planes):
            at = which * rows + k * hid
            total = ins[0][at : at + hid, :].astype(f32)
            for ref in ins[1:]:
                total = total + ref[at : at + hid, :].astype(f32)
            if k == 0:
                total = total + old[which]
            both[which, k * hid : (k + 1) * hid, :] = total.astype(bf16)
    mine = place[0] // (planes // 2)
    keep[:rows, :] = both[mine]
    give[:rows, :] = both[1 - mine]
    small_write(keep, small)
    small_write(give, small)


def plane_sum_kernel(mask, planes, place, keep, got, out):
    rows = keep.shape[0] - 16
    hid = rows // planes
    for k in range(planes):
        at, by = k * hid, (k ^ mask) * hid
        total = keep[at : at + hid, :].astype(f32) + got[by : by + hid, :].astype(f32)
        out[at : at + hid, :] = total.astype(bf16)
    small_write(out, small_read(keep) + small_read(got))


def att_to_owner_kernel(chips, planes, place, *refs):
    ins, old, outs, scratch = refs[:chips], refs[chips], refs[chips + 1 : -1], refs[-1]
    span = old.shape[1]
    for k in range(planes):
        for which in range(4):
            at = (k * 4 + which) * span
            total = ins[0][at : at + span, :].astype(f32)
            for ref in ins[1:]:
                total = total + ref[at : at + span, :].astype(f32)
            if k == 0:
                total = total + old[which]
            scratch[which, k * span : (k + 1) * span, :] = total.astype(bf16)
    for u, out in enumerate(outs):
        out[...] = scratch[place[0] ^ u]


def near_sum_kernel(planes, place, keep, got, *refs):
    ins, (out, small_out) = refs[:planes], refs[planes:]
    rows = keep.shape[0] - 16
    hid = rows // planes
    span = ins[0].shape[0] // planes
    for k in range(planes):
        at, by = k * hid, (k ^ 1) * hid
        total = keep[at : at + hid, :].astype(f32) + got[by : by + hid, :].astype(f32)
        out[at : at + hid, :] = total.astype(bf16)
        total = jnp.zeros((span, D), f32)
        for u, ref in enumerate(ins):
            at = (k ^ u) * span
            total = total + ref[at : at + span, :].astype(f32)
        out[rows + k * span : rows + (k + 1) * span, :] = total.astype(bf16)
    small_out[...] = small_read(keep) + small_read(got)


def newton_kernel(planes, chips, base_row, groups, with_rows, place, own, other, *refs):
    outs, x_ref, low_ref = refs[:-2], refs[-2], refs[-1]
    dim, cols = x_ref.shape
    group = cols // planes
    half_group = group // 2
    span = half_group // chips
    tall = own.shape[0] // chips
    chunk = 512
    total = jnp.zeros((1, D), f32)
    for half in (own, other):
        for m in range(chips):
            at = m * tall + base_row
            part = half[at : at + planes * span, :].astype(f32)
            total = total + jnp.sum(part * part, axis=0, keepdims=True)
    inverse = 1.0 / (jnp.sqrt(jnp.sum(total, axis=1, keepdims=True)) + 1e-07)
    for k in range(planes):
        rows = []
        for half in (own, other):
            for m in range(chips):
                at = m * tall + base_row + k * span
                rows.append(half[at : at + span, :])
        part = jnp.concatenate(rows, 0).astype(f32).T * inverse
        x_ref[:, k * group : (k + 1) * group] = part
        low_ref[:, k * group : (k + 1) * group] = part.astype(bf16)
    diagonal = lax.broadcasted_iota(jnp.int32, (dim, dim), 0) == lax.broadcasted_iota(
        jnp.int32, (dim, dim), 1
    )

    def step(spans):
        gram = jnp.zeros((dim, dim), f32)
        for at in range(0, cols, chunk):
            part = low_ref[:, at : at + chunk]
            gram = gram + mm(part, part, nt)
        trace = jnp.sum(
            jnp.sum(jnp.where(diagonal, gram, 0.0), axis=0, keepdims=True), axis=1, keepdims=True
        )
        shift = trace * (1.0 / dim)
        rest = jnp.where(diagonal, gram - shift, gram)
        rest_low = rest.astype(bf16)
        poly = (newton_two + 2.0 * newton_three * shift) * rest + newton_three * mm(
            rest_low, rest_low, nn
        )
        poly = poly.astype(bf16)
        scale = newton_one + newton_two * shift + newton_three * shift * shift
        for part in spans:
            new = scale * x_ref[:, part] + mm(poly, low_ref[:, part], nn)
            x_ref[:, part] = new
            low_ref[:, part] = new.astype(bf16)

    everything = [slice(at, at + chunk) for at in range(0, cols, chunk)]
    for _ in range(4):
        step(everything)
    if with_rows:
        step(everything)
    else:
        step([slice(k * group, k * group + half_group) for k in groups])
    for k, out in zip(groups, outs):
        part = x_ref[:, k * group : (k + 1) * group].T.astype(bf16)
        base = half_group if with_rows else 0
        for m in range(chips):
            chip = place[1] // 2 ^ m
            if with_rows:
                at = m * tall + base_row + k * span
                out[pl.ds(pl.multiple_of(chip * span, span), span), :] = own[at : at + span, :]
            to = pl.multiple_of(base + chip * span, span)
            out[pl.ds(to, span), :] = part[m * span : (m + 1) * span, :]


def newton(place, own, other, planes, base_row, cols, groups, with_rows, name):
    rows = cols // planes // 2 * (2 if with_rows else 1)
    return run(
        functools.partial(
            newton_kernel, planes, lax.axis_size("dp") // 2, base_row, groups, with_rows
        ),
        place,
        [own, other],
        [like((rows, D), bf16)] * len(groups),
        name,
        scratch=[pltpu.VMEM((D, cols), f32), pltpu.VMEM((D, cols), bf16)],
        flops=10 * D * D * (2 * cols + D),
    )


def momentum_rows_kernel(planes, chips, group, place, own, out):
    span = out.shape[0] // chips
    for m in range(chips):
        to = pl.multiple_of((place[1] // 2 ^ m) * span, span)
        at = m * (own.shape[0] // chips) + group * span
        out[pl.ds(to, span), :] = own[at : at + span, :]


def att_final_kernel(planes, span, place, mine, got, *refs):
    old, outs, rows = refs[:4], refs[4:-1], refs[-1]
    half = mine.shape[1] // 2
    core = place[1] % 2
    for which in range(4):
        slot = place[0] ^ which
        for kind in range(2):
            for at in range(0, half, span):
                from_at = kind * half + at
                rows[pl.ds(pl.multiple_of(2 * at + core * span, span), span), :] = mine[
                    slot, from_at : from_at + span, :
                ]
                rows[pl.ds(pl.multiple_of(2 * at + (1 - core) * span, span), span), :] = got[
                    slot, from_at : from_at + span, :
                ]
            part = rows[...].astype(f32)
            part = part.T if which < 3 else part
            if kind == 0:
                outs[which][...] = part
            else:
                outs[4 + which][...] = old[which][...] - muon_rates[which] * part


def ffn_buffers_kernel(planes, chips, place, own, other, far, far_got, eo, co):
    span = far.shape[0] // chips
    core = place[1] % 2

    def fill(mine_out, far_out):
        for m in range(chips):
            chip = place[1] // 2 ^ m
            here = pl.multiple_of((2 * chip + core) * span, span)
            there = pl.multiple_of((2 * chip + 1 - core) * span, span)
            at = m * (own.shape[0] // chips)
            mine_out[pl.ds(here, span), :] = own[at : at + span, :].astype(f32)
            mine_out[pl.ds(there, span), :] = other[at : at + span, :].astype(f32)
            at = m * span
            here = pl.multiple_of((2 * m + core) * span, span)
            there = pl.multiple_of((2 * m + 1 - core) * span, span)
            far_out[pl.ds(here, span), :] = far[at : at + span, :].astype(f32)
            far_out[pl.ds(there, span), :] = got[at : at + span, :].astype(f32)

    got = far_got
    pl.when(place[0] < planes // 2)(lambda: fill(co, eo))
    pl.when(place[0] >= planes // 2)(lambda: fill(eo, co))


def ffn_final_kernel(planes, chips, place, mine, far, got, we, wc, eo, co):
    rows = mine.shape[0]
    span = rows // chips
    core = place[1] % 2

    def fill(mine_out, mine_w, mine_rate, far_out, far_w, far_rate):
        for m in range(chips):
            at = slice(m * span, (m + 1) * span)
            far_at = slice(rows + m * span, rows + (m + 1) * span)
            here = pl.ds(pl.multiple_of((2 * m + core) * span, span), span)
            there = pl.ds(pl.multiple_of((2 * m + 1 - core) * span, span), span)
            mine_out[here, :] = mine_w[here, :] - mine_rate * mine[at, :].astype(f32)
            mine_out[there, :] = mine_w[there, :] - mine_rate * got[at, :].astype(f32)
            far_out[here, :] = far_w[here, :] - far_rate * far[at, :].astype(f32)
            far_out[there, :] = far_w[there, :] - far_rate * got[far_at, :].astype(f32)

    expand, contract = (eo, we, muon_rates[4]), (co, wc, muon_rates[5])
    pl.when(place[0] < planes // 2)(lambda: fill(*contract, *expand))
    pl.when(place[0] >= planes // 2)(lambda: fill(*expand, *contract))


def shards(
    layer_in,
    doc_ids,
    out_grad,
    w_query,
    w_key,
    w_value,
    w_output,
    w_expand,
    w_contract,
    small_params,
    buffer_query,
    buffer_key,
    buffer_value,
    buffer_output,
    buffer_expand,
    buffer_contract,
    small_first,
    small_second,
):
    planes = lax.axis_size("mp")
    spots = lax.axis_size("dp")
    chips = spots // 2
    plane = lax.axis_index("mp")
    spot = lax.axis_index("dp")
    place = jnp.stack([plane, spot]).astype(jnp.int32)
    length = layer_in.shape[1]
    head_cols = w_query.shape[1]
    hidden_rows = w_expand.shape[0]
    span = head_cols // spots
    hid = hidden_rows // spots
    to_planes = range(1, planes)
    to_chips = range(1, chips)
    weights_old = (w_query, w_key, w_value, w_output, w_expand, w_contract)
    buffers_old = (
        buffer_query,
        buffer_key,
        buffer_value,
        buffer_output,
        buffer_expand,
        buffer_contract,
    )

    def around_planes(x):
        return [x] + [swap(x, "mp", k) for k in to_planes]

    def around_chips(x):
        return [x] + [swap(x, "dp", 2 * m) for m in to_chips]

    def together(*groups):
        return lax.optimization_barrier(groups)

    def together(*groups):
        return lax.optimization_barrier(groups)

    qkv_piece, rest_piece = pieces(
        weight_pieces_kernel,
        place,
        weights_old,
        [like((3 * span, D), bf16), like((span + 2 * hid, D), bf16)],
        "weight_pieces",
    )
    inputs = layer_in
    documents = pick(doc_ids, plane)
    last = (
        jnp.sum(documents[None, :] <= documents[:, None], axis=1, dtype=jnp.int32)[None, :] - 1
    )
    start = jnp.sum(documents[None, :] < documents[:, None], axis=1, dtype=jnp.int32)[None, :]

    def to_slots(bias):
        return reorder(reorder(bias, plane, 0), spot, 1)

    bias = to_slots(small_params[:FF].reshape(planes, spots, hid))
    bias = bias.reshape(planes, chips, 2, hid).transpose(2, 1, 0, 3)
    bias = bias.reshape(2, chips, 1, planes * hid)
    bout = small_params[FF : FF + D].reshape(1, D)
    alphas = small_params[FF + D :]
    token_span = length // planes
    ups = split_positions(out_grad, place)

    qkv_own, ups = together(around_planes(qkv_piece), ups)
    qkv_own = around_chips(jnp.stack(qkv_own))
    rest_own = around_planes(rest_piece)
    qkv_own, rest_own, last, start, bias = together(
        qkv_own, rest_own, last, start, bias
    )
    qkv_own = jnp.stack(qkv_own)
    qkv_halves = [qkv_own, swap(qkv_own, "dp", 1)]
    rest_own, ups = together(jnp.stack(rest_own), ups)
    rest_own = around_chips(rest_own)
    ups = [ups[0]] + [swap(ups[u], "mp", u) for u in to_planes]
    qkv, heads = attention(place, last, inputs, qkv_halves)
    heads, rest_own, ups, buffers_old = together(heads, rest_own, ups, buffers_old)
    rest_halves = interleave(rest_own, [swap(part, "dp", 1) for part in rest_own])
    att_old, ffn_old = pieces(
        buffer_pieces_kernel,
        place,
        buffers_old,
        [like((4, span, D), f32), like((2, hid, D), f32)],
        "buffer_pieces",
    )
    rest_halves, att_old, ffn_old = together(rest_halves, att_old, ffn_old)
    lays, rest = feed_forward(place, alphas, inputs, heads, ups, rest_halves, bias, bout)
    ffn_keep, ffn_give, grad_output, heads_grad, middle_grad, gb_in, gb_out, g_alpha = rest

    ffn_rows = (chips * 2 * planes * hid, D)
    ffn_got = swap(ffn_give.reshape(ffn_rows), "dp", 1)
    gb_in = gb_in.reshape(2, chips, planes, hid).transpose(2, 1, 0, 3).reshape(planes, spots, hid)
    small = jnp.concatenate(
        [to_slots(gb_in).reshape(-1), gb_out.reshape(-1), jnp.sum(g_alpha, axis=1)]
    )
    small = jnp.pad(small, (0, 8 * D - small.size)).reshape(8, D)
    high = lax.reduce_precision(small, 8, 7)
    pair = jnp.concatenate([high, lax.reduce_precision(small - high, 8, 7)]).astype(bf16)
    pair = swap(pair, "dp", 1).astype(f32)
    small = small + pair[:8] + pair[8:]
    parts = run(
        ffn_core_kernel,
        place,
        [ffn_keep.reshape(ffn_rows), ffn_got, small],
        [like((2 * planes * hid + 16, D), bf16)] * chips,
        "ffn_core_sum",
    )
    middle_grad, parts = together(middle_grad, parts)
    got = [parts[0]] + [swap(parts[m], "dp", 2 * m) for m in to_chips]
    lay_far = [swap(lays[u], "mp", u) for u in to_planes[1:]]
    ins, att_keep, att_give = attention_back(
        place, start, inputs, qkv_halves, qkv, heads_grad, heads, grad_output, middle_grad,
        0, planes, True,
    )
    ins, att_keep, att_give, got, lay_far = together(ins, att_keep, att_give, got, lay_far)

    far = planes // 2
    parts = got
    rows = planes * hid
    give, keep = run(
        functools.partial(ffn_chip_kernel, chips, planes),
        place,
        [ffn_old, *parts],
        [like((rows + 16, D), bf16)] * 2,
        "ffn_chip_sum",
        scratch=[pltpu.VMEM((2, rows, D), bf16)],
    )
    give, att_give, lays = together(give, att_give, lays)
    got = swap(give, "mp", far)
    lay_near = swap(lays[1], "mp", 1)
    att_got = swap(att_give, "dp", 1)
    att_parts = run(
        att_core_kernel,
        place,
        [att_keep, att_got],
        [like((planes * 4 * span, D), bf16)] * chips,
        "att_core_sum",
    )
    att_got = [att_parts[0]] + [swap(att_parts[m], "dp", 2 * m) for m in to_chips]
    got, att_got, lay_near = together(got, att_got, lay_near)
    half_sum = run(
        functools.partial(plane_sum_kernel, far, planes),
        place,
        [keep, got],
        [like((rows + 16, D), bf16)],
        "ffn_far_sum",
    )[0]
    got = swap(half_sum, "mp", 1)
    att_parts = run(
        functools.partial(att_to_owner_kernel, chips, planes),
        place,
        att_got + [att_old],
        [like((planes * span, D), bf16)] * planes,
        "att_chip_sum",
        scratch=[pltpu.VMEM((4, planes * span, D), bf16)],
    )
    att_got = [att_parts[0]] + [swap(att_parts[u], "mp", u) for u in to_planes]
    message, small_grad = run(
        functools.partial(near_sum_kernel, planes),
        place,
        [half_sum, got, *att_got],
        [like((rows + planes * span, D), bf16), like((8, D), f32)],
        "near_sum",
    )
    small_grad = small_grad.reshape(-1)[: FF + D + 2]
    message, ins = together(message, ins)
    got = around_chips(message)
    in_got = [ins[0], None, swap(ins[2], "mp", 2), None]
    first_new = 0.5 * small_first + 0.5 * small_grad
    second_new = 0.5 * small_second + 0.5 * small_grad * small_grad
    correction = 1.0 - 0.5**STEP
    small_new = small_params - adam_rate * (first_new / correction) / (
        jnp.sqrt(second_new / correction) + 1e-08
    )
    smalls = (small_new, first_new, second_new)
    got, smalls, in_got, ins = together(got, smalls, in_got, ins)
    in_got[3] = swap(ins[3], "mp", 3)
    in_got[1] = swap(ins[1], "mp", 1)
    own = jnp.concatenate(got)
    other = swap(own, "dp", 1)
    far_m = run(
        functools.partial(momentum_rows_kernel, planes, chips, far),
        place,
        [own],
        [like((hidden_rows // 2, D), bf16)],
        "momentum_rows",
    )[0]
    far_m = swap(far_m, "mp", far)
    att_x = newton(
        place, own, other, planes, rows, D, tuple(range(planes)), True, "newton_att"
    )
    att_x, in_got, other = together(att_x, in_got, other)
    att_x = jnp.stack([att_x[0]] + [swap(att_x[u], "mp", u) for u in to_planes])
    step, far_step = newton(
        place, own, other, planes, 0, planes * hidden_rows, (0, far), False, "newton_ffn"
    )
    step, att_x = together(step, att_x)
    far_step = swap(far_step, "mp", far)
    far_m_got = swap(far_m, "dp", 1)
    att_other = swap(att_x, "dp", 1)
    new_be, new_bc = run(
        functools.partial(ffn_buffers_kernel, planes, chips),
        place,
        [own, other, far_m, far_m_got],
        [like((hidden_rows, D), f32)] * 2,
        "ffn_buffers",
    )
    layer_out = join_positions([lays[0], lay_near, *lay_far], place)
    in_grad = join_positions(in_got, place)
    att_out = run(
        functools.partial(att_final_kernel, planes, span),
        place,
        [att_x, att_other, *weights_old[:4]],
        [like(w.shape, f32) for w in weights_old[:4]] * 2,
        "att_final",
        scratch=[pltpu.VMEM((head_cols, D), bf16)],
    )
    far_step, new_be, layer_out, in_grad, att_out = together(
        far_step, new_be, layer_out, in_grad, att_out
    )
    got = swap(jnp.concatenate([step, far_step]), "dp", 1)
    new_we, new_wc = run(
        functools.partial(ffn_final_kernel, planes, chips),
        place,
        [step, far_step, got, w_expand, w_contract],
        [like((hidden_rows, D), f32)] * 2,
        "ffn_final",
    )
    return (
        (layer_out, in_grad)
        + tuple(att_out[:4])
        + (new_be, new_bc)
        + tuple(att_out[4:])
        + (new_we, new_wc)
        + smalls
    )


def solution(mesh):
    in_specs = (
        P("dp", None, None),
        P("dp", None),
        P("dp", "mp", None),
        P(None, "mp"),
        P(None, "mp"),
        P(None, "mp"),
        P("mp", None),
        P("mp", None),
        P("mp", None),
        P(),
        P(None, "mp"),
        P(None, "mp"),
        P(None, "mp"),
        P("mp", None),
        P("mp", None),
        P("mp", None),
        P(),
        P(),
    )
    out_specs = (
        P("dp", "mp", None),
        P("dp", "mp", None),
        P(None, "mp"),
        P(None, "mp"),
        P(None, "mp"),
        P("mp", None),
        P("mp", None),
        P("mp", None),
        P(None, "mp"),
        P(None, "mp"),
        P(None, "mp"),
        P("mp", None),
        P("mp", None),
        P("mp", None),
        P(),
        P(),
        P(),
    )
    block = mesh.shape["mp"] == 4 and mesh.shape["dp"] == 8
    return jax.shard_map(shards if block else general_shards, mesh=mesh, in_specs=in_specs, out_specs=out_specs, check_vma=False)
```

```python
import functools
import math

import jax
import jax.numpy as jnp
from jax import lax
from jax.experimental import pallas as pl
from jax.experimental.pallas import tpu as pltpu
from jax.sharding import PartitionSpec as P

D = 512
HEAD_DIM = 64
FF = 2048
MICRO = 2
STEP = 10


newton_one = 3.4445
newton_two = -4.775
newton_three = 2.0315
muon_rates = (1.0, 1.0, 1.0, 5.0, 2.0, 1.0)
adam_rate = 0.25
mask_fill = -1e30
highest_precision = lax.Precision.HIGHEST


def shortened(x):
    return jax.tree.map(lambda a: a.astype(jnp.bfloat16) if a.dtype == jnp.float32 else a, x)


def gelu_tanh(values):
    return jax.nn.gelu(values, approximate=True)


def block_scores(query_blk, key_part, docs_query, docs_key, first_row):
    scores = jnp.einsum(
        "sqhd,skhd->shqk", query_blk, key_part, preferred_element_type=jnp.float32
    ) * HEAD_DIM ** (-0.5)
    rows_at = first_row + jnp.arange(query_blk.shape[1])
    cols_at = jnp.arange(key_part.shape[1])
    allowed = (rows_at[:, None] >= cols_at[None, :])[None] & (
        docs_query[:, :, None] == docs_key[:, None, :]
    )
    return jnp.where(allowed[:, None], scores, mask_fill)


def attend(query_all, key_all, value_all, documents, span_rows):
    block_outs = []
    log_sums = []
    for block_index in range(query_all.shape[1] // span_rows):
        row_start = block_index * span_rows
        finish = row_start + span_rows
        scores = block_scores(
            query_all[:, row_start:finish],
            key_all[:, :finish],
            documents[:, row_start:finish],
            documents[:, :finish],
            row_start,
        )
        row_peak = jnp.max(scores, axis=-1, keepdims=True)
        exponent = jnp.exp(scores - row_peak)
        row_total = jnp.sum(exponent, axis=-1, keepdims=True)
        prob_low = (exponent / row_total).astype(jnp.bfloat16)
        block_outs.append(
            jnp.einsum(
                "shqk,skhd->sqhd",
                prob_low,
                value_all[:, :finish],
                preferred_element_type=jnp.float32,
            ).astype(jnp.bfloat16)
        )
        log_sums.append(row_peak + jnp.log(row_total))
    return (jnp.concatenate(block_outs, 1), log_sums)


def attend_back(query_all, key_all, value_all, documents, span_rows, log_sums, heads_grad):
    query_grads = []
    key_grad = jnp.zeros(key_all.shape, jnp.float32)
    value_grad = jnp.zeros(value_all.shape, jnp.float32)
    scale = HEAD_DIM ** (-0.5)
    for block_index in range(query_all.shape[1] // span_rows):
        row_start = block_index * span_rows
        finish = row_start + span_rows
        query_blk = query_all[:, row_start:finish]
        scores = block_scores(
            query_blk,
            key_all[:, :finish],
            documents[:, row_start:finish],
            documents[:, :finish],
            row_start,
        )
        probs = jnp.exp(scores - log_sums[block_index])
        prob_low = probs.astype(jnp.bfloat16)
        grad_blk = heads_grad[:, row_start:finish]
        grad_probs = jnp.einsum(
            "sqhd,skhd->shqk", grad_blk, value_all[:, :finish], preferred_element_type=jnp.float32
        )
        row_delta = jnp.sum(probs * grad_probs, axis=-1, keepdims=True)
        grad_scores = (probs * (grad_probs - row_delta)).astype(jnp.bfloat16)
        query_grads.append(
            jnp.einsum(
                "shqk,skhd->sqhd",
                grad_scores,
                key_all[:, :finish],
                preferred_element_type=jnp.float32,
            )
            * scale
        )
        key_grad = key_grad.at[:, :finish].add(
            jnp.einsum(
                "shqk,sqhd->skhd", grad_scores, query_blk, preferred_element_type=jnp.float32
            )
            * scale
        )
        value_grad = value_grad.at[:, :finish].add(
            jnp.einsum("shqk,sqhd->skhd", prob_low, grad_blk, preferred_element_type=jnp.float32)
        )
    return (jnp.concatenate(query_grads, 1), key_grad, value_grad)


def gram_part(iterate, by_columns):
    if by_columns:
        return lax.dot_general(
            iterate,
            iterate,
            (((1,), (1,)), ((), ())),
            precision=highest_precision,
            preferred_element_type=jnp.float32,
        )
    return lax.dot_general(
        iterate,
        iterate,
        (((0,), (0,)), ((), ())),
        precision=highest_precision,
        preferred_element_type=jnp.float32,
    )


def newton_update(iterate, gram_sum, by_columns):
    square = jnp.dot(gram_sum, gram_sum, precision=highest_precision)
    polynomial = newton_two * gram_sum + newton_three * square
    if by_columns:
        applied = jnp.dot(polynomial, iterate, precision=highest_precision)
    else:
        applied = lax.dot_general(
            iterate,
            polynomial,
            (((1,), (1,)), ((), ())),
            precision=highest_precision,
            preferred_element_type=jnp.float32,
        )
    return newton_one * iterate + applied


def general_shards(
    layer_in,
    doc_ids,
    out_grad,
    w_query,
    w_key,
    w_value,
    w_output,
    w_expand,
    w_contract,
    small_params,
    buffer_query,
    buffer_key,
    buffer_value,
    buffer_output,
    buffer_expand,
    buffer_contract,
    small_first,
    small_second,
):
    group_count = lax.axis_size("mp")
    group_index = lax.axis_index("mp")
    seq_count, length, model_width = layer_in.shape
    per_micro = seq_count // MICRO
    token_span = length // group_count
    head_cols = w_query.shape[1]
    heads_here = head_cols // HEAD_DIM
    span_rows = min(512, length)
    expansion_bias = small_params[:FF]
    contraction_bias = small_params[FF : FF + D]
    alpha_attend = small_params[FF + D]
    alpha_ffn = small_params[FF + D + 1]
    query_key_value_weight = jnp.concatenate((w_query, w_key, w_value), 1).astype(jnp.bfloat16)
    row_local = (
        w_output.astype(jnp.bfloat16),
        w_expand.astype(jnp.bfloat16),
        w_contract.astype(jnp.bfloat16),
    )
    grad_qkv_weight = jnp.zeros((model_width, 3 * head_cols), jnp.float32)
    grad_output = jnp.zeros((D, D), jnp.float32)
    grad_expand = jnp.zeros((FF, D), jnp.float32)
    grad_contract = jnp.zeros((FF, D), jnp.float32)
    grad_bias_expand = jnp.zeros((FF,), jnp.float32)
    grad_bias_contract = jnp.zeros((D,), jnp.float32)
    grad_alpha_attend = jnp.zeros((), jnp.float32)
    grad_alpha_ffn = jnp.zeros((), jnp.float32)
    out_blocks = []
    grad_blocks = []
    for micro_index in range(MICRO):
        rows_from = micro_index * per_micro
        layer_inputs = layer_in[rows_from : rows_from + per_micro]
        documents = doc_ids[rows_from : rows_from + per_micro]
        upstream = out_grad[rows_from : rows_from + per_micro]
        query_key_value_rows = jnp.einsum(
            "orv,vx->orx", layer_inputs, query_key_value_weight, preferred_element_type=jnp.float32
        ).astype(jnp.bfloat16)
        qkv_split = query_key_value_rows.reshape(per_micro, length, 3, heads_here, HEAD_DIM)
        query_all = qkv_split[:, :, 0]
        key_all = qkv_split[:, :, 1]
        value_all = qkv_split[:, :, 2]
        head_outputs, log_sums = attend(query_all, key_all, value_all, documents, span_rows)
        heads_flat = head_outputs.reshape(per_micro, length, head_cols)
        heads_tok = lax.all_to_all(heads_flat, "mp", split_axis=1, concat_axis=2, tiled=True)
        row_now = (
            lax.all_gather(row_local[0], "mp", axis=0, tiled=True),
            lax.all_gather(row_local[1], "mp", axis=0, tiled=True),
            lax.all_gather(row_local[2], "mp", axis=0, tiled=True),
        )
        output_full, expand_full, contract_full = row_now
        attention_result = jnp.einsum(
            "std,de->ste", heads_tok, output_full, preferred_element_type=jnp.float32
        )
        local_in = lax.dynamic_slice_in_dim(
            layer_inputs, group_index * token_span, token_span, 1
        ).astype(jnp.float32)
        middle_activation = local_in + alpha_attend * attention_result
        middle_low = middle_activation.astype(jnp.bfloat16)
        preactivation = (
            jnp.einsum("std,fd->stf", middle_low, expand_full, preferred_element_type=jnp.float32)
            + expansion_bias
        )
        hidden_state, gelu_back = jax.vjp(gelu_tanh, preactivation)
        hidden_low = hidden_state.astype(jnp.bfloat16)
        residual_branch = (
            jnp.einsum("stf,fd->std", hidden_low, contract_full, preferred_element_type=jnp.float32)
            + contraction_bias
        )
        out_blocks.append(middle_activation + alpha_ffn * residual_branch)
        grad_alpha_ffn = grad_alpha_ffn + jnp.sum(upstream * residual_branch)
        branch_grad = (alpha_ffn * upstream).astype(jnp.bfloat16)
        grad_bias_contract = grad_bias_contract + jnp.sum(
            branch_grad, axis=(0, 1), dtype=jnp.float32
        )
        grad_contract = grad_contract + jnp.einsum(
            "stf,std->fd", hidden_low, branch_grad, preferred_element_type=jnp.float32
        )
        hidden_grad = jnp.einsum(
            "std,fd->stf", branch_grad, contract_full, preferred_element_type=jnp.float32
        )
        pre_grad = gelu_back(hidden_grad)[0].astype(jnp.bfloat16)
        grad_bias_expand = grad_bias_expand + jnp.sum(pre_grad, axis=(0, 1), dtype=jnp.float32)
        grad_expand = grad_expand + jnp.einsum(
            "stf,std->fd", pre_grad, middle_low, preferred_element_type=jnp.float32
        )
        middle_grad = upstream + jnp.einsum(
            "stf,fd->std", pre_grad, expand_full, preferred_element_type=jnp.float32
        )
        grad_alpha_attend = grad_alpha_attend + jnp.sum(middle_grad * attention_result)
        attend_grad = (alpha_attend * middle_grad).astype(jnp.bfloat16)
        grad_output = grad_output + jnp.einsum(
            "std,ste->de", heads_tok, attend_grad, preferred_element_type=jnp.float32
        )
        heads_grad_tok = jnp.einsum(
            "ste,de->std", attend_grad, output_full, preferred_element_type=jnp.float32
        ).astype(jnp.bfloat16)
        heads_grad = lax.all_to_all(heads_grad_tok, "mp", split_axis=2, concat_axis=1, tiled=True)
        heads_grad = heads_grad.reshape(per_micro, length, heads_here, HEAD_DIM)
        query_grad, key_grad, value_grad = attend_back(
            query_all, key_all, value_all, documents, span_rows, log_sums, heads_grad
        )
        query_key_value_gradient = (
            jnp.stack((query_grad, key_grad, value_grad), 2)
            .reshape(per_micro, length, 3 * head_cols)
            .astype(jnp.bfloat16)
        )
        grad_qkv_weight = grad_qkv_weight + jnp.einsum(
            "tmf,tmp->fp",
            layer_inputs,
            query_key_value_gradient,
            preferred_element_type=jnp.float32,
        )
        partial_grad = jnp.einsum(
            "nrj,yj->nry",
            query_key_value_gradient,
            query_key_value_weight,
            preferred_element_type=jnp.float32,
        )
        head_part = lax.psum_scatter(
            partial_grad.astype(jnp.bfloat16), "mp", scatter_dimension=1, tiled=True
        ).astype(jnp.float32)
        grad_blocks.append(middle_grad + head_part)
    layer_out = jnp.concatenate(out_blocks, 0)
    in_grad = jnp.concatenate(grad_blocks, 0)
    output_part, expand_part, contract_part = (
        lax.psum_scatter(
            grad_output.astype(jnp.bfloat16), "mp", scatter_dimension=0, tiled=True
        ).astype(jnp.float32),
        lax.psum_scatter(
            grad_expand.astype(jnp.bfloat16), "mp", scatter_dimension=0, tiled=True
        ).astype(jnp.float32),
        lax.psum_scatter(
            grad_contract.astype(jnp.bfloat16), "mp", scatter_dimension=0, tiled=True
        ).astype(jnp.float32),
    )
    matrix_grads = (
        lax.psum(grad_qkv_weight[:, :head_cols].astype(jnp.bfloat16), "dp").astype(jnp.float32),
        lax.psum(grad_qkv_weight[:, head_cols : 2 * head_cols].astype(jnp.bfloat16), "dp").astype(
            jnp.float32
        ),
        lax.psum(grad_qkv_weight[:, 2 * head_cols :].astype(jnp.bfloat16), "dp").astype(
            jnp.float32
        ),
        lax.psum(output_part.astype(jnp.bfloat16), "dp").astype(jnp.float32),
        lax.psum(expand_part.astype(jnp.bfloat16), "dp").astype(jnp.float32),
        lax.psum(contract_part.astype(jnp.bfloat16), "dp").astype(jnp.float32),
    )
    small_local = jnp.concatenate(
        (grad_bias_expand, grad_bias_contract, jnp.stack((grad_alpha_attend, grad_alpha_ffn)))
    )
    small_grad = lax.psum(small_local, ("dp", "mp"))
    first_new = 0.5 * small_first + 0.5 * small_grad
    second_new = 0.5 * small_second + 0.5 * small_grad * small_grad
    correction = 1.0 - 0.5**STEP
    small_new = small_params - adam_rate * (first_new / correction) / (
        jnp.sqrt(second_new / correction) + 1e-08
    )
    olds = (buffer_query, buffer_key, buffer_value, buffer_output, buffer_expand, buffer_contract)
    weights_old = (w_query, w_key, w_value, w_output, w_expand, w_contract)
    by_columns = (True, True, True, False, False, False)
    buffers = tuple(
        (0.5 * old_buffer + grad_matrix for old_buffer, grad_matrix in zip(olds, matrix_grads))
    )
    squares = lax.psum(tuple((jnp.sum(matrix * matrix) for matrix in buffers)), "mp")
    iterates = [
        matrix / (jnp.sqrt(square_sum) + 1e-07) for matrix, square_sum in zip(buffers, squares)
    ]
    for newton_step in range(5):
        gram_sums = jax.tree.map(
            lambda part: part.astype(jnp.float32),
            lax.psum(
                shortened(
                    tuple(
                        (
                            gram_part(iterate, column_flag)
                            for iterate, column_flag in zip(iterates, by_columns)
                        )
                    )
                ),
                "mp",
            ),
        )
        iterates = [
            newton_update(iterate, gram_sum, column_flag)
            for iterate, gram_sum, column_flag in zip(iterates, gram_sums, by_columns)
        ]
    new_weights = tuple(
        (
            weight - rate * iterate
            for weight, rate, iterate in zip(weights_old, muon_rates, iterates)
        )
    )
    return (layer_out, in_grad) + buffers + new_weights + (small_new, first_new, second_new)


max_doc = 512
q_rows = 256
f32 = jnp.float32
bf16 = jnp.bfloat16
nt = (((1,), (1,)), ((), ()))
nn = (((1,), (0,)), ((), ()))
tn = (((0,), (0,)), ((), ()))
gelu_root = 0.7978845608028654
gelu_cube = 0.044715


def mm(a, b, dims):
    return lax.dot_general(a, b, dims, preferred_element_type=f32)


def swap(x, axis, mask):
    size = lax.axis_size(axis)
    return lax.ppermute(x, axis, [(a, a ^ mask) for a in range(size)])


def reorder(x, index, axis):
    parts = [
        lax.dynamic_slice_in_dim(x, slot ^ index, 1, axis) for slot in range(x.shape[axis])
    ]
    return jnp.concatenate(parts, axis)


def pick(x, index):
    return lax.dynamic_index_in_dim(x, index, 0, keepdims=False)


def like(shape, dtype):
    return jax.ShapeDtypeStruct(shape, dtype)


whole = pl.BlockSpec(memory_space=pltpu.VMEM)
hbm = pl.BlockSpec(memory_space=pl.ANY)


def run(kernel, place, args, outs, name, grid=(1,), in_specs=None, out_specs=None, scratch=(), flops=0, spare=4):
    moved = sum(a.size * a.dtype.itemsize for a in args)
    moved += sum(o.size * jnp.dtype(o.dtype).itemsize for o in outs)
    held = moved + sum(
        math.prod(b.shape) * b.dtype.itemsize for b in scratch if b.memory_space == pltpu.VMEM
    )
    return pl.pallas_call(
        kernel,
        grid_spec=pltpu.PrefetchScalarGridSpec(
            num_scalar_prefetch=1,
            grid=grid,
            in_specs=in_specs or [whole] * len(args),
            out_specs=out_specs or [whole] * len(outs),
            scratch_shapes=list(scratch),
        ),
        out_shape=list(outs),
        compiler_params=pltpu.CompilerParams(vmem_limit_bytes=min(56 << 20, held + (spare << 20))),
        cost_estimate=pl.CostEstimate(
            flops=flops, bytes_accessed=moved if flops else 0, transcendentals=0
        ),
        name=name,
    )(place, *args)


def weight_pieces_kernel(place, q, k, v, o, e, c, qkv_out, rest_out, turned):
    span = o.shape[0]
    at = pl.multiple_of(place[1] * span, span)
    for which, ref in enumerate((q, k, v)):
        turned[...] = ref[...].T
        qkv_out[which * span : (which + 1) * span, :] = turned[pl.ds(at, span), :].astype(bf16)
    hid = e.shape[0]
    rest_out[:span, :] = o[...].astype(bf16)
    rest_out[span : span + hid, :] = e[...].astype(bf16)
    rest_out[span + hid :, :] = c[...].astype(bf16)


def buffer_pieces_kernel(place, q, k, v, o, e, c, att_out, ffn_out, turned):
    span = o.shape[0]
    at = pl.multiple_of(place[1] * span, span)
    for which, ref in enumerate((q, k, v)):
        turned[...] = ref[...].T
        att_out[which] = 0.5 * turned[pl.ds(at, span), :]
    att_out[3] = 0.5 * o[...]
    ffn_out[0] = 0.5 * c[...]
    ffn_out[1] = 0.5 * e[...]


def pieces(kernel, place, arrays, outs, name):
    q, k, v, o, e, c = arrays
    spots = lax.axis_size("dp")
    span, hid = o.shape[0] // spots, e.shape[0] // spots
    row = lambda size: pl.BlockSpec((size, D), lambda g, place: (place[1], 0))
    return run(
        kernel,
        place,
        arrays,
        outs,
        name,
        in_specs=[whole, whole, whole, row(span), row(hid), row(hid)],
        spare=56,
        scratch=[pltpu.VMEM((q.shape[1], D), f32)],
    )


def split_positions_kernel(place, *refs):
    count = len(refs) // 2
    for u in range(count):
        refs[count + u][...] = refs[u][0].astype(bf16)


def split_positions(x, place):
    planes, span, width = x.shape
    block = lambda u: pl.BlockSpec((1, span, width), lambda g, place: (place[0] ^ u, 0, 0))
    return run(
        split_positions_kernel,
        place,
        [x] * planes,
        [like((span, width), bf16)] * planes,
        "split_positions",
        in_specs=[block(u) for u in range(planes)],
    )


def join_positions_kernel(place, *refs):
    out = refs[-1]
    for u, ref in enumerate(refs[:-1]):
        out[place[0] ^ u] = ref[...].astype(f32)


def join_positions(parts, place):
    span, width = parts[0].shape
    return run(
        join_positions_kernel,
        place,
        parts,
        [like((len(parts), span, width), f32)],
        "join_positions",
    )[0]


def window(first_row):
    return max(0, first_row + 1 - max_doc) // 128 * 128


def pair_weights(own, other, span):
    parts = []
    for which in range(3):
        for m in range(own.shape[0]):
            for half in (own, other):
                parts.append(half[m, 0, which * span : (which + 1) * span, :])
    return jnp.concatenate(parts, 0)


def interleave(own, other):
    return [half for pair in zip(own, other) for half in pair]


def in_lanes(low, high, x, rest):
    lane = lax.broadcasted_iota(jnp.int32, x.shape, 1)
    return jnp.where((lane >= low) & (lane < high), x, rest)


def spare_lanes(half, values, like_x):
    lane = lax.broadcasted_iota(jnp.int32, like_x.shape, 1)
    first = HEAD_DIM * (1 - half)
    out = jnp.zeros_like(like_x)
    for at, value in enumerate(values):
        out = jnp.where(lane == first + at, value, out)
    return out


def head_lanes(half, x, values=()):
    return in_lanes(HEAD_DIM * half, HEAD_DIM * (half + 1), x, spare_lanes(half, values, x))


def two_parts(x):
    high = x.astype(bf16)
    return high, (x - high.astype(f32)).astype(bf16)


def forward_kernel(place, last_ref, in_ref, *refs):
    own, other, x_ref, o_ref, bias_ref, q_ref, v_ref = refs
    length = in_ref.shape[1]
    span = own.shape[2] // 3
    blocks = [(first, window(first), first + q_rows) for first in range(0, length, q_rows)]

    @pl.when(pl.program_id(0) == 0)
    def _():
        for first, low, high in blocks:
            row = first + lax.broadcasted_iota(jnp.int32, (q_rows, high - low), 0)
            col = low + lax.broadcasted_iota(jnp.int32, (q_rows, high - low), 1)
            allowed = (col <= row) & (row <= last_ref[:, low:high])
            bias_ref[first:high, : high - low] = jnp.where(allowed, 0.0, mask_fill)

    weight = pair_weights(own, other, span)
    rows = mm(in_ref[0], weight, nt).astype(bf16)
    query = rows[:, :128] * jnp.asarray(HEAD_DIM**-0.5, bf16)
    x_ref[0, 2] = rows[:, 128:256]
    x_ref[0, 3] = rows[:, 256:]
    one = jnp.asarray(1, bf16)
    for half in range(2):
        q_ref[half] = head_lanes(half, query)
        v_ref[half] = head_lanes(half, rows[:, 256:], (one,))
    for first, low, high in blocks:
        found = []
        for half in range(2):
            spare = HEAD_DIM * (1 - half)
            scores = mm(q_ref[half, first:high, :], x_ref[0, 2, low:high, :], nt)
            scores = scores + bias_ref[first:high, : high - low]
            peak = jnp.max(scores, axis=1, keepdims=True)
            weight = jnp.exp(scores - peak).astype(bf16)
            out = mm(weight, v_ref[half, low:high, :], nn)
            total = out[:, spare : spare + 1]
            found.append(out * (1.0 / total))
            parts = two_parts(-(peak + jnp.log(total)))
            x_ref[0, half, first:high, :] = head_lanes(half, q_ref[half, first:high, :], parts)
        o_ref[first:high, :] = in_lanes(0, HEAD_DIM, found[0], found[1]).astype(bf16)


def attention(place, last, inputs, halves):
    length = inputs.shape[1]
    chips, planes, rows, _ = halves[0].shape
    half = pl.BlockSpec((chips, 1, rows, D), lambda h, place: (0, h, 0, 0))
    return run(
        forward_kernel,
        place,
        [last, inputs, *halves],
        [like((planes, 4, length, 128), bf16), like((length, D), bf16)],
        "attention_forward",
        spare=56,
        grid=(planes,),
        in_specs=[whole, pl.BlockSpec((1, length, D), lambda h, place: (place[0], 0, 0))]
        + [half] * len(halves),
        out_specs=[
            pl.BlockSpec((1, 4, length, 128), lambda h, place: (h, 0, 0, 0)),
            pl.BlockSpec((length, 128), lambda h, place: (0, h)),
        ],
        scratch=[
            pltpu.VMEM((length, 768), f32),
            pltpu.VMEM((2, length, 128), bf16),
            pltpu.VMEM((2, length, 128), bf16),
        ],
        flops=8 * length * D * D + 2 * length * 768 * 512 * planes,
    )


def backward_kernel(
    is_last, spots, place, start_ref, in_hbm, x_ref, g_ref, o_ref, gout_ref, gmid_hbm, *rest
):
    own, other, rest = rest[0], rest[1], rest[2:]
    ins, rest = rest[:-12], rest[-12:]
    keep_ref, give_ref, dk_ref, dv_ref, dq_ref, acc_ref, bias_ref, k_ref, v_ref, gs_ref = rest[:10]
    in_ref, sems = rest[10:]
    length = in_ref.shape[0]
    load_acc = pltpu.make_async_copy(gmid_hbm, acc_ref, sems.at[0])
    load_in = pltpu.make_async_copy(in_hbm.at[place[0]], in_ref, sems.at[1])
    span = own.shape[2] // 3
    chips = spots // 2
    step = pl.program_id(0)
    blocks = [(first, window(first), first + q_rows) for first in range(0, length, q_rows)]

    @pl.when(step == 0)
    def _():
        load_acc.start()
        load_in.start()
        for first, low, high in blocks:
            col = low + lax.broadcasted_iota(jnp.int32, (high - low, q_rows), 0)
            row = first + lax.broadcasted_iota(jnp.int32, (high - low, q_rows), 1)
            allowed = (col <= row) & (col >= start_ref[:, first:high])
            bias_ref[: high - low, first:high] = jnp.where(allowed, 0.0, mask_fill)

    dk_ref[...] = jnp.zeros_like(dk_ref)
    dv_ref[...] = jnp.zeros_like(dv_ref)
    one = jnp.asarray(1, bf16)
    product = g_ref[...].astype(f32) * o_ref[...].astype(f32)
    for half in range(2):
        k_ref[half] = head_lanes(half, x_ref[0, 2], (one, one))
        v_ref[half] = head_lanes(half, x_ref[0, 3], (one, one))
        delta = jnp.sum(head_lanes(half, product), axis=1, keepdims=True)
        gs_ref[half] = head_lanes(half, g_ref[...], two_parts(-delta))
    for first, low, high in blocks:
        q_both = jnp.concatenate([head_lanes(half, x_ref[0, half, first:high, :]) for half in range(2)], 0)
        g_both = jnp.concatenate([head_lanes(half, g_ref[first:high, :]) for half in range(2)], 0)
        dq = jnp.zeros((q_rows, 128), f32)
        for at in range(low, high, q_rows):
            keys = slice(at, at + q_rows)
            bias = bias_ref[at - low : at - low + q_rows, first:high]
            probs, g_scores = [], []
            for half in range(2):
                scores = mm(k_ref[half, keys, :], x_ref[0, half, first:high, :], nt) + bias
                weight = jnp.exp(scores)
                g_probs = mm(v_ref[half, keys, :], gs_ref[half, first:high, :], nt)
                probs.append(weight.astype(bf16))
                g_scores.append((weight * g_probs).astype(bf16))
            k_both = jnp.concatenate([head_lanes(half, x_ref[0, 2, keys, :]) for half in range(2)], 0)
            dq = dq + mm(jnp.concatenate(g_scores, 0), k_both, tn)
            dv_ref[keys, :] += mm(jnp.concatenate(probs, 1), g_both, nn)
            dk_ref[keys, :] += mm(jnp.concatenate(g_scores, 1), q_both, nn)
        dq_ref[first:high, :] = (dq * HEAD_DIM**-0.5).astype(bf16)
    grads = (dq_ref[...], dk_ref[...].astype(bf16), dv_ref[...].astype(bf16))
    grads = jnp.concatenate(grads, 1)
    weight = pair_weights(own, other, span)

    @pl.when(step == 0)
    def _():
        load_acc.wait()
        load_in.wait()

    acc_ref[...] += mm(grads, weight, nn)
    all_rows = mm(grads, in_ref[...], tn).astype(bf16)
    for which in range(4):
        if which < 3:
            rows = all_rows[which * 128 : (which + 1) * 128, :]
        else:
            rows = gout_ref[...]
        for m in range(chips):
            for c, ref in enumerate((keep_ref, give_ref)):
                at = (2 * m + c) * span
                ref[m, 0, which * span : (which + 1) * span, :] = rows[at : at + span, :]

    @pl.when(step == pl.num_programs(0) - 1)
    def _():
        if not is_last:
            save = pltpu.make_async_copy(acc_ref, ins[0], sems.at[0])
            save.start()
            save.wait()
            return
        rows = ins[0].shape[0]
        for u, ref in enumerate(ins):
            at = pl.multiple_of((place[0] ^ u) * rows, rows)
            ref[...] = acc_ref[pl.ds(at, rows), :].astype(bf16)


def attention_back(
    place, start, inputs, halves, qkv, heads_grad, heads, grad_output, so_far, first, count, is_last
):
    length = inputs.shape[1]
    chips, planes, rows, _ = halves[0].shape
    spots = 2 * chips
    span = rows // 3
    half = pl.BlockSpec((chips, 1, rows, D), lambda h, place: (0, first + h, 0, 0))
    out_half = pl.BlockSpec((chips, 1, 4 * span, D), lambda h, place: (0, h, 0, 0))
    outs = [like((length // planes, D), bf16)] * planes if is_last else [like((length, D), f32)]
    out = run(
        functools.partial(backward_kernel, is_last, spots),
        place,
        [start, inputs, qkv, heads_grad, heads, grad_output, so_far, *halves],
        outs + [like((chips, count, 4 * span, D), bf16)] * 2,
        "attention_backward",
        spare=56,
        grid=(count,),
        in_specs=[
            whole,
            hbm,
            pl.BlockSpec((1, 4, length, 128), lambda h, place: (first + h, 0, 0, 0)),
            pl.BlockSpec((length, 128), lambda h, place: (0, first + h)),
            pl.BlockSpec((length, 128), lambda h, place: (0, first + h)),
            pl.BlockSpec((128, D), lambda h, place: (first + h, 0)),
            hbm,
        ]
        + [half] * 2,
        out_specs=([whole] * planes if is_last else [hbm]) + [out_half] * 2,
        scratch=[
            pltpu.VMEM((length, 128), f32),
            pltpu.VMEM((length, 128), f32),
            pltpu.VMEM((length, 128), bf16),
            pltpu.VMEM((length, D), f32),
            pltpu.VMEM((768, length), f32),
            pltpu.VMEM((2, length, 128), bf16),
            pltpu.VMEM((2, length, 128), bf16),
            pltpu.VMEM((2, length, 128), bf16),
            pltpu.VMEM((length, D), bf16),
            pltpu.SemaphoreType.DMA((2,)),
        ],
        flops=(12 * length * D * D + 5 * length * 768 * 512 * planes) * count // planes,
    )
    return out[:-2], out[-2], out[-1]


def ffn_kernel(planes, spots, per, place, *refs):
    alphas, in_hbm, heads_hbm = refs[:3]
    ups = refs[3 : 3 + planes]
    halves = refs[3 + planes : 3 + planes + spots]
    bias_ref, bout_ref = refs[3 + planes + spots : 5 + planes + spots]
    outs = refs[5 + planes + spots :]
    lays = outs[:planes]
    keep_ref, give_ref, gout_ref, gheads_hbm, gmid_hbm, gbin_ref, gbout_ref, galpha_ref = outs[
        planes : planes + 8
    ]
    (
        attended, middle, mid_low, g_low, up, branch, o_low, lay, weights, in_ref, heads_ref,
        o_parts, gmid_ref, gheads_ref, sems, w_sems, out_sems,
    ) = outs[planes + 8 :]
    chips = spots // 2
    length = in_ref.shape[0]
    block = length // planes
    hid = keep_ref.shape[2] // planes
    span = halves[0].shape[1] - 2 * hid
    step = pl.program_id(0)
    steps = pl.num_programs(0)
    alpha_att, alpha_ffn = alphas[0], alphas[1]
    size = 512
    tiles = [slice(at, at + size) for at in range(0, length, size)]

    def order(at):
        return 2 * (at % chips) + at // chips

    def weight_copy(at):
        return pltpu.make_async_copy(
            halves[order(at)].at[:, span:, :], weights.at[at], w_sems.at[at]
        )

    @pl.when(step == 0)
    def _():
        first = [
            pltpu.make_async_copy(half.at[:, :span, :], o_parts.at[at], sems.at[at])
            for at, half in enumerate(halves)
        ]
        first.append(pltpu.make_async_copy(heads_hbm, heads_ref, sems.at[spots]))
        first.append(pltpu.make_async_copy(in_hbm.at[place[0]], in_ref, sems.at[spots + 1]))
        for u in range(planes):
            at = pl.multiple_of((place[0] ^ u) * block, block)
            first.append(
                pltpu.make_async_copy(ups[u], up.at[pl.ds(at, block), :], sems.at[spots + 2 + u])
            )
        for copy in first:
            copy.start()
        for at in range(spots):
            weight_copy(at).start()
        for copy in first:
            copy.wait()
        for k in range(planes):
            for at in range(spots):
                row = (k * spots + at) * span
                o_low[row : row + span, :] = o_parts[at, k]
        total = jnp.zeros((1, D), f32)
        for t in tiles:
            found = mm(heads_ref[t, :], o_low[...], nn)
            attended[t, :] = found
            mid = in_ref[t, :].astype(f32) + alpha_att * found
            middle[t, :] = mid
            mid_low[t, :] = mid.astype(bf16)
            upstream = up[t, :].astype(f32)
            grad = (alpha_ffn * upstream).astype(bf16)
            g_low[t, :] = grad
            total = total + jnp.sum(grad.astype(f32), axis=0, keepdims=True)
            branch[t, :] = jnp.zeros((size, D), f32)
            gmid_ref[t, :] = upstream
        gbout_ref[...] = total

    for at in range(spots):

        @pl.when(step == at // per)
        def _():
            weight_copy(at).wait()

    rows = [weights[step * per + g] for g in range(per)]
    expand = jnp.concatenate([row[:, :hid, :].reshape(planes * hid, D) for row in rows], 0)
    contract = jnp.concatenate([row[:, hid:, :].reshape(planes * hid, D) for row in rows], 0)
    bias = bias_ref[0]
    gc = jnp.zeros((per * planes * hid, D), f32)
    ge = jnp.zeros((per * planes * hid, D), f32)
    gb = jnp.zeros((1, per * planes * hid), f32)
    for t in tiles:
        mid = mid_low[t, :]
        grad = g_low[t, :]
        pre = mm(mid, expand, nt) + bias
        square = pre * pre
        tanh = jnp.tanh(gelu_root * pre * (1.0 + gelu_cube * square))
        half = 0.5 * (1.0 + tanh)
        hidden = (pre * half).astype(bf16)
        slope = half + (0.5 * gelu_root) * pre * (1.0 - tanh * tanh) * (
            1.0 + (3.0 * gelu_cube) * square
        )
        branch[t, :] += mm(hidden, contract, nn)
        g_pre = (mm(grad, contract, nt) * slope).astype(bf16)
        gmid_ref[t, :] += mm(g_pre, expand, nn)
        gc = gc + mm(hidden, grad, tn)
        ge = ge + mm(g_pre, mid, tn)
        gb = gb + jnp.sum(g_pre.astype(f32), axis=0, keepdims=True)
    gc = gc.astype(bf16)
    ge = ge.astype(bf16)
    group = planes * hid

    def store(ref):
        for g in range(per):
            ref[g, 0] = gc[g * group : (g + 1) * group, :]
            ref[g, 1] = ge[g * group : (g + 1) * group, :]

    pl.when(step < steps // 2)(lambda: store(keep_ref))
    pl.when(step >= steps // 2)(lambda: store(give_ref))
    gbin_ref[0] = gb

    @pl.when(step == steps - 1)
    def _():
        sum_ffn = jnp.zeros((1, D), f32)
        sum_att = jnp.zeros((1, D), f32)
        gout = jnp.zeros((D, D), f32)
        copies = []
        for at, t in enumerate(tiles):
            gm = gmid_ref[t, :]
            copies.append(
                pltpu.make_async_copy(gmid_ref.at[t, :], gmid_hbm.at[t, :], out_sems.at[0, at])
            )
            copies[-1].start()
            g_att = (alpha_att * gm).astype(bf16)
            gheads_ref[t, :] = mm(g_att, o_low[...], nt).astype(bf16)
            copies.append(
                pltpu.make_async_copy(gheads_ref.at[t, :], gheads_hbm.at[t, :], out_sems.at[1, at])
            )
            copies[-1].start()
            gout = gout + mm(heads_ref[t, :], g_att, tn)
            sum_att = sum_att + jnp.sum(gm * attended[t, :], axis=0, keepdims=True)
            final = branch[t, :] + bout_ref[...]
            lay[t, :] = middle[t, :] + alpha_ffn * final
            sum_ffn = sum_ffn + jnp.sum(up[t, :].astype(f32) * final, axis=0, keepdims=True)
        gout_ref[...] = gout.astype(bf16)
        galpha_ref[0:1, :] = sum_att
        galpha_ref[1:2, :] = sum_ffn
        for u, ref in enumerate(lays):
            at = pl.multiple_of((place[0] ^ u) * block, block)
            ref[...] = lay[pl.ds(at, block), :].astype(bf16)
        for copy in copies:
            copy.wait()


def feed_forward(place, alphas, inputs, heads, ups, halves, bias, bout):
    length = inputs.shape[1]
    planes = len(ups)
    spots = len(halves)
    chips = spots // 2
    span, hid = heads.shape[1] // (planes * spots), bias.shape[-1] // planes
    per = 2 if chips % 2 == 0 else 1
    steps = spots // per
    bias = bias.reshape(steps, 1, per * planes * hid)
    tiles = length // 512
    group = planes * hid
    out = run(
        functools.partial(ffn_kernel, planes, spots, per),
        place,
        [alphas, inputs, heads, *ups, *halves, bias, bout],
        [like((length // planes, D), bf16)] * planes
        + [
            like((chips, 2, group, D), bf16),
            like((chips, 2, group, D), bf16),
            like((D, D), bf16),
            like((length, D), bf16),
            like((length, D), f32),
            like((steps, 1, per * group), f32),
            like((1, D), f32),
            like((2, D), f32),
        ],
        "feed_forward",
        spare=56,
        grid=(steps,),
        in_specs=[pl.BlockSpec(memory_space=pltpu.SMEM)]
        + [hbm] * (2 + planes + spots)
        + [pl.BlockSpec((1, 1, per * group), lambda t, place: (t, 0, 0)), whole],
        out_specs=[whole] * planes
        + [
            pl.BlockSpec(
                (per, 2, group, D), lambda t, place: (jnp.minimum(t, steps // 2 - 1), 0, 0, 0)
            ),
            pl.BlockSpec(
                (per, 2, group, D), lambda t, place: (jnp.maximum(t - steps // 2, 0), 0, 0, 0)
            ),
            whole,
            hbm,
            hbm,
            pl.BlockSpec((1, 1, per * group), lambda t, place: (t, 0, 0)),
            whole,
            whole,
        ],
        scratch=[
            pltpu.VMEM((length, D), f32),
            pltpu.VMEM((length, D), f32),
            pltpu.VMEM((length, D), bf16),
            pltpu.VMEM((length, D), bf16),
            pltpu.VMEM((length, D), bf16),
            pltpu.VMEM((length, D), f32),
            pltpu.VMEM((D, D), bf16),
            pltpu.VMEM((length, D), f32),
            pltpu.VMEM((spots, planes, 2 * hid, D), bf16),
            pltpu.VMEM((length, D), bf16),
            pltpu.VMEM((length, D), bf16),
            pltpu.VMEM((spots, planes, span, D), bf16),
            pltpu.VMEM((length, D), f32),
            pltpu.VMEM((length, D), bf16),
            pltpu.SemaphoreType.DMA((spots + 2 + planes,)),
            pltpu.SemaphoreType.DMA((spots,)),
            pltpu.SemaphoreType.DMA((2, tiles)),
        ],
        flops=12 * length * D * 2 * chips * group,
    )
    return out[:planes], out[planes:]


def att_core_kernel(place, keep, got, *outs):
    rows = keep.shape[2]
    for m, out in enumerate(outs):
        for k in range(keep.shape[1]):
            total = keep[m, k].astype(f32) + got[m, k].astype(f32)
            out[k * rows : (k + 1) * rows, :] = total.astype(bf16)


def small_write(out, total):
    at = out.shape[0] - 2 * total.shape[0]
    high = total.astype(bf16)
    out[at : at + total.shape[0], :] = high
    out[at + total.shape[0] :, :] = (total - high.astype(f32)).astype(bf16)


def small_read(ref):
    rows = ref.shape[0]
    return ref[rows - 16 : rows - 8, :].astype(f32) + ref[rows - 8 :, :].astype(f32)


def ffn_core_kernel(place, own, got, small, *outs):
    rows = own.shape[0] // len(outs)
    total = small[...]
    for at, out in enumerate(outs):
        for r in range(0, rows, 256):
            a = own[at * rows + r : at * rows + r + 256, :].astype(f32)
            b = got[at * rows + r : at * rows + r + 256, :].astype(f32)
            out[r : r + 256, :] = (a + b).astype(bf16)
        small_write(out, total)


def ffn_chip_kernel(chips, planes, place, old, *refs):
    ins, give, keep, both = refs[:chips], refs[-3], refs[-2], refs[-1]
    hid = old.shape[1]
    rows = planes * hid
    small = small_read(ins[0])
    for ref in ins[1:]:
        small = small + small_read(ref)
    for which in range(2):
        for k in range(planes):
            at = which * rows + k * hid
            total = ins[0][at : at + hid, :].astype(f32)
            for ref in ins[1:]:
                total = total + ref[at : at + hid, :].astype(f32)
            if k == 0:
                total = total + old[which]
            both[which, k * hid : (k + 1) * hid, :] = total.astype(bf16)
    mine = place[0] // (planes // 2)
    keep[:rows, :] = both[mine]
    give[:rows, :] = both[1 - mine]
    small_write(keep, small)
    small_write(give, small)


def plane_sum_kernel(mask, planes, place, keep, got, out):
    rows = keep.shape[0] - 16
    hid = rows // planes
    for k in range(planes):
        at, by = k * hid, (k ^ mask) * hid
        total = keep[at : at + hid, :].astype(f32) + got[by : by + hid, :].astype(f32)
        out[at : at + hid, :] = total.astype(bf16)
    small_write(out, small_read(keep) + small_read(got))


def att_to_owner_kernel(chips, planes, place, *refs):
    ins, old, outs, scratch = refs[:chips], refs[chips], refs[chips + 1 : -1], refs[-1]
    span = old.shape[1]
    for k in range(planes):
        for which in range(4):
            at = (k * 4 + which) * span
            total = ins[0][at : at + span, :].astype(f32)
            for ref in ins[1:]:
                total = total + ref[at : at + span, :].astype(f32)
            if k == 0:
                total = total + old[which]
            scratch[which, k * span : (k + 1) * span, :] = total.astype(bf16)
    for u, out in enumerate(outs):
        out[...] = scratch[place[0] ^ u]


def near_sum_kernel(planes, place, keep, got, *refs):
    ins, (out, small_out) = refs[:planes], refs[planes:]
    rows = keep.shape[0] - 16
    hid = rows // planes
    span = ins[0].shape[0] // planes
    for k in range(planes):
        at, by = k * hid, (k ^ 1) * hid
        total = keep[at : at + hid, :].astype(f32) + got[by : by + hid, :].astype(f32)
        out[at : at + hid, :] = total.astype(bf16)
        total = jnp.zeros((span, D), f32)
        for u, ref in enumerate(ins):
            at = (k ^ u) * span
            total = total + ref[at : at + span, :].astype(f32)
        out[rows + k * span : rows + (k + 1) * span, :] = total.astype(bf16)
    small_out[...] = small_read(keep) + small_read(got)


def newton_kernel(planes, chips, base_row, groups, with_rows, place, own, other, *refs):
    outs, x_ref, low_ref = refs[:-2], refs[-2], refs[-1]
    dim, cols = x_ref.shape
    group = cols // planes
    half_group = group // 2
    span = half_group // chips
    tall = own.shape[0] // chips
    chunk = 512
    total = jnp.zeros((1, D), f32)
    for half in (own, other):
        for m in range(chips):
            at = m * tall + base_row
            part = half[at : at + planes * span, :].astype(f32)
            total = total + jnp.sum(part * part, axis=0, keepdims=True)
    inverse = 1.0 / (jnp.sqrt(jnp.sum(total, axis=1, keepdims=True)) + 1e-07)
    for k in range(planes):
        rows = []
        for half in (own, other):
            for m in range(chips):
                at = m * tall + base_row + k * span
                rows.append(half[at : at + span, :])
        part = jnp.concatenate(rows, 0).astype(f32).T * inverse
        x_ref[:, k * group : (k + 1) * group] = part
        low_ref[:, k * group : (k + 1) * group] = part.astype(bf16)
    diagonal = lax.broadcasted_iota(jnp.int32, (dim, dim), 0) == lax.broadcasted_iota(
        jnp.int32, (dim, dim), 1
    )

    def step(spans):
        gram = jnp.zeros((dim, dim), f32)
        for at in range(0, cols, chunk):
            part = low_ref[:, at : at + chunk]
            gram = gram + mm(part, part, nt)
        trace = jnp.sum(
            jnp.sum(jnp.where(diagonal, gram, 0.0), axis=0, keepdims=True), axis=1, keepdims=True
        )
        shift = trace * (1.0 / dim)
        rest = jnp.where(diagonal, gram - shift, gram)
        rest_low = rest.astype(bf16)
        poly = (newton_two + 2.0 * newton_three * shift) * rest + newton_three * mm(
            rest_low, rest_low, nn
        )
        poly = poly.astype(bf16)
        scale = newton_one + newton_two * shift + newton_three * shift * shift
        for part in spans:
            new = scale * x_ref[:, part] + mm(poly, low_ref[:, part], nn)
            x_ref[:, part] = new
            low_ref[:, part] = new.astype(bf16)

    everything = [slice(at, at + chunk) for at in range(0, cols, chunk)]
    for _ in range(4):
        step(everything)
    if with_rows:
        step(everything)
    else:
        step([slice(k * group, k * group + half_group) for k in groups])
    for k, out in zip(groups, outs):
        part = x_ref[:, k * group : (k + 1) * group].T.astype(bf16)
        base = half_group if with_rows else 0
        for m in range(chips):
            chip = place[1] // 2 ^ m
            if with_rows:
                at = m * tall + base_row + k * span
                out[pl.ds(pl.multiple_of(chip * span, span), span), :] = own[at : at + span, :]
            to = pl.multiple_of(base + chip * span, span)
            out[pl.ds(to, span), :] = part[m * span : (m + 1) * span, :]


def newton(place, own, other, planes, base_row, cols, groups, with_rows, name):
    rows = cols // planes // 2 * (2 if with_rows else 1)
    return run(
        functools.partial(
            newton_kernel, planes, lax.axis_size("dp") // 2, base_row, groups, with_rows
        ),
        place,
        [own, other],
        [like((rows, D), bf16)] * len(groups),
        name,
        scratch=[pltpu.VMEM((D, cols), f32), pltpu.VMEM((D, cols), bf16)],
        flops=10 * D * D * (2 * cols + D),
    )


def momentum_rows_kernel(planes, chips, group, place, own, out):
    span = out.shape[0] // chips
    for m in range(chips):
        to = pl.multiple_of((place[1] // 2 ^ m) * span, span)
        at = m * (own.shape[0] // chips) + group * span
        out[pl.ds(to, span), :] = own[at : at + span, :]


def att_final_kernel(planes, span, place, mine, got, *refs):
    old, outs, rows = refs[:4], refs[4:-1], refs[-1]
    half = mine.shape[1] // 2
    core = place[1] % 2
    for which in range(4):
        slot = place[0] ^ which
        for kind in range(2):
            for at in range(0, half, span):
                from_at = kind * half + at
                rows[pl.ds(pl.multiple_of(2 * at + core * span, span), span), :] = mine[
                    slot, from_at : from_at + span, :
                ]
                rows[pl.ds(pl.multiple_of(2 * at + (1 - core) * span, span), span), :] = got[
                    slot, from_at : from_at + span, :
                ]
            part = rows[...].astype(f32)
            part = part.T if which < 3 else part
            if kind == 0:
                outs[which][...] = part
            else:
                outs[4 + which][...] = old[which][...] - muon_rates[which] * part


def ffn_buffers_kernel(planes, chips, place, own, other, far, far_got, eo, co):
    span = far.shape[0] // chips
    core = place[1] % 2

    def fill(mine_out, far_out):
        for m in range(chips):
            chip = place[1] // 2 ^ m
            here = pl.multiple_of((2 * chip + core) * span, span)
            there = pl.multiple_of((2 * chip + 1 - core) * span, span)
            at = m * (own.shape[0] // chips)
            mine_out[pl.ds(here, span), :] = own[at : at + span, :].astype(f32)
            mine_out[pl.ds(there, span), :] = other[at : at + span, :].astype(f32)
            at = m * span
            here = pl.multiple_of((2 * m + core) * span, span)
            there = pl.multiple_of((2 * m + 1 - core) * span, span)
            far_out[pl.ds(here, span), :] = far[at : at + span, :].astype(f32)
            far_out[pl.ds(there, span), :] = got[at : at + span, :].astype(f32)

    got = far_got
    pl.when(place[0] < planes // 2)(lambda: fill(co, eo))
    pl.when(place[0] >= planes // 2)(lambda: fill(eo, co))


def ffn_final_kernel(planes, chips, place, mine, far, got, we, wc, eo, co):
    rows = mine.shape[0]
    span = rows // chips
    core = place[1] % 2

    def fill(mine_out, mine_w, mine_rate, far_out, far_w, far_rate):
        for m in range(chips):
            at = slice(m * span, (m + 1) * span)
            far_at = slice(rows + m * span, rows + (m + 1) * span)
            here = pl.ds(pl.multiple_of((2 * m + core) * span, span), span)
            there = pl.ds(pl.multiple_of((2 * m + 1 - core) * span, span), span)
            mine_out[here, :] = mine_w[here, :] - mine_rate * mine[at, :].astype(f32)
            mine_out[there, :] = mine_w[there, :] - mine_rate * got[at, :].astype(f32)
            far_out[here, :] = far_w[here, :] - far_rate * far[at, :].astype(f32)
            far_out[there, :] = far_w[there, :] - far_rate * got[far_at, :].astype(f32)

    expand, contract = (eo, we, muon_rates[4]), (co, wc, muon_rates[5])
    pl.when(place[0] < planes // 2)(lambda: fill(*contract, *expand))
    pl.when(place[0] >= planes // 2)(lambda: fill(*expand, *contract))


def shards(
    layer_in,
    doc_ids,
    out_grad,
    w_query,
    w_key,
    w_value,
    w_output,
    w_expand,
    w_contract,
    small_params,
    buffer_query,
    buffer_key,
    buffer_value,
    buffer_output,
    buffer_expand,
    buffer_contract,
    small_first,
    small_second,
):
    planes = lax.axis_size("mp")
    spots = lax.axis_size("dp")
    chips = spots // 2
    plane = lax.axis_index("mp")
    spot = lax.axis_index("dp")
    place = jnp.stack([plane, spot]).astype(jnp.int32)
    length = layer_in.shape[1]
    head_cols = w_query.shape[1]
    hidden_rows = w_expand.shape[0]
    span = head_cols // spots
    hid = hidden_rows // spots
    to_planes = range(1, planes)
    to_chips = range(1, chips)
    weights_old = (w_query, w_key, w_value, w_output, w_expand, w_contract)
    buffers_old = (
        buffer_query,
        buffer_key,
        buffer_value,
        buffer_output,
        buffer_expand,
        buffer_contract,
    )

    def around_planes(x):
        return [x] + [swap(x, "mp", k) for k in to_planes]

    def around_chips(x):
        return [x] + [swap(x, "dp", 2 * m) for m in to_chips]

    def together(*groups):
        return lax.optimization_barrier(groups)

    def together(*groups):
        return lax.optimization_barrier(groups)

    qkv_piece, rest_piece = pieces(
        weight_pieces_kernel,
        place,
        weights_old,
        [like((3 * span, D), bf16), like((span + 2 * hid, D), bf16)],
        "weight_pieces",
    )
    inputs = layer_in
    documents = pick(doc_ids, plane)
    last = (
        jnp.sum(documents[None, :] <= documents[:, None], axis=1, dtype=jnp.int32)[None, :] - 1
    )
    start = jnp.sum(documents[None, :] < documents[:, None], axis=1, dtype=jnp.int32)[None, :]

    def to_slots(bias):
        return reorder(reorder(bias, plane, 0), spot, 1)

    bias = to_slots(small_params[:FF].reshape(planes, spots, hid))
    bias = bias.reshape(planes, chips, 2, hid).transpose(2, 1, 0, 3)
    bias = bias.reshape(2, chips, 1, planes * hid)
    bout = small_params[FF : FF + D].reshape(1, D)
    alphas = small_params[FF + D :]
    token_span = length // planes
    ups = split_positions(out_grad, place)

    qkv_own, ups = together(around_planes(qkv_piece), ups)
    qkv_own = around_chips(jnp.stack(qkv_own))
    rest_own = around_planes(rest_piece)
    qkv_own, rest_own, last, start, bias = together(
        qkv_own, rest_own, last, start, bias
    )
    qkv_own = jnp.stack(qkv_own)
    qkv_halves = [qkv_own, swap(qkv_own, "dp", 1)]
    rest_own, ups = together(jnp.stack(rest_own), ups)
    rest_own = around_chips(rest_own)
    up_near = ups[1]
    ups = [ups[0], None] + [swap(ups[u], "mp", u) for u in to_planes[1:]]
    qkv, heads = attention(place, last, inputs, qkv_halves)
    heads, up_near, buffers_old = together(heads, up_near, buffers_old)
    ups[1] = swap(up_near, "mp", 1)
    att_old, ffn_old = pieces(
        buffer_pieces_kernel,
        place,
        buffers_old,
        [like((4, span, D), f32), like((2, hid, D), f32)],
        "buffer_pieces",
    )
    heads, rest_own, ups, att_old, ffn_old = together(heads, rest_own, ups, att_old, ffn_old)
    rest_halves = interleave(rest_own, [swap(part, "dp", 1) for part in rest_own])
    lays, rest = feed_forward(place, alphas, inputs, heads, ups, rest_halves, bias, bout)
    ffn_keep, ffn_give, grad_output, heads_grad, middle_grad, gb_in, gb_out, g_alpha = rest

    ffn_rows = (chips * 2 * planes * hid, D)
    ffn_got = swap(ffn_give.reshape(ffn_rows), "dp", 1)
    gb_in = gb_in.reshape(2, chips, planes, hid).transpose(2, 1, 0, 3).reshape(planes, spots, hid)
    small = jnp.concatenate(
        [to_slots(gb_in).reshape(-1), gb_out.reshape(-1), jnp.sum(g_alpha, axis=1)]
    )
    small = jnp.pad(small, (0, 8 * D - small.size)).reshape(8, D)
    high = lax.reduce_precision(small, 8, 7)
    pair = jnp.concatenate([high, lax.reduce_precision(small - high, 8, 7)]).astype(bf16)
    pair = swap(pair, "dp", 1).astype(f32)
    small = small + pair[:8] + pair[8:]
    parts = run(
        ffn_core_kernel,
        place,
        [ffn_keep.reshape(ffn_rows), ffn_got, small],
        [like((2 * planes * hid + 16, D), bf16)] * chips,
        "ffn_core_sum",
    )
    middle_grad, parts = together(middle_grad, parts)
    got = [parts[0]] + [swap(parts[m], "dp", 2 * m) for m in to_chips]
    lay_far = [swap(lays[u], "mp", u) for u in to_planes[1:]]
    ins, att_keep, att_give = attention_back(
        place, start, inputs, qkv_halves, qkv, heads_grad, heads, grad_output, middle_grad,
        0, planes, True,
    )
    ins, att_keep, att_give, got, lay_far = together(ins, att_keep, att_give, got, lay_far)

    far = planes // 2
    parts = got
    rows = planes * hid
    give, keep = run(
        functools.partial(ffn_chip_kernel, chips, planes),
        place,
        [ffn_old, *parts],
        [like((rows + 16, D), bf16)] * 2,
        "ffn_chip_sum",
        scratch=[pltpu.VMEM((2, rows, D), bf16)],
    )
    give, att_give, lays = together(give, att_give, lays)
    got = swap(give, "mp", far)
    lay_near = swap(lays[1], "mp", 1)
    att_got = swap(att_give, "dp", 1)
    att_parts = run(
        att_core_kernel,
        place,
        [att_keep, att_got],
        [like((planes * 4 * span, D), bf16)] * chips,
        "att_core_sum",
    )
    att_got = [att_parts[0]] + [swap(att_parts[m], "dp", 2 * m) for m in to_chips]
    got, att_got, lay_near = together(got, att_got, lay_near)
    half_sum = run(
        functools.partial(plane_sum_kernel, far, planes),
        place,
        [keep, got],
        [like((rows + 16, D), bf16)],
        "ffn_far_sum",
    )[0]
    got = swap(half_sum, "mp", 1)
    att_parts = run(
        functools.partial(att_to_owner_kernel, chips, planes),
        place,
        att_got + [att_old],
        [like((planes * span, D), bf16)] * planes,
        "att_chip_sum",
        scratch=[pltpu.VMEM((4, planes * span, D), bf16)],
    )
    att_got = [att_parts[0]] + [swap(att_parts[u], "mp", u) for u in to_planes]
    message, small_grad = run(
        functools.partial(near_sum_kernel, planes),
        place,
        [half_sum, got, *att_got],
        [like((rows + planes * span, D), bf16), like((8, D), f32)],
        "near_sum",
    )
    small_grad = small_grad.reshape(-1)[: FF + D + 2]
    message, ins = together(message, ins)
    got = around_chips(message)
    in_got = [ins[0], None, swap(ins[2], "mp", 2), None]
    first_new = 0.5 * small_first + 0.5 * small_grad
    second_new = 0.5 * small_second + 0.5 * small_grad * small_grad
    correction = 1.0 - 0.5**STEP
    small_new = small_params - adam_rate * (first_new / correction) / (
        jnp.sqrt(second_new / correction) + 1e-08
    )
    smalls = (small_new, first_new, second_new)
    got, smalls, in_got, ins = together(got, smalls, in_got, ins)
    in_got[3] = swap(ins[3], "mp", 3)
    in_got[1] = swap(ins[1], "mp", 1)
    own = jnp.concatenate(got)
    other = swap(own, "dp", 1)
    far_m = run(
        functools.partial(momentum_rows_kernel, planes, chips, far),
        place,
        [own],
        [like((hidden_rows // 2, D), bf16)],
        "momentum_rows",
    )[0]
    far_m = swap(far_m, "mp", far)
    att_x = newton(
        place, own, other, planes, rows, D, tuple(range(planes)), True, "newton_att"
    )
    att_x, in_got, other = together(att_x, in_got, other)
    att_x = jnp.stack([att_x[0]] + [swap(att_x[u], "mp", u) for u in to_planes])
    step, far_step = newton(
        place, own, other, planes, 0, planes * hidden_rows, (0, far), False, "newton_ffn"
    )
    step, att_x = together(step, att_x)
    far_step = swap(far_step, "mp", far)
    far_m_got = swap(far_m, "dp", 1)
    att_other = swap(att_x, "dp", 1)
    new_be, new_bc = run(
        functools.partial(ffn_buffers_kernel, planes, chips),
        place,
        [own, other, far_m, far_m_got],
        [like((hidden_rows, D), f32)] * 2,
        "ffn_buffers",
    )
    layer_out = join_positions([lays[0], lay_near, *lay_far], place)
    in_grad = join_positions(in_got, place)
    att_out = run(
        functools.partial(att_final_kernel, planes, span),
        place,
        [att_x, att_other, *weights_old[:4]],
        [like(w.shape, f32) for w in weights_old[:4]] * 2,
        "att_final",
        scratch=[pltpu.VMEM((head_cols, D), bf16)],
    )
    far_step, new_be, layer_out, in_grad, att_out = together(
        far_step, new_be, layer_out, in_grad, att_out
    )
    got = swap(jnp.concatenate([step, far_step]), "dp", 1)
    new_we, new_wc = run(
        functools.partial(ffn_final_kernel, planes, chips),
        place,
        [step, far_step, got, w_expand, w_contract],
        [like((hidden_rows, D), f32)] * 2,
        "ffn_final",
    )
    return (
        (layer_out, in_grad)
        + tuple(att_out[:4])
        + (new_be, new_bc)
        + tuple(att_out[4:])
        + (new_we, new_wc)
        + smalls
    )


def solution(mesh):
    in_specs = (
        P("dp", None, None),
        P("dp", None),
        P("dp", "mp", None),
        P(None, "mp"),
        P(None, "mp"),
        P(None, "mp"),
        P("mp", None),
        P("mp", None),
        P("mp", None),
        P(),
        P(None, "mp"),
        P(None, "mp"),
        P(None, "mp"),
        P("mp", None),
        P("mp", None),
        P("mp", None),
        P(),
        P(),
    )
    out_specs = (
        P("dp", "mp", None),
        P("dp", "mp", None),
        P(None, "mp"),
        P(None, "mp"),
        P(None, "mp"),
        P("mp", None),
        P("mp", None),
        P("mp", None),
        P(None, "mp"),
        P(None, "mp"),
        P(None, "mp"),
        P("mp", None),
        P("mp", None),
        P("mp", None),
        P(),
        P(),
        P(),
    )
    block = mesh.shape["mp"] == 4 and mesh.shape["dp"] == 8
    return jax.shard_map(shards if block else general_shards, mesh=mesh, in_specs=in_specs, out_specs=out_specs, check_vma=False)
```

```python
import functools
import math

import jax
import jax.numpy as jnp
from jax import lax
from jax.experimental import pallas as pl
from jax.experimental.pallas import tpu as pltpu
from jax.sharding import PartitionSpec as P

D = 512
HEAD_DIM = 64
FF = 2048
MICRO = 2
STEP = 10


newton_one = 3.4445
newton_two = -4.775
newton_three = 2.0315
muon_rates = (1.0, 1.0, 1.0, 5.0, 2.0, 1.0)
adam_rate = 0.25
mask_fill = -1e30
highest_precision = lax.Precision.HIGHEST


def shortened(x):
    return jax.tree.map(lambda a: a.astype(jnp.bfloat16) if a.dtype == jnp.float32 else a, x)


def gelu_tanh(values):
    return jax.nn.gelu(values, approximate=True)


def block_scores(query_blk, key_part, docs_query, docs_key, first_row):
    scores = jnp.einsum(
        "sqhd,skhd->shqk", query_blk, key_part, preferred_element_type=jnp.float32
    ) * HEAD_DIM ** (-0.5)
    rows_at = first_row + jnp.arange(query_blk.shape[1])
    cols_at = jnp.arange(key_part.shape[1])
    allowed = (rows_at[:, None] >= cols_at[None, :])[None] & (
        docs_query[:, :, None] == docs_key[:, None, :]
    )
    return jnp.where(allowed[:, None], scores, mask_fill)


def attend(query_all, key_all, value_all, documents, span_rows):
    block_outs = []
    log_sums = []
    for block_index in range(query_all.shape[1] // span_rows):
        row_start = block_index * span_rows
        finish = row_start + span_rows
        scores = block_scores(
            query_all[:, row_start:finish],
            key_all[:, :finish],
            documents[:, row_start:finish],
            documents[:, :finish],
            row_start,
        )
        row_peak = jnp.max(scores, axis=-1, keepdims=True)
        exponent = jnp.exp(scores - row_peak)
        row_total = jnp.sum(exponent, axis=-1, keepdims=True)
        prob_low = (exponent / row_total).astype(jnp.bfloat16)
        block_outs.append(
            jnp.einsum(
                "shqk,skhd->sqhd",
                prob_low,
                value_all[:, :finish],
                preferred_element_type=jnp.float32,
            ).astype(jnp.bfloat16)
        )
        log_sums.append(row_peak + jnp.log(row_total))
    return (jnp.concatenate(block_outs, 1), log_sums)


def attend_back(query_all, key_all, value_all, documents, span_rows, log_sums, heads_grad):
    query_grads = []
    key_grad = jnp.zeros(key_all.shape, jnp.float32)
    value_grad = jnp.zeros(value_all.shape, jnp.float32)
    scale = HEAD_DIM ** (-0.5)
    for block_index in range(query_all.shape[1] // span_rows):
        row_start = block_index * span_rows
        finish = row_start + span_rows
        query_blk = query_all[:, row_start:finish]
        scores = block_scores(
            query_blk,
            key_all[:, :finish],
            documents[:, row_start:finish],
            documents[:, :finish],
            row_start,
        )
        probs = jnp.exp(scores - log_sums[block_index])
        prob_low = probs.astype(jnp.bfloat16)
        grad_blk = heads_grad[:, row_start:finish]
        grad_probs = jnp.einsum(
            "sqhd,skhd->shqk", grad_blk, value_all[:, :finish], preferred_element_type=jnp.float32
        )
        row_delta = jnp.sum(probs * grad_probs, axis=-1, keepdims=True)
        grad_scores = (probs * (grad_probs - row_delta)).astype(jnp.bfloat16)
        query_grads.append(
            jnp.einsum(
                "shqk,skhd->sqhd",
                grad_scores,
                key_all[:, :finish],
                preferred_element_type=jnp.float32,
            )
            * scale
        )
        key_grad = key_grad.at[:, :finish].add(
            jnp.einsum(
                "shqk,sqhd->skhd", grad_scores, query_blk, preferred_element_type=jnp.float32
            )
            * scale
        )
        value_grad = value_grad.at[:, :finish].add(
            jnp.einsum("shqk,sqhd->skhd", prob_low, grad_blk, preferred_element_type=jnp.float32)
        )
    return (jnp.concatenate(query_grads, 1), key_grad, value_grad)


def gram_part(iterate, by_columns):
    if by_columns:
        return lax.dot_general(
            iterate,
            iterate,
            (((1,), (1,)), ((), ())),
            precision=highest_precision,
            preferred_element_type=jnp.float32,
        )
    return lax.dot_general(
        iterate,
        iterate,
        (((0,), (0,)), ((), ())),
        precision=highest_precision,
        preferred_element_type=jnp.float32,
    )


def newton_update(iterate, gram_sum, by_columns):
    square = jnp.dot(gram_sum, gram_sum, precision=highest_precision)
    polynomial = newton_two * gram_sum + newton_three * square
    if by_columns:
        applied = jnp.dot(polynomial, iterate, precision=highest_precision)
    else:
        applied = lax.dot_general(
            iterate,
            polynomial,
            (((1,), (1,)), ((), ())),
            precision=highest_precision,
            preferred_element_type=jnp.float32,
        )
    return newton_one * iterate + applied


def general_shards(
    layer_in,
    doc_ids,
    out_grad,
    w_query,
    w_key,
    w_value,
    w_output,
    w_expand,
    w_contract,
    small_params,
    buffer_query,
    buffer_key,
    buffer_value,
    buffer_output,
    buffer_expand,
    buffer_contract,
    small_first,
    small_second,
):
    group_count = lax.axis_size("mp")
    group_index = lax.axis_index("mp")
    seq_count, length, model_width = layer_in.shape
    per_micro = seq_count // MICRO
    token_span = length // group_count
    head_cols = w_query.shape[1]
    heads_here = head_cols // HEAD_DIM
    span_rows = min(512, length)
    expansion_bias = small_params[:FF]
    contraction_bias = small_params[FF : FF + D]
    alpha_attend = small_params[FF + D]
    alpha_ffn = small_params[FF + D + 1]
    query_key_value_weight = jnp.concatenate((w_query, w_key, w_value), 1).astype(jnp.bfloat16)
    row_local = (
        w_output.astype(jnp.bfloat16),
        w_expand.astype(jnp.bfloat16),
        w_contract.astype(jnp.bfloat16),
    )
    grad_qkv_weight = jnp.zeros((model_width, 3 * head_cols), jnp.float32)
    grad_output = jnp.zeros((D, D), jnp.float32)
    grad_expand = jnp.zeros((FF, D), jnp.float32)
    grad_contract = jnp.zeros((FF, D), jnp.float32)
    grad_bias_expand = jnp.zeros((FF,), jnp.float32)
    grad_bias_contract = jnp.zeros((D,), jnp.float32)
    grad_alpha_attend = jnp.zeros((), jnp.float32)
    grad_alpha_ffn = jnp.zeros((), jnp.float32)
    out_blocks = []
    grad_blocks = []
    for micro_index in range(MICRO):
        rows_from = micro_index * per_micro
        layer_inputs = layer_in[rows_from : rows_from + per_micro]
        documents = doc_ids[rows_from : rows_from + per_micro]
        upstream = out_grad[rows_from : rows_from + per_micro]
        query_key_value_rows = jnp.einsum(
            "orv,vx->orx", layer_inputs, query_key_value_weight, preferred_element_type=jnp.float32
        ).astype(jnp.bfloat16)
        qkv_split = query_key_value_rows.reshape(per_micro, length, 3, heads_here, HEAD_DIM)
        query_all = qkv_split[:, :, 0]
        key_all = qkv_split[:, :, 1]
        value_all = qkv_split[:, :, 2]
        head_outputs, log_sums = attend(query_all, key_all, value_all, documents, span_rows)
        heads_flat = head_outputs.reshape(per_micro, length, head_cols)
        heads_tok = lax.all_to_all(heads_flat, "mp", split_axis=1, concat_axis=2, tiled=True)
        row_now = (
            lax.all_gather(row_local[0], "mp", axis=0, tiled=True),
            lax.all_gather(row_local[1], "mp", axis=0, tiled=True),
            lax.all_gather(row_local[2], "mp", axis=0, tiled=True),
        )
        output_full, expand_full, contract_full = row_now
        attention_result = jnp.einsum(
            "std,de->ste", heads_tok, output_full, preferred_element_type=jnp.float32
        )
        local_in = lax.dynamic_slice_in_dim(
            layer_inputs, group_index * token_span, token_span, 1
        ).astype(jnp.float32)
        middle_activation = local_in + alpha_attend * attention_result
        middle_low = middle_activation.astype(jnp.bfloat16)
        preactivation = (
            jnp.einsum("std,fd->stf", middle_low, expand_full, preferred_element_type=jnp.float32)
            + expansion_bias
        )
        hidden_state, gelu_back = jax.vjp(gelu_tanh, preactivation)
        hidden_low = hidden_state.astype(jnp.bfloat16)
        residual_branch = (
            jnp.einsum("stf,fd->std", hidden_low, contract_full, preferred_element_type=jnp.float32)
            + contraction_bias
        )
        out_blocks.append(middle_activation + alpha_ffn * residual_branch)
        grad_alpha_ffn = grad_alpha_ffn + jnp.sum(upstream * residual_branch)
        branch_grad = (alpha_ffn * upstream).astype(jnp.bfloat16)
        grad_bias_contract = grad_bias_contract + jnp.sum(
            branch_grad, axis=(0, 1), dtype=jnp.float32
        )
        grad_contract = grad_contract + jnp.einsum(
            "stf,std->fd", hidden_low, branch_grad, preferred_element_type=jnp.float32
        )
        hidden_grad = jnp.einsum(
            "std,fd->stf", branch_grad, contract_full, preferred_element_type=jnp.float32
        )
        pre_grad = gelu_back(hidden_grad)[0].astype(jnp.bfloat16)
        grad_bias_expand = grad_bias_expand + jnp.sum(pre_grad, axis=(0, 1), dtype=jnp.float32)
        grad_expand = grad_expand + jnp.einsum(
            "stf,std->fd", pre_grad, middle_low, preferred_element_type=jnp.float32
        )
        middle_grad = upstream + jnp.einsum(
            "stf,fd->std", pre_grad, expand_full, preferred_element_type=jnp.float32
        )
        grad_alpha_attend = grad_alpha_attend + jnp.sum(middle_grad * attention_result)
        attend_grad = (alpha_attend * middle_grad).astype(jnp.bfloat16)
        grad_output = grad_output + jnp.einsum(
            "std,ste->de", heads_tok, attend_grad, preferred_element_type=jnp.float32
        )
        heads_grad_tok = jnp.einsum(
            "ste,de->std", attend_grad, output_full, preferred_element_type=jnp.float32
        ).astype(jnp.bfloat16)
        heads_grad = lax.all_to_all(heads_grad_tok, "mp", split_axis=2, concat_axis=1, tiled=True)
        heads_grad = heads_grad.reshape(per_micro, length, heads_here, HEAD_DIM)
        query_grad, key_grad, value_grad = attend_back(
            query_all, key_all, value_all, documents, span_rows, log_sums, heads_grad
        )
        query_key_value_gradient = (
            jnp.stack((query_grad, key_grad, value_grad), 2)
            .reshape(per_micro, length, 3 * head_cols)
            .astype(jnp.bfloat16)
        )
        grad_qkv_weight = grad_qkv_weight + jnp.einsum(
            "tmf,tmp->fp",
            layer_inputs,
            query_key_value_gradient,
            preferred_element_type=jnp.float32,
        )
        partial_grad = jnp.einsum(
            "nrj,yj->nry",
            query_key_value_gradient,
            query_key_value_weight,
            preferred_element_type=jnp.float32,
        )
        head_part = lax.psum_scatter(
            partial_grad.astype(jnp.bfloat16), "mp", scatter_dimension=1, tiled=True
        ).astype(jnp.float32)
        grad_blocks.append(middle_grad + head_part)
    layer_out = jnp.concatenate(out_blocks, 0)
    in_grad = jnp.concatenate(grad_blocks, 0)
    output_part, expand_part, contract_part = (
        lax.psum_scatter(
            grad_output.astype(jnp.bfloat16), "mp", scatter_dimension=0, tiled=True
        ).astype(jnp.float32),
        lax.psum_scatter(
            grad_expand.astype(jnp.bfloat16), "mp", scatter_dimension=0, tiled=True
        ).astype(jnp.float32),
        lax.psum_scatter(
            grad_contract.astype(jnp.bfloat16), "mp", scatter_dimension=0, tiled=True
        ).astype(jnp.float32),
    )
    matrix_grads = (
        lax.psum(grad_qkv_weight[:, :head_cols].astype(jnp.bfloat16), "dp").astype(jnp.float32),
        lax.psum(grad_qkv_weight[:, head_cols : 2 * head_cols].astype(jnp.bfloat16), "dp").astype(
            jnp.float32
        ),
        lax.psum(grad_qkv_weight[:, 2 * head_cols :].astype(jnp.bfloat16), "dp").astype(
            jnp.float32
        ),
        lax.psum(output_part.astype(jnp.bfloat16), "dp").astype(jnp.float32),
        lax.psum(expand_part.astype(jnp.bfloat16), "dp").astype(jnp.float32),
        lax.psum(contract_part.astype(jnp.bfloat16), "dp").astype(jnp.float32),
    )
    small_local = jnp.concatenate(
        (grad_bias_expand, grad_bias_contract, jnp.stack((grad_alpha_attend, grad_alpha_ffn)))
    )
    small_grad = lax.psum(small_local, ("dp", "mp"))
    first_new = 0.5 * small_first + 0.5 * small_grad
    second_new = 0.5 * small_second + 0.5 * small_grad * small_grad
    correction = 1.0 - 0.5**STEP
    small_new = small_params - adam_rate * (first_new / correction) / (
        jnp.sqrt(second_new / correction) + 1e-08
    )
    olds = (buffer_query, buffer_key, buffer_value, buffer_output, buffer_expand, buffer_contract)
    weights_old = (w_query, w_key, w_value, w_output, w_expand, w_contract)
    by_columns = (True, True, True, False, False, False)
    buffers = tuple(
        (0.5 * old_buffer + grad_matrix for old_buffer, grad_matrix in zip(olds, matrix_grads))
    )
    squares = lax.psum(tuple((jnp.sum(matrix * matrix) for matrix in buffers)), "mp")
    iterates = [
        matrix / (jnp.sqrt(square_sum) + 1e-07) for matrix, square_sum in zip(buffers, squares)
    ]
    for newton_step in range(5):
        gram_sums = jax.tree.map(
            lambda part: part.astype(jnp.float32),
            lax.psum(
                shortened(
                    tuple(
                        (
                            gram_part(iterate, column_flag)
                            for iterate, column_flag in zip(iterates, by_columns)
                        )
                    )
                ),
                "mp",
            ),
        )
        iterates = [
            newton_update(iterate, gram_sum, column_flag)
            for iterate, gram_sum, column_flag in zip(iterates, gram_sums, by_columns)
        ]
    new_weights = tuple(
        (
            weight - rate * iterate
            for weight, rate, iterate in zip(weights_old, muon_rates, iterates)
        )
    )
    return (layer_out, in_grad) + buffers + new_weights + (small_new, first_new, second_new)


max_doc = 512
q_rows = 256
f32 = jnp.float32
bf16 = jnp.bfloat16
nt = (((1,), (1,)), ((), ()))
nn = (((1,), (0,)), ((), ()))
tn = (((0,), (0,)), ((), ()))
gelu_root = 0.7978845608028654
gelu_cube = 0.044715


def mm(a, b, dims):
    return lax.dot_general(a, b, dims, preferred_element_type=f32)


def swap(x, axis, mask):
    size = lax.axis_size(axis)
    return lax.ppermute(x, axis, [(a, a ^ mask) for a in range(size)])


def reorder(x, index, axis):
    parts = [
        lax.dynamic_slice_in_dim(x, slot ^ index, 1, axis) for slot in range(x.shape[axis])
    ]
    return jnp.concatenate(parts, axis)


def pick(x, index):
    return lax.dynamic_index_in_dim(x, index, 0, keepdims=False)


def like(shape, dtype):
    return jax.ShapeDtypeStruct(shape, dtype)


whole = pl.BlockSpec(memory_space=pltpu.VMEM)
hbm = pl.BlockSpec(memory_space=pl.ANY)


def run(kernel, place, args, outs, name, grid=(1,), in_specs=None, out_specs=None, scratch=(), flops=0, spare=4):
    moved = sum(a.size * a.dtype.itemsize for a in args)
    moved += sum(o.size * jnp.dtype(o.dtype).itemsize for o in outs)
    held = moved + sum(
        math.prod(b.shape) * b.dtype.itemsize for b in scratch if b.memory_space == pltpu.VMEM
    )
    return pl.pallas_call(
        kernel,
        grid_spec=pltpu.PrefetchScalarGridSpec(
            num_scalar_prefetch=1,
            grid=grid,
            in_specs=in_specs or [whole] * len(args),
            out_specs=out_specs or [whole] * len(outs),
            scratch_shapes=list(scratch),
        ),
        out_shape=list(outs),
        compiler_params=pltpu.CompilerParams(vmem_limit_bytes=min(56 << 20, held + (spare << 20))),
        cost_estimate=pl.CostEstimate(
            flops=flops, bytes_accessed=moved if flops else 0, transcendentals=0
        ),
        name=name,
    )(place, *args)


def weight_pieces_kernel(place, q, k, v, o, e, c, qkv_out, rest_out, turned):
    span = o.shape[0]
    at = pl.multiple_of(place[1] * span, span)
    for which, ref in enumerate((q, k, v)):
        turned[...] = ref[...].T
        qkv_out[which * span : (which + 1) * span, :] = turned[pl.ds(at, span), :].astype(bf16)
    hid = e.shape[0]
    rest_out[:span, :] = o[...].astype(bf16)
    rest_out[span : span + hid, :] = e[...].astype(bf16)
    rest_out[span + hid :, :] = c[...].astype(bf16)


def buffer_pieces_kernel(place, q, k, v, o, e, c, att_out, ffn_out, turned):
    span = o.shape[0]
    at = pl.multiple_of(place[1] * span, span)
    for which, ref in enumerate((q, k, v)):
        turned[...] = ref[...].T
        att_out[which] = 0.5 * turned[pl.ds(at, span), :]
    att_out[3] = 0.5 * o[...]
    ffn_out[0] = 0.5 * c[...]
    ffn_out[1] = 0.5 * e[...]


def pieces(kernel, place, arrays, outs, name):
    q, k, v, o, e, c = arrays
    spots = lax.axis_size("dp")
    span, hid = o.shape[0] // spots, e.shape[0] // spots
    row = lambda size: pl.BlockSpec((size, D), lambda g, place: (place[1], 0))
    return run(
        kernel,
        place,
        arrays,
        outs,
        name,
        in_specs=[whole, whole, whole, row(span), row(hid), row(hid)],
        spare=56,
        scratch=[pltpu.VMEM((q.shape[1], D), f32)],
    )


def split_positions_kernel(place, *refs):
    count = len(refs) // 2
    for u in range(count):
        refs[count + u][...] = refs[u][0].astype(bf16)


def split_positions(x, place):
    planes, span, width = x.shape
    block = lambda u: pl.BlockSpec((1, span, width), lambda g, place: (place[0] ^ u, 0, 0))
    return run(
        split_positions_kernel,
        place,
        [x] * planes,
        [like((span, width), bf16)] * planes,
        "split_positions",
        in_specs=[block(u) for u in range(planes)],
    )


def join_positions_kernel(place, *refs):
    out = refs[-1]
    for u, ref in enumerate(refs[:-1]):
        out[place[0] ^ u] = ref[...].astype(f32)


def join_positions(parts, place):
    span, width = parts[0].shape
    return run(
        join_positions_kernel,
        place,
        parts,
        [like((len(parts), span, width), f32)],
        "join_positions",
    )[0]


def window(first_row):
    return max(0, first_row + 1 - max_doc) // 128 * 128


def pair_weights(own, other, span):
    parts = []
    for which in range(3):
        for m in range(own.shape[0]):
            for half in (own, other):
                parts.append(half[m, 0, which * span : (which + 1) * span, :])
    return jnp.concatenate(parts, 0)


def interleave(own, other):
    return [half for pair in zip(own, other) for half in pair]


def in_lanes(low, high, x, rest):
    lane = lax.broadcasted_iota(jnp.int32, x.shape, 1)
    return jnp.where((lane >= low) & (lane < high), x, rest)


def spare_lanes(half, values, like_x):
    lane = lax.broadcasted_iota(jnp.int32, like_x.shape, 1)
    first = HEAD_DIM * (1 - half)
    out = jnp.zeros_like(like_x)
    for at, value in enumerate(values):
        out = jnp.where(lane == first + at, value, out)
    return out


def head_lanes(half, x, values=()):
    return in_lanes(HEAD_DIM * half, HEAD_DIM * (half + 1), x, spare_lanes(half, values, x))


def low_parts(x):
    parts = []
    for _ in range(3):
        parts.append(x.astype(bf16))
        x = x - parts[-1].astype(f32)
    return parts


def forward_kernel(place, last_ref, in_ref, *refs):
    own, other, x_ref, o_ref, bias_ref, q_ref, v_ref = refs
    length = in_ref.shape[1]
    span = own.shape[2] // 3
    blocks = [(first, window(first), first + q_rows) for first in range(0, length, q_rows)]

    @pl.when(pl.program_id(0) == 0)
    def _():
        for first, low, high in blocks:
            row = first + lax.broadcasted_iota(jnp.int32, (q_rows, high - low), 0)
            col = low + lax.broadcasted_iota(jnp.int32, (q_rows, high - low), 1)
            allowed = (col <= row) & (row <= last_ref[:, low:high])
            bias_ref[first:high, : high - low] = jnp.where(allowed, 0.0, mask_fill)

    weight = pair_weights(own, other, span)
    rows = mm(in_ref[0], weight, nt).astype(bf16)
    query = rows[:, :128] * jnp.asarray(HEAD_DIM**-0.5, bf16)
    x_ref[0, 2] = rows[:, 128:256]
    x_ref[0, 3] = rows[:, 256:]
    one = jnp.asarray(1, bf16)
    for half in range(2):
        q_ref[half] = head_lanes(half, query)
        v_ref[half] = head_lanes(half, rows[:, 256:], (one,))
    for first, low, high in blocks:
        found = []
        for half in range(2):
            spare = HEAD_DIM * (1 - half)
            scores = mm(q_ref[half, first:high, :], x_ref[0, 2, low:high, :], nt)
            scores = scores + bias_ref[first:high, : high - low]
            peak = jnp.max(scores, axis=1, keepdims=True)
            weight = jnp.exp(scores - peak).astype(bf16)
            out = mm(weight, v_ref[half, low:high, :], nn)
            total = out[:, spare : spare + 1]
            found.append(out * (1.0 / total))
            parts = low_parts(-(peak + jnp.log(total)))
            x_ref[0, half, first:high, :] = head_lanes(half, q_ref[half, first:high, :], parts)
        o_ref[first:high, :] = in_lanes(0, HEAD_DIM, found[0], found[1]).astype(bf16)


def attention(place, last, inputs, halves):
    length = inputs.shape[1]
    chips, planes, rows, _ = halves[0].shape
    half = pl.BlockSpec((chips, 1, rows, D), lambda h, place: (0, h, 0, 0))
    return run(
        forward_kernel,
        place,
        [last, inputs, *halves],
        [like((planes, 4, length, 128), bf16), like((length, D), bf16)],
        "attention_forward",
        spare=56,
        grid=(planes,),
        in_specs=[whole, pl.BlockSpec((1, length, D), lambda h, place: (place[0], 0, 0))]
        + [half] * len(halves),
        out_specs=[
            pl.BlockSpec((1, 4, length, 128), lambda h, place: (h, 0, 0, 0)),
            pl.BlockSpec((length, 128), lambda h, place: (0, h)),
        ],
        scratch=[
            pltpu.VMEM((length, 768), f32),
            pltpu.VMEM((2, length, 128), bf16),
            pltpu.VMEM((2, length, 128), bf16),
        ],
        flops=8 * length * D * D + 2 * length * 768 * 512 * planes,
    )


def backward_kernel(
    is_last, spots, place, start_ref, in_hbm, x_ref, g_ref, o_ref, gout_ref, gmid_hbm, *rest
):
    own, other, rest = rest[0], rest[1], rest[2:]
    ins, rest = rest[:-12], rest[-12:]
    keep_ref, give_ref, dk_ref, dv_ref, dq_ref, acc_ref, bias_ref, k_ref, v_ref, gs_ref = rest[:10]
    in_ref, sems = rest[10:]
    length = in_ref.shape[0]
    load_acc = pltpu.make_async_copy(gmid_hbm, acc_ref, sems.at[0])
    load_in = pltpu.make_async_copy(in_hbm.at[place[0]], in_ref, sems.at[1])
    span = own.shape[2] // 3
    chips = spots // 2
    step = pl.program_id(0)
    blocks = [(first, window(first), first + q_rows) for first in range(0, length, q_rows)]

    @pl.when(step == 0)
    def _():
        load_acc.start()
        load_in.start()
        for first, low, high in blocks:
            col = low + lax.broadcasted_iota(jnp.int32, (high - low, q_rows), 0)
            row = first + lax.broadcasted_iota(jnp.int32, (high - low, q_rows), 1)
            allowed = (col <= row) & (col >= start_ref[:, first:high])
            bias_ref[: high - low, first:high] = jnp.where(allowed, 0.0, mask_fill)

    dk_ref[...] = jnp.zeros_like(dk_ref)
    dv_ref[...] = jnp.zeros_like(dv_ref)
    one = jnp.asarray(1, bf16)
    product = g_ref[...].astype(f32) * o_ref[...].astype(f32)
    for half in range(2):
        k_ref[half] = head_lanes(half, x_ref[0, 2], (one,) * 3)
        v_ref[half] = head_lanes(half, x_ref[0, 3], (one,) * 3)
        delta = jnp.sum(head_lanes(half, product), axis=1, keepdims=True)
        gs_ref[half] = head_lanes(half, g_ref[...], low_parts(-delta))
    for first, low, high in blocks:
        q_both = jnp.concatenate([head_lanes(half, x_ref[0, half, first:high, :]) for half in range(2)], 0)
        g_both = jnp.concatenate([head_lanes(half, g_ref[first:high, :]) for half in range(2)], 0)
        dq = jnp.zeros((q_rows, 128), f32)
        for at in range(low, high, q_rows):
            keys = slice(at, at + q_rows)
            bias = bias_ref[at - low : at - low + q_rows, first:high]
            probs, g_scores = [], []
            for half in range(2):
                scores = mm(k_ref[half, keys, :], x_ref[0, half, first:high, :], nt) + bias
                weight = jnp.exp(scores)
                g_probs = mm(v_ref[half, keys, :], gs_ref[half, first:high, :], nt)
                probs.append(weight.astype(bf16))
                g_scores.append((weight * g_probs).astype(bf16))
            k_both = jnp.concatenate([head_lanes(half, x_ref[0, 2, keys, :]) for half in range(2)], 0)
            dq = dq + mm(jnp.concatenate(g_scores, 0), k_both, tn)
            dv_ref[keys, :] += mm(jnp.concatenate(probs, 1), g_both, nn)
            dk_ref[keys, :] += mm(jnp.concatenate(g_scores, 1), q_both, nn)
        dq_ref[first:high, :] = (dq * HEAD_DIM**-0.5).astype(bf16)
    grads = (dq_ref[...], dk_ref[...].astype(bf16), dv_ref[...].astype(bf16))
    grads = jnp.concatenate(grads, 1)
    weight = pair_weights(own, other, span)

    @pl.when(step == 0)
    def _():
        load_acc.wait()
        load_in.wait()

    acc_ref[...] += mm(grads, weight, nn)
    all_rows = mm(grads, in_ref[...], tn).astype(bf16)
    for which in range(4):
        if which < 3:
            rows = all_rows[which * 128 : (which + 1) * 128, :]
        else:
            rows = gout_ref[...]
        for m in range(chips):
            for c, ref in enumerate((keep_ref, give_ref)):
                at = (2 * m + c) * span
                ref[m, 0, which * span : (which + 1) * span, :] = rows[at : at + span, :]

    @pl.when(step == pl.num_programs(0) - 1)
    def _():
        if not is_last:
            save = pltpu.make_async_copy(acc_ref, ins[0], sems.at[0])
            save.start()
            save.wait()
            return
        rows = ins[0].shape[0]
        for u, ref in enumerate(ins):
            at = pl.multiple_of((place[0] ^ u) * rows, rows)
            ref[...] = acc_ref[pl.ds(at, rows), :].astype(bf16)


def attention_back(
    place, start, inputs, halves, qkv, heads_grad, heads, grad_output, so_far, first, count, is_last
):
    length = inputs.shape[1]
    chips, planes, rows, _ = halves[0].shape
    spots = 2 * chips
    span = rows // 3
    half = pl.BlockSpec((chips, 1, rows, D), lambda h, place: (0, first + h, 0, 0))
    out_half = pl.BlockSpec((chips, 1, 4 * span, D), lambda h, place: (0, h, 0, 0))
    outs = [like((length // planes, D), bf16)] * planes if is_last else [like((length, D), f32)]
    out = run(
        functools.partial(backward_kernel, is_last, spots),
        place,
        [start, inputs, qkv, heads_grad, heads, grad_output, so_far, *halves],
        outs + [like((chips, count, 4 * span, D), bf16)] * 2,
        "attention_backward",
        spare=56,
        grid=(count,),
        in_specs=[
            whole,
            hbm,
            pl.BlockSpec((1, 4, length, 128), lambda h, place: (first + h, 0, 0, 0)),
            pl.BlockSpec((length, 128), lambda h, place: (0, first + h)),
            pl.BlockSpec((length, 128), lambda h, place: (0, first + h)),
            pl.BlockSpec((128, D), lambda h, place: (first + h, 0)),
            hbm,
        ]
        + [half] * 2,
        out_specs=([whole] * planes if is_last else [hbm]) + [out_half] * 2,
        scratch=[
            pltpu.VMEM((length, 128), f32),
            pltpu.VMEM((length, 128), f32),
            pltpu.VMEM((length, 128), bf16),
            pltpu.VMEM((length, D), f32),
            pltpu.VMEM((768, length), f32),
            pltpu.VMEM((2, length, 128), bf16),
            pltpu.VMEM((2, length, 128), bf16),
            pltpu.VMEM((2, length, 128), bf16),
            pltpu.VMEM((length, D), bf16),
            pltpu.SemaphoreType.DMA((2,)),
        ],
        flops=(12 * length * D * D + 5 * length * 768 * 512 * planes) * count // planes,
    )
    return out[:-2], out[-2], out[-1]


def ffn_kernel(planes, spots, per, place, *refs):
    alphas, in_hbm, heads_hbm = refs[:3]
    ups = refs[3 : 3 + planes]
    halves = refs[3 + planes : 3 + planes + spots]
    bias_ref, bout_ref = refs[3 + planes + spots : 5 + planes + spots]
    outs = refs[5 + planes + spots :]
    lays = outs[:planes]
    keep_ref, give_ref, gout_ref, gheads_hbm, gmid_hbm, gbin_ref, gbout_ref, galpha_ref = outs[
        planes : planes + 8
    ]
    (
        attended, middle, mid_low, g_low, up, branch, o_low, lay, weights, in_ref, heads_ref,
        o_parts, gmid_ref, gheads_ref, sems, w_sems, out_sems,
    ) = outs[planes + 8 :]
    chips = spots // 2
    length = in_ref.shape[0]
    block = length // planes
    hid = keep_ref.shape[2] // planes
    span = halves[0].shape[1] - 2 * hid
    step = pl.program_id(0)
    steps = pl.num_programs(0)
    alpha_att, alpha_ffn = alphas[0], alphas[1]
    size = 512
    tiles = [slice(at, at + size) for at in range(0, length, size)]

    def order(at):
        return 2 * (at % chips) + at // chips

    def weight_copy(at):
        return pltpu.make_async_copy(
            halves[order(at)].at[:, span:, :], weights.at[at], w_sems.at[at]
        )

    @pl.when(step == 0)
    def _():
        first = [
            pltpu.make_async_copy(half.at[:, :span, :], o_parts.at[at], sems.at[at])
            for at, half in enumerate(halves)
        ]
        first.append(pltpu.make_async_copy(heads_hbm, heads_ref, sems.at[spots]))
        first.append(pltpu.make_async_copy(in_hbm.at[place[0]], in_ref, sems.at[spots + 1]))
        for u in range(planes):
            at = pl.multiple_of((place[0] ^ u) * block, block)
            first.append(
                pltpu.make_async_copy(ups[u], up.at[pl.ds(at, block), :], sems.at[spots + 2 + u])
            )
        for copy in first:
            copy.start()
        for at in range(spots):
            weight_copy(at).start()
        for copy in first:
            copy.wait()
        for k in range(planes):
            for at in range(spots):
                row = (k * spots + at) * span
                o_low[row : row + span, :] = o_parts[at, k]
        total = jnp.zeros((1, D), f32)
        for t in tiles:
            found = mm(heads_ref[t, :], o_low[...], nn)
            attended[t, :] = found
            mid = in_ref[t, :].astype(f32) + alpha_att * found
            middle[t, :] = mid
            mid_low[t, :] = mid.astype(bf16)
            upstream = up[t, :].astype(f32)
            grad = (alpha_ffn * upstream).astype(bf16)
            g_low[t, :] = grad
            total = total + jnp.sum(grad.astype(f32), axis=0, keepdims=True)
            branch[t, :] = jnp.zeros((size, D), f32)
            gmid_ref[t, :] = upstream
        gbout_ref[...] = total

    for at in range(spots):

        @pl.when(step == at // per)
        def _():
            weight_copy(at).wait()

    rows = [weights[step * per + g] for g in range(per)]
    expand = jnp.concatenate([row[:, :hid, :].reshape(planes * hid, D) for row in rows], 0)
    contract = jnp.concatenate([row[:, hid:, :].reshape(planes * hid, D) for row in rows], 0)
    bias = bias_ref[0]
    gc = jnp.zeros((per * planes * hid, D), f32)
    ge = jnp.zeros((per * planes * hid, D), f32)
    gb = jnp.zeros((1, per * planes * hid), f32)
    for t in tiles:
        mid = mid_low[t, :]
        grad = g_low[t, :]
        pre = mm(mid, expand, nt) + bias
        square = pre * pre
        tanh = jnp.tanh(gelu_root * pre * (1.0 + gelu_cube * square))
        half = 0.5 * (1.0 + tanh)
        hidden = (pre * half).astype(bf16)
        slope = half + (0.5 * gelu_root) * pre * (1.0 - tanh * tanh) * (
            1.0 + (3.0 * gelu_cube) * square
        )
        branch[t, :] += mm(hidden, contract, nn)
        g_pre = (mm(grad, contract, nt) * slope).astype(bf16)
        gmid_ref[t, :] += mm(g_pre, expand, nn)
        gc = gc + mm(hidden, grad, tn)
        ge = ge + mm(g_pre, mid, tn)
        gb = gb + jnp.sum(g_pre.astype(f32), axis=0, keepdims=True)
    gc = gc.astype(bf16)
    ge = ge.astype(bf16)
    group = planes * hid

    def store(ref):
        for g in range(per):
            ref[g, 0] = gc[g * group : (g + 1) * group, :]
            ref[g, 1] = ge[g * group : (g + 1) * group, :]

    pl.when(step < steps // 2)(lambda: store(keep_ref))
    pl.when(step >= steps // 2)(lambda: store(give_ref))
    gbin_ref[0] = gb

    @pl.when(step == steps - 1)
    def _():
        sum_ffn = jnp.zeros((1, D), f32)
        sum_att = jnp.zeros((1, D), f32)
        gout = jnp.zeros((D, D), f32)
        copies = []
        for at, t in enumerate(tiles):
            gm = gmid_ref[t, :]
            copies.append(
                pltpu.make_async_copy(gmid_ref.at[t, :], gmid_hbm.at[t, :], out_sems.at[0, at])
            )
            copies[-1].start()
            g_att = (alpha_att * gm).astype(bf16)
            gheads_ref[t, :] = mm(g_att, o_low[...], nt).astype(bf16)
            copies.append(
                pltpu.make_async_copy(gheads_ref.at[t, :], gheads_hbm.at[t, :], out_sems.at[1, at])
            )
            copies[-1].start()
            gout = gout + mm(heads_ref[t, :], g_att, tn)
            sum_att = sum_att + jnp.sum(gm * attended[t, :], axis=0, keepdims=True)
            final = branch[t, :] + bout_ref[...]
            lay[t, :] = middle[t, :] + alpha_ffn * final
            sum_ffn = sum_ffn + jnp.sum(up[t, :].astype(f32) * final, axis=0, keepdims=True)
        gout_ref[...] = gout.astype(bf16)
        galpha_ref[0:1, :] = sum_att
        galpha_ref[1:2, :] = sum_ffn
        for u, ref in enumerate(lays):
            at = pl.multiple_of((place[0] ^ u) * block, block)
            ref[...] = lay[pl.ds(at, block), :].astype(bf16)
        for copy in copies:
            copy.wait()


def feed_forward(place, alphas, inputs, heads, ups, halves, bias, bout):
    length = inputs.shape[1]
    planes = len(ups)
    spots = len(halves)
    chips = spots // 2
    span, hid = heads.shape[1] // (planes * spots), bias.shape[-1] // planes
    per = 2 if chips % 2 == 0 else 1
    steps = spots // per
    bias = bias.reshape(steps, 1, per * planes * hid)
    tiles = length // 512
    group = planes * hid
    out = run(
        functools.partial(ffn_kernel, planes, spots, per),
        place,
        [alphas, inputs, heads, *ups, *halves, bias, bout],
        [like((length // planes, D), bf16)] * planes
        + [
            like((chips, 2, group, D), bf16),
            like((chips, 2, group, D), bf16),
            like((D, D), bf16),
            like((length, D), bf16),
            like((length, D), f32),
            like((steps, 1, per * group), f32),
            like((1, D), f32),
            like((2, D), f32),
        ],
        "feed_forward",
        spare=56,
        grid=(steps,),
        in_specs=[pl.BlockSpec(memory_space=pltpu.SMEM)]
        + [hbm] * (2 + planes + spots)
        + [pl.BlockSpec((1, 1, per * group), lambda t, place: (t, 0, 0)), whole],
        out_specs=[whole] * planes
        + [
            pl.BlockSpec(
                (per, 2, group, D), lambda t, place: (jnp.minimum(t, steps // 2 - 1), 0, 0, 0)
            ),
            pl.BlockSpec(
                (per, 2, group, D), lambda t, place: (jnp.maximum(t - steps // 2, 0), 0, 0, 0)
            ),
            whole,
            hbm,
            hbm,
            pl.BlockSpec((1, 1, per * group), lambda t, place: (t, 0, 0)),
            whole,
            whole,
        ],
        scratch=[
            pltpu.VMEM((length, D), f32),
            pltpu.VMEM((length, D), f32),
            pltpu.VMEM((length, D), bf16),
            pltpu.VMEM((length, D), bf16),
            pltpu.VMEM((length, D), bf16),
            pltpu.VMEM((length, D), f32),
            pltpu.VMEM((D, D), bf16),
            pltpu.VMEM((length, D), f32),
            pltpu.VMEM((spots, planes, 2 * hid, D), bf16),
            pltpu.VMEM((length, D), bf16),
            pltpu.VMEM((length, D), bf16),
            pltpu.VMEM((spots, planes, span, D), bf16),
            pltpu.VMEM((length, D), f32),
            pltpu.VMEM((length, D), bf16),
            pltpu.SemaphoreType.DMA((spots + 2 + planes,)),
            pltpu.SemaphoreType.DMA((spots,)),
            pltpu.SemaphoreType.DMA((2, tiles)),
        ],
        flops=12 * length * D * 2 * chips * group,
    )
    return out[:planes], out[planes:]


def att_core_kernel(place, keep, got, *outs):
    rows = keep.shape[2]
    for m, out in enumerate(outs):
        for k in range(keep.shape[1]):
            total = keep[m, k].astype(f32) + got[m, k].astype(f32)
            out[k * rows : (k + 1) * rows, :] = total.astype(bf16)


def small_write(out, total):
    at = out.shape[0] - 2 * total.shape[0]
    high = total.astype(bf16)
    out[at : at + total.shape[0], :] = high
    out[at + total.shape[0] :, :] = (total - high.astype(f32)).astype(bf16)


def small_read(ref):
    rows = ref.shape[0]
    return ref[rows - 16 : rows - 8, :].astype(f32) + ref[rows - 8 :, :].astype(f32)


def ffn_core_kernel(place, own, got, small, *outs):
    rows = own.shape[0] // len(outs)
    total = small[...]
    for at, out in enumerate(outs):
        for r in range(0, rows, 256):
            a = own[at * rows + r : at * rows + r + 256, :].astype(f32)
            b = got[at * rows + r : at * rows + r + 256, :].astype(f32)
            out[r : r + 256, :] = (a + b).astype(bf16)
        small_write(out, total)


def ffn_chip_kernel(chips, planes, place, old, *refs):
    ins, give, keep, both = refs[:chips], refs[-3], refs[-2], refs[-1]
    hid = old.shape[1]
    rows = planes * hid
    small = small_read(ins[0])
    for ref in ins[1:]:
        small = small + small_read(ref)
    for which in range(2):
        for k in range(planes):
            at = which * rows + k * hid
            total = ins[0][at : at + hid, :].astype(f32)
            for ref in ins[1:]:
                total = total + ref[at : at + hid, :].astype(f32)
            if k == 0:
                total = total + old[which]
            both[which, k * hid : (k + 1) * hid, :] = total.astype(bf16)
    mine = place[0] // (planes // 2)
    keep[:rows, :] = both[mine]
    give[:rows, :] = both[1 - mine]
    small_write(keep, small)
    small_write(give, small)


def plane_sum_kernel(mask, planes, place, keep, got, out):
    rows = keep.shape[0] - 16
    hid = rows // planes
    for k in range(planes):
        at, by = k * hid, (k ^ mask) * hid
        total = keep[at : at + hid, :].astype(f32) + got[by : by + hid, :].astype(f32)
        out[at : at + hid, :] = total.astype(bf16)
    small_write(out, small_read(keep) + small_read(got))


def att_to_owner_kernel(chips, planes, place, *refs):
    ins, old, outs, scratch = refs[:chips], refs[chips], refs[chips + 1 : -1], refs[-1]
    span = old.shape[1]
    for k in range(planes):
        for which in range(4):
            at = (k * 4 + which) * span
            total = ins[0][at : at + span, :].astype(f32)
            for ref in ins[1:]:
                total = total + ref[at : at + span, :].astype(f32)
            if k == 0:
                total = total + old[which]
            scratch[which, k * span : (k + 1) * span, :] = total.astype(bf16)
    for u, out in enumerate(outs):
        out[...] = scratch[place[0] ^ u]


def near_sum_kernel(planes, place, keep, got, *refs):
    ins, (out, small_out) = refs[:planes], refs[planes:]
    rows = keep.shape[0] - 16
    hid = rows // planes
    span = ins[0].shape[0] // planes
    for k in range(planes):
        at, by = k * hid, (k ^ 1) * hid
        total = keep[at : at + hid, :].astype(f32) + got[by : by + hid, :].astype(f32)
        out[at : at + hid, :] = total.astype(bf16)
        total = jnp.zeros((span, D), f32)
        for u, ref in enumerate(ins):
            at = (k ^ u) * span
            total = total + ref[at : at + span, :].astype(f32)
        out[rows + k * span : rows + (k + 1) * span, :] = total.astype(bf16)
    small_out[...] = small_read(keep) + small_read(got)


def newton_kernel(planes, chips, base_row, groups, with_rows, place, own, other, *refs):
    outs, x_ref, low_ref = refs[:-2], refs[-2], refs[-1]
    dim, cols = x_ref.shape
    group = cols // planes
    half_group = group // 2
    span = half_group // chips
    tall = own.shape[0] // chips
    chunk = 512
    total = jnp.zeros((1, D), f32)
    for half in (own, other):
        for m in range(chips):
            at = m * tall + base_row
            part = half[at : at + planes * span, :].astype(f32)
            total = total + jnp.sum(part * part, axis=0, keepdims=True)
    inverse = 1.0 / (jnp.sqrt(jnp.sum(total, axis=1, keepdims=True)) + 1e-07)
    for k in range(planes):
        rows = []
        for half in (own, other):
            for m in range(chips):
                at = m * tall + base_row + k * span
                rows.append(half[at : at + span, :])
        part = jnp.concatenate(rows, 0).astype(f32).T * inverse
        x_ref[:, k * group : (k + 1) * group] = part
        low_ref[:, k * group : (k + 1) * group] = part.astype(bf16)
    diagonal = lax.broadcasted_iota(jnp.int32, (dim, dim), 0) == lax.broadcasted_iota(
        jnp.int32, (dim, dim), 1
    )

    def step(spans):
        gram = jnp.zeros((dim, dim), f32)
        for at in range(0, cols, chunk):
            part = low_ref[:, at : at + chunk]
            gram = gram + mm(part, part, nt)
        trace = jnp.sum(
            jnp.sum(jnp.where(diagonal, gram, 0.0), axis=0, keepdims=True), axis=1, keepdims=True
        )
        shift = trace * (1.0 / dim)
        rest = jnp.where(diagonal, gram - shift, gram)
        rest_low = rest.astype(bf16)
        poly = (newton_two + 2.0 * newton_three * shift) * rest + newton_three * mm(
            rest_low, rest_low, nn
        )
        poly = poly.astype(bf16)
        scale = newton_one + newton_two * shift + newton_three * shift * shift
        for part in spans:
            new = scale * x_ref[:, part] + mm(poly, low_ref[:, part], nn)
            x_ref[:, part] = new
            low_ref[:, part] = new.astype(bf16)

    everything = [slice(at, at + chunk) for at in range(0, cols, chunk)]
    for _ in range(4):
        step(everything)
    if with_rows:
        step(everything)
    else:
        step([slice(k * group, k * group + half_group) for k in groups])
    for k, out in zip(groups, outs):
        part = x_ref[:, k * group : (k + 1) * group].T.astype(bf16)
        base = half_group if with_rows else 0
        for m in range(chips):
            chip = place[1] // 2 ^ m
            if with_rows:
                at = m * tall + base_row + k * span
                out[pl.ds(pl.multiple_of(chip * span, span), span), :] = own[at : at + span, :]
            to = pl.multiple_of(base + chip * span, span)
            out[pl.ds(to, span), :] = part[m * span : (m + 1) * span, :]


def newton(place, own, other, planes, base_row, cols, groups, with_rows, name):
    rows = cols // planes // 2 * (2 if with_rows else 1)
    return run(
        functools.partial(
            newton_kernel, planes, lax.axis_size("dp") // 2, base_row, groups, with_rows
        ),
        place,
        [own, other],
        [like((rows, D), bf16)] * len(groups),
        name,
        scratch=[pltpu.VMEM((D, cols), f32), pltpu.VMEM((D, cols), bf16)],
        flops=10 * D * D * (2 * cols + D),
    )


def momentum_rows_kernel(planes, chips, group, place, own, out):
    span = out.shape[0] // chips
    for m in range(chips):
        to = pl.multiple_of((place[1] // 2 ^ m) * span, span)
        at = m * (own.shape[0] // chips) + group * span
        out[pl.ds(to, span), :] = own[at : at + span, :]


def att_final_kernel(planes, span, place, mine, got, *refs):
    old, outs, rows = refs[:4], refs[4:-1], refs[-1]
    half = mine.shape[1] // 2
    core = place[1] % 2
    for which in range(4):
        slot = place[0] ^ which
        for kind in range(2):
            for at in range(0, half, span):
                from_at = kind * half + at
                rows[pl.ds(pl.multiple_of(2 * at + core * span, span), span), :] = mine[
                    slot, from_at : from_at + span, :
                ]
                rows[pl.ds(pl.multiple_of(2 * at + (1 - core) * span, span), span), :] = got[
                    slot, from_at : from_at + span, :
                ]
            part = rows[...].astype(f32)
            part = part.T if which < 3 else part
            if kind == 0:
                outs[which][...] = part
            else:
                outs[4 + which][...] = old[which][...] - muon_rates[which] * part


def ffn_buffers_kernel(planes, chips, place, own, other, far, far_got, eo, co):
    span = far.shape[0] // chips
    core = place[1] % 2

    def fill(mine_out, far_out):
        for m in range(chips):
            chip = place[1] // 2 ^ m
            here = pl.multiple_of((2 * chip + core) * span, span)
            there = pl.multiple_of((2 * chip + 1 - core) * span, span)
            at = m * (own.shape[0] // chips)
            mine_out[pl.ds(here, span), :] = own[at : at + span, :].astype(f32)
            mine_out[pl.ds(there, span), :] = other[at : at + span, :].astype(f32)
            at = m * span
            here = pl.multiple_of((2 * m + core) * span, span)
            there = pl.multiple_of((2 * m + 1 - core) * span, span)
            far_out[pl.ds(here, span), :] = far[at : at + span, :].astype(f32)
            far_out[pl.ds(there, span), :] = got[at : at + span, :].astype(f32)

    got = far_got
    pl.when(place[0] < planes // 2)(lambda: fill(co, eo))
    pl.when(place[0] >= planes // 2)(lambda: fill(eo, co))


def ffn_final_kernel(planes, chips, place, mine, far, got, we, wc, eo, co):
    rows = mine.shape[0]
    span = rows // chips
    core = place[1] % 2

    def fill(mine_out, mine_w, mine_rate, far_out, far_w, far_rate):
        for m in range(chips):
            at = slice(m * span, (m + 1) * span)
            far_at = slice(rows + m * span, rows + (m + 1) * span)
            here = pl.ds(pl.multiple_of((2 * m + core) * span, span), span)
            there = pl.ds(pl.multiple_of((2 * m + 1 - core) * span, span), span)
            mine_out[here, :] = mine_w[here, :] - mine_rate * mine[at, :].astype(f32)
            mine_out[there, :] = mine_w[there, :] - mine_rate * got[at, :].astype(f32)
            far_out[here, :] = far_w[here, :] - far_rate * far[at, :].astype(f32)
            far_out[there, :] = far_w[there, :] - far_rate * got[far_at, :].astype(f32)

    expand, contract = (eo, we, muon_rates[4]), (co, wc, muon_rates[5])
    pl.when(place[0] < planes // 2)(lambda: fill(*contract, *expand))
    pl.when(place[0] >= planes // 2)(lambda: fill(*expand, *contract))


def shards(
    layer_in,
    doc_ids,
    out_grad,
    w_query,
    w_key,
    w_value,
    w_output,
    w_expand,
    w_contract,
    small_params,
    buffer_query,
    buffer_key,
    buffer_value,
    buffer_output,
    buffer_expand,
    buffer_contract,
    small_first,
    small_second,
):
    planes = lax.axis_size("mp")
    spots = lax.axis_size("dp")
    chips = spots // 2
    plane = lax.axis_index("mp")
    spot = lax.axis_index("dp")
    place = jnp.stack([plane, spot]).astype(jnp.int32)
    length = layer_in.shape[1]
    head_cols = w_query.shape[1]
    hidden_rows = w_expand.shape[0]
    span = head_cols // spots
    hid = hidden_rows // spots
    to_planes = range(1, planes)
    to_chips = range(1, chips)
    weights_old = (w_query, w_key, w_value, w_output, w_expand, w_contract)
    buffers_old = (
        buffer_query,
        buffer_key,
        buffer_value,
        buffer_output,
        buffer_expand,
        buffer_contract,
    )

    def around_planes(x):
        return [x] + [swap(x, "mp", k) for k in to_planes]

    def around_chips(x):
        return [x] + [swap(x, "dp", 2 * m) for m in to_chips]

    def together(*groups):
        return lax.optimization_barrier(groups)

    def together(*groups):
        return lax.optimization_barrier(groups)

    qkv_piece, rest_piece = pieces(
        weight_pieces_kernel,
        place,
        weights_old,
        [like((3 * span, D), bf16), like((span + 2 * hid, D), bf16)],
        "weight_pieces",
    )
    inputs = layer_in
    documents = pick(doc_ids, plane)
    last = (
        jnp.sum(documents[None, :] <= documents[:, None], axis=1, dtype=jnp.int32)[None, :] - 1
    )
    start = jnp.sum(documents[None, :] < documents[:, None], axis=1, dtype=jnp.int32)[None, :]

    def to_slots(bias):
        return reorder(reorder(bias, plane, 0), spot, 1)

    bias = to_slots(small_params[:FF].reshape(planes, spots, hid))
    bias = bias.reshape(planes, chips, 2, hid).transpose(2, 1, 0, 3)
    bias = bias.reshape(2, chips, 1, planes * hid)
    bout = small_params[FF : FF + D].reshape(1, D)
    alphas = small_params[FF + D :]
    token_span = length // planes
    ups = split_positions(out_grad, place)

    qkv_own, ups = together(around_planes(qkv_piece), ups)
    qkv_own = around_chips(jnp.stack(qkv_own))
    rest_own = around_planes(rest_piece)
    qkv_own, rest_own, last, start, bias = together(
        qkv_own, rest_own, last, start, bias
    )
    qkv_own = jnp.stack(qkv_own)
    qkv_halves = [qkv_own, swap(qkv_own, "dp", 1)]
    rest_own, ups = together(jnp.stack(rest_own), ups)
    rest_own = around_chips(rest_own)
    up_near = ups[1]
    ups = [ups[0], None] + [swap(ups[u], "mp", u) for u in to_planes[1:]]
    qkv, heads = attention(place, last, inputs, qkv_halves)
    heads, up_near, buffers_old = together(heads, up_near, buffers_old)
    ups[1] = swap(up_near, "mp", 1)
    att_old, ffn_old = pieces(
        buffer_pieces_kernel,
        place,
        buffers_old,
        [like((4, span, D), f32), like((2, hid, D), f32)],
        "buffer_pieces",
    )
    heads, rest_own, ups, att_old, ffn_old = together(heads, rest_own, ups, att_old, ffn_old)
    rest_halves = interleave(rest_own, [swap(part, "dp", 1) for part in rest_own])
    lays, rest = feed_forward(place, alphas, inputs, heads, ups, rest_halves, bias, bout)
    ffn_keep, ffn_give, grad_output, heads_grad, middle_grad, gb_in, gb_out, g_alpha = rest

    ffn_rows = (chips * 2 * planes * hid, D)
    ffn_got = swap(ffn_give.reshape(ffn_rows), "dp", 1)
    gb_in = gb_in.reshape(2, chips, planes, hid).transpose(2, 1, 0, 3).reshape(planes, spots, hid)
    small = jnp.concatenate(
        [to_slots(gb_in).reshape(-1), gb_out.reshape(-1), jnp.sum(g_alpha, axis=1)]
    )
    small = jnp.pad(small, (0, 8 * D - small.size)).reshape(8, D)
    high = lax.reduce_precision(small, 8, 7)
    pair = jnp.concatenate([high, lax.reduce_precision(small - high, 8, 7)]).astype(bf16)
    pair = swap(pair, "dp", 1).astype(f32)
    small = small + pair[:8] + pair[8:]
    parts = run(
        ffn_core_kernel,
        place,
        [ffn_keep.reshape(ffn_rows), ffn_got, small],
        [like((2 * planes * hid + 16, D), bf16)] * chips,
        "ffn_core_sum",
    )
    middle_grad, parts = together(middle_grad, parts)
    got = [parts[0]] + [swap(parts[m], "dp", 2 * m) for m in to_chips]
    lay_far = [swap(lays[u], "mp", u) for u in to_planes[1:]]
    ins, att_keep, att_give = attention_back(
        place, start, inputs, qkv_halves, qkv, heads_grad, heads, grad_output, middle_grad,
        0, planes, True,
    )
    ins, att_keep, att_give, got, lay_far = together(ins, att_keep, att_give, got, lay_far)

    far = planes // 2
    parts = got
    rows = planes * hid
    give, keep = run(
        functools.partial(ffn_chip_kernel, chips, planes),
        place,
        [ffn_old, *parts],
        [like((rows + 16, D), bf16)] * 2,
        "ffn_chip_sum",
        scratch=[pltpu.VMEM((2, rows, D), bf16)],
    )
    give, att_give, lays = together(give, att_give, lays)
    got = swap(give, "mp", far)
    lay_near = swap(lays[1], "mp", 1)
    att_got = swap(att_give, "dp", 1)
    att_parts = run(
        att_core_kernel,
        place,
        [att_keep, att_got],
        [like((planes * 4 * span, D), bf16)] * chips,
        "att_core_sum",
    )
    att_got = [att_parts[0]] + [swap(att_parts[m], "dp", 2 * m) for m in to_chips]
    got, att_got, lay_near = together(got, att_got, lay_near)
    half_sum = run(
        functools.partial(plane_sum_kernel, far, planes),
        place,
        [keep, got],
        [like((rows + 16, D), bf16)],
        "ffn_far_sum",
    )[0]
    got = swap(half_sum, "mp", 1)
    att_parts = run(
        functools.partial(att_to_owner_kernel, chips, planes),
        place,
        att_got + [att_old],
        [like((planes * span, D), bf16)] * planes,
        "att_chip_sum",
        scratch=[pltpu.VMEM((4, planes * span, D), bf16)],
    )
    att_got = [att_parts[0]] + [swap(att_parts[u], "mp", u) for u in to_planes]
    message, small_grad = run(
        functools.partial(near_sum_kernel, planes),
        place,
        [half_sum, got, *att_got],
        [like((rows + planes * span, D), bf16), like((8, D), f32)],
        "near_sum",
    )
    small_grad = small_grad.reshape(-1)[: FF + D + 2]
    message, ins = together(message, ins)
    got = around_chips(message)
    in_got = [ins[0], None, swap(ins[2], "mp", 2), None]
    first_new = 0.5 * small_first + 0.5 * small_grad
    second_new = 0.5 * small_second + 0.5 * small_grad * small_grad
    correction = 1.0 - 0.5**STEP
    small_new = small_params - adam_rate * (first_new / correction) / (
        jnp.sqrt(second_new / correction) + 1e-08
    )
    smalls = (small_new, first_new, second_new)
    got, smalls, in_got, ins = together(got, smalls, in_got, ins)
    in_got[3] = swap(ins[3], "mp", 3)
    in_got[1] = swap(ins[1], "mp", 1)
    own = jnp.concatenate(got)
    other = swap(own, "dp", 1)
    far_m = run(
        functools.partial(momentum_rows_kernel, planes, chips, far),
        place,
        [own],
        [like((hidden_rows // 2, D), bf16)],
        "momentum_rows",
    )[0]
    far_m = swap(far_m, "mp", far)
    att_x = newton(
        place, own, other, planes, rows, D, tuple(range(planes)), True, "newton_att"
    )
    att_x, in_got, other = together(att_x, in_got, other)
    att_x = jnp.stack([att_x[0]] + [swap(att_x[u], "mp", u) for u in to_planes])
    step, far_step = newton(
        place, own, other, planes, 0, planes * hidden_rows, (0, far), False, "newton_ffn"
    )
    step, att_x = together(step, att_x)
    far_step = swap(far_step, "mp", far)
    far_m_got = swap(far_m, "dp", 1)
    att_other = swap(att_x, "dp", 1)
    new_be, new_bc = run(
        functools.partial(ffn_buffers_kernel, planes, chips),
        place,
        [own, other, far_m, far_m_got],
        [like((hidden_rows, D), f32)] * 2,
        "ffn_buffers",
    )
    layer_out = join_positions([lays[0], lay_near, *lay_far], place)
    in_grad = join_positions(in_got, place)
    att_out = run(
        functools.partial(att_final_kernel, planes, span),
        place,
        [att_x, att_other, *weights_old[:4]],
        [like(w.shape, f32) for w in weights_old[:4]] * 2,
        "att_final",
        scratch=[pltpu.VMEM((head_cols, D), bf16)],
    )
    far_step, new_be, layer_out, in_grad, att_out = together(
        far_step, new_be, layer_out, in_grad, att_out
    )
    got = swap(jnp.concatenate([step, far_step]), "dp", 1)
    new_we, new_wc = run(
        functools.partial(ffn_final_kernel, planes, chips),
        place,
        [step, far_step, got, w_expand, w_contract],
        [like((hidden_rows, D), f32)] * 2,
        "ffn_final",
    )
    return (
        (layer_out, in_grad)
        + tuple(att_out[:4])
        + (new_be, new_bc)
        + tuple(att_out[4:])
        + (new_we, new_wc)
        + smalls
    )


def solution(mesh):
    in_specs = (
        P("dp", None, None),
        P("dp", None),
        P("dp", "mp", None),
        P(None, "mp"),
        P(None, "mp"),
        P(None, "mp"),
        P("mp", None),
        P("mp", None),
        P("mp", None),
        P(),
        P(None, "mp"),
        P(None, "mp"),
        P(None, "mp"),
        P("mp", None),
        P("mp", None),
        P("mp", None),
        P(),
        P(),
    )
    out_specs = (
        P("dp", "mp", None),
        P("dp", "mp", None),
        P(None, "mp"),
        P(None, "mp"),
        P(None, "mp"),
        P("mp", None),
        P("mp", None),
        P("mp", None),
        P(None, "mp"),
        P(None, "mp"),
        P(None, "mp"),
        P("mp", None),
        P("mp", None),
        P("mp", None),
        P(),
        P(),
        P(),
    )
    block = mesh.shape["mp"] == 4 and mesh.shape["dp"] == 8
    return jax.shard_map(shards if block else general_shards, mesh=mesh, in_specs=in_specs, out_specs=out_specs, check_vma=False)
```
